256 devices in a mesh: azimuth: 4 (over x), meridian: 32 (over z, y), depth: 2 (over core).
Axes of the slice: x: 4, y: 4, z: 8, core: 2. Of those that a mesh axis runs over, the one named last changes fastest.
Arguments:
- adjoint_end: float32 [6, 6, 6, 4, 16, 4096], P(None, None, None, 'depth', 'azimuth', 'meridian'), may hold values from -6 to 6
- temp_early: bfloat16 [6, 6, 6, 4, 16, 4096], P(None, None, None, 'depth', 'azimuth', 'meridian'), may hold values from -3 to 3
- temp_late: bfloat16 [6, 6, 6, 4, 16, 4096], P(None, None, None, 'depth', 'azimuth', 'meridian'), may hold values from -3 to 3
- mass_inverse: float32 [6, 6, 6, 4, 16, 4096], P(None, None, None, 'depth', 'azimuth', 'meridian'), may hold values from 0.5 to 2
- thermal_transport_coefficient: float32 [6, 6, 6, 4, 16, 4096], P(None, None, None, 'depth', 'azimuth', 'meridian'), may hold values from 0.3 to 3
- jacobian_quadrature_scales: bfloat16 [3, 6, 6, 6, 4, 16, 4096], P(None, None, None, None, 'depth', 'azimuth', 'meridian'), may hold values from 0.0049743652 to 0.029907227
- measured: float32 [2, 4096], P(None, ('azimuth', 'meridian', 'depth')), may hold values from -5 to 5
- sensor_cell_slot: int32 [4096], P(('azimuth', 'meridian', 'depth')), may hold values from 0 to 1023
- sensor_gridsite_slot: int32 [4096], P(('azimuth', 'meridian', 'depth')), may hold values from 0 to 215
- face_weight: float32 [2, 6, 6, 16, 4096], P('depth', None, None, 'azimuth', 'meridian'), may hold values from 0.002 to 0.02
- panel_owner: int32 [2, 16, 4096], P('depth', 'azimuth', 'meridian'), may hold values from 0 to 4095, as said below
Outputs:
- adjoint_start: float32 [6, 6, 6, 4, 16, 4096], P(None, None, None, 'depth', 'azimuth', 'meridian')
- panel_grad: float32 [4096], P(('azimuth', 'meridian', 'depth'))
The draws below stay inside these ranges and needn't reach their ends.
Inputs may be any that keep to these rules, and one draw needn't show every extreme that they name: `panel_owner`: the device with joined index f (azimuth slowest, then meridian, then depth) owns panels f * 16 to (f + 1) * 16 - 1. Each entry names a panel owned by the device that holds the entry, or by the device one step lower along azimuth (cyclically) with the same meridian and depth index.
All inputs are finite; a program needn't handle non-finite values.
Results may differ from the reference program's by a relative error of at most 0.0008.
Values sent between devices are 32-bit elements; how exact they have to be, the bound alone decides.
A program may use at most 128 MiB of HBM per device.

```python
import math
import jax
import jax.numpy as jnp
import numpy as np
from jax import lax

NP = 6
D_EL = 2
A_EL = 4
M_EL = 128
S_DEV = 16
PAN_DEV = 16
D_TOT = 4
A_TOT = 16
M_TOT = 4096
E_DEV = 1024
S_TOT = 4096
NPANEL = 4096
N_AZIMUTH = 4
N_MERIDIAN = 32
N_DEPTH = 2


def draw_panel_owner(key, part):
    key = jax.random.fold_in(key, 11)
    coin_key, panel_key = jax.random.split(key)
    grid_shape = (2, A_TOT, M_TOT)
    surface_side = lax.broadcasted_iota(jnp.int32, grid_shape, 0)
    azimuth_pos = lax.broadcasted_iota(jnp.int32, grid_shape, 1)
    meridian_pos = lax.broadcasted_iota(jnp.int32, grid_shape, 2)
    flip_coin = jax.random.randint(coin_key, grid_shape, 0, 2)
    backward = jnp.logical_and(azimuth_pos % A_EL == 0, flip_coin == 1)
    sector_index = azimuth_pos // A_EL
    sector_index = jnp.where(backward, (sector_index + N_AZIMUTH - 1) % N_AZIMUTH, sector_index)
    device_flat = (sector_index * N_MERIDIAN + meridian_pos // M_EL) * N_DEPTH + surface_side
    panel_slot = jax.random.randint(panel_key, grid_shape, 0, PAN_DEV)
    return (device_flat * PAN_DEV + panel_slot).astype(jnp.int32)


def plant(values, stream_key, low, high):
    spot = [jax.random.randint(jax.random.fold_in(stream_key, axis), (), 0, length) for axis, length in enumerate(values.shape)]
    longest = values.shape.index(max(values.shape))
    neighbour = spot[:longest] + [(spot[longest] + 1) % values.shape[longest]] + spot[longest + 1:]
    return values.at[tuple(spot)].set(low).at[tuple(neighbour)].set(high)


def level_of(rng, dims, shards, low, high):
    def one(position, shards_of):
        steps = jax.random.uniform(jax.random.fold_in(jax.random.fold_in(rng, 6), position), (shards_of,), jnp.float32, low / len(shards), high / len(shards))
        return jnp.repeat(jnp.exp(steps), dims[position] // shards_of).reshape((-1,) + (1,) * (len(dims) - position - 1))

    gain = one(*shards[0])
    for cut in shards[1:]:
        gain = gain * one(*cut)
    return gain


def gaussian(rng, shape, width, limit, pieces=(), kind=jnp.bfloat16):
    values = jax.random.normal(rng, shape, jnp.float32) * width
    if len(pieces) > 0:
        values = level_of(rng, shape, pieces, -0.22, 0.18) * values
    return jnp.clip(values, min=-limit, max=limit).astype(kind)


def setup_inputs(seed: int = 0) -> dict:
    streams_of = jax.random.split(jax.random.key(seed), 12)
    return {
        "adjoint_end": gaussian(streams_of[0], (NP, NP, NP, D_TOT, A_TOT, M_TOT), 1.0, 6.0, ((3, 2), (4, 4), (5, 32)), jnp.float32),
        "temp_early": gaussian(streams_of[1], (NP, NP, NP, D_TOT, A_TOT, M_TOT), 0.7, 3.0, ((3, 2), (4, 4), (5, 32))),
        "temp_late": gaussian(streams_of[2], (NP, NP, NP, D_TOT, A_TOT, M_TOT), 0.7, 3.0, ((3, 2), (4, 4), (5, 32))),
        "mass_inverse": jnp.clip(jnp.exp(math.log(2.0) - 1.3862944 * jax.random.uniform(streams_of[3], (NP, NP, NP, D_TOT, A_TOT, M_TOT), jnp.float32) ** level_of(streams_of[3], (NP, NP, NP, D_TOT, A_TOT, M_TOT), ((3, 2), (4, 4), (5, 32)), -0.2, 0.2)), 0.5, 2.0),
        "thermal_transport_coefficient": jnp.clip(jnp.exp(math.log(3.0) - 2.3025851 * jax.random.uniform(streams_of[4], (NP, NP, NP, D_TOT, A_TOT, M_TOT), jnp.float32) ** level_of(streams_of[4], (NP, NP, NP, D_TOT, A_TOT, M_TOT), ((3, 2), (4, 4), (5, 32)), -0.2, 0.2)), 0.3, 3.0),
        "jacobian_quadrature_scales": jnp.clip(jnp.exp(math.log(0.029907227) - 1.7938024 * jax.random.uniform(streams_of[5], (3, NP, NP, NP, D_TOT, A_TOT, M_TOT), jnp.float32) ** level_of(streams_of[5], (3, NP, NP, NP, D_TOT, A_TOT, M_TOT), ((4, 2), (5, 4), (6, 32)), -0.2, 0.2)), 0.0049743652, 0.029907227).astype(jnp.bfloat16),
        "measured": gaussian(streams_of[6], (2, S_TOT), 1.0, 5.0, ((1, 256),), jnp.float32),
        "sensor_cell_slot": plant(jax.random.randint(streams_of[7], (S_TOT,), 0, E_DEV), jax.random.fold_in(streams_of[7], 1), 0, E_DEV - 1).astype(jnp.int32),
        "sensor_gridsite_slot": plant(jax.random.randint(streams_of[8], (S_TOT,), 0, NP * NP * NP), jax.random.fold_in(streams_of[8], 1), 0, (NP * NP * NP) - 1).astype(jnp.int32),
        "face_weight": jnp.clip(jnp.exp(math.log(0.02) - 2.30258502 * jax.random.uniform(streams_of[9], (2, NP, NP, A_TOT, M_TOT), jnp.float32) ** level_of(streams_of[9], (2, NP, NP, A_TOT, M_TOT), ((0, 2), (3, 4), (4, 32)), -0.2, 0.2)), 0.002, 0.02),
        "panel_owner": draw_panel_owner(jax.random.fold_in(streams_of[11], 71), 0),
    }


interval_length = 0.1

def gll_derivative():
    root_seven = math.sqrt(7.0)
    inner_near = math.sqrt((7.0 - 2.0 * root_seven) / 21.0)
    inner_far = math.sqrt((7.0 + 2.0 * root_seven) / 21.0)
    points = np.array([-1.0, -inner_far, -inner_near, inner_near, inner_far, 1.0])
    legendre = (63.0 * points ** 5 - 70.0 * points ** 3 + 15.0 * points) / 8.0
    entries = np.zeros((6, 6))
    for row_index in range(6):
        for col_index in range(6):
            if row_index != col_index:
                entries[row_index, col_index] = legendre[row_index] / (legendre[col_index] * (points[row_index] - points[col_index]))
    entries[0, 0] = -7.5
    entries[5, 5] = 7.5
    return jnp.asarray(entries, jnp.float32)

def along(matrix, field, direction):
    forms = ('ij,jbcxyz->ibcxyz', 'ij,ajcxyz->aicxyz', 'ij,abjxyz->abixyz')
    return jnp.einsum(forms[direction], matrix, field, precision=lax.Precision.HIGHEST)

def costate_forcing(normalized_solution, thermal_state_solution, thermal_transport_coefficient, jacobian_quadrature_scales, collocation_differentiator):
    thermal_load_amounts = thermal_state_solution.astype(jnp.float32)
    metric = jacobian_quadrature_scales.astype(jnp.float32)
    conduct = thermal_transport_coefficient * (1.0 + 0.5 * thermal_load_amounts * thermal_load_amounts)
    conduct_slope = thermal_transport_coefficient * thermal_load_amounts
    flipped = collocation_differentiator.T
    conductive_outflow = jnp.zeros_like(normalized_solution)
    cross_term = jnp.zeros_like(normalized_solution)
    for direction in range(3):
        grad_adjoint = along(collocation_differentiator, normalized_solution, direction)
        grad_heat = along(collocation_differentiator, thermal_load_amounts, direction)
        cross_term = cross_term + metric[direction] * grad_heat * grad_adjoint
        conductive_outflow = conductive_outflow + along(flipped, metric[direction] * conduct * grad_adjoint, direction)
    return conductive_outflow + conduct_slope * cross_term

def end_faces(field, node_dim, elem_dim):
    nodes_along = field.shape[node_dim]
    elements = field.shape[elem_dim]
    lower = lax.slice_in_dim(field, 0, 1, axis=node_dim)
    upper = lax.slice_in_dim(field, nodes_along - 1, nodes_along, axis=node_dim)
    lower_first = lax.slice_in_dim(lower, 0, 1, axis=elem_dim)
    upper_last = lax.slice_in_dim(upper, elements - 1, elements, axis=elem_dim)
    return (lower, upper, lower_first, upper_last)

def join_faces(field, lower, upper, lower_next, upper_prev, node_dim, elem_dim):
    nodes_along = field.shape[node_dim]
    elements = field.shape[elem_dim]
    new_upper = upper + jnp.concatenate([lax.slice_in_dim(lower, 1, elements, axis=elem_dim), lower_next], axis=elem_dim)
    new_lower = lower + jnp.concatenate([upper_prev, lax.slice_in_dim(upper, 0, elements - 1, axis=elem_dim)], axis=elem_dim)
    middle_nodes = lax.slice_in_dim(field, 1, nodes_along - 1, axis=node_dim)
    return jnp.concatenate([new_lower, middle_nodes, new_upper], axis=node_dim)

def assemble_pass(field, node_dim, elem_dim, closed):
    lower, upper, lower_first, upper_last = end_faces(field, node_dim, elem_dim)
    if closed:
        lower_next, upper_prev = (lower_first, upper_last)
    else:
        lower_next, upper_prev = (jnp.zeros_like(lower_first), jnp.zeros_like(upper_last))
    return join_faces(field, lower, upper, lower_next, upper_prev, node_dim, elem_dim)

def assemble(field):
    field = assemble_pass(field, 1, 4, True)
    field = assemble_pass(field, 2, 5, False)
    return assemble_pass(field, 0, 3, False)

def sensor_forcings(thermal_state_solution, measured_sensor_line, sensor_cell_slot, sensor_gridsite_slot):
    holder = (jnp.arange(S_TOT) // S_DEV).astype(jnp.int32)
    azim_device = holder // (N_MERIDIAN * N_DEPTH)
    merid_device = holder // N_DEPTH % N_MERIDIAN
    depth_device = holder % N_DEPTH
    element = sensor_cell_slot.astype(jnp.int32)
    throughdepth_cell = depth_device * D_EL + element // (A_EL * M_EL)
    circumferential_cell = azim_device * A_EL + element // M_EL % A_EL
    longitudinal_cell = merid_device * M_EL + element % M_EL
    node_index = sensor_gridsite_slot.astype(jnp.int32)
    throughdepth_gridsite = node_index // (NP * NP)
    circumferential_gridsite = node_index // NP % NP
    longitudinal_gridsite = node_index % NP
    matrix_numbers = thermal_state_solution[throughdepth_gridsite, circumferential_gridsite, longitudinal_gridsite, throughdepth_cell, circumferential_cell, longitudinal_cell].astype(jnp.float32)
    located_amounts = jnp.zeros(thermal_state_solution.shape, jnp.float32)
    return located_amounts.at[throughdepth_gridsite, circumferential_gridsite, longitudinal_gridsite, throughdepth_cell, circumferential_cell, longitudinal_cell].add(matrix_numbers - measured_sensor_line)

def backward_march_update(costate_solution, normalized_solution, thermal_state_solution, measured_sensor_line, thermal_transport_coefficient, jacobian_quadrature_scales, sensor_cell_slot, sensor_gridsite_slot, collocation_differentiator):
    piecewise_shares = []
    for sector in range(N_AZIMUTH):
        opening_slot_number = sector * A_EL
        closing_slot_number = opening_slot_number + A_EL
        piecewise_shares.append(costate_forcing(normalized_solution[:, :, :, :, opening_slot_number:closing_slot_number, :], thermal_state_solution[:, :, :, :, opening_slot_number:closing_slot_number, :], thermal_transport_coefficient[:, :, :, :, opening_slot_number:closing_slot_number, :], jacobian_quadrature_scales[:, :, :, :, :, opening_slot_number:closing_slot_number, :], collocation_differentiator))
    conductive_outflow = jnp.concatenate(piecewise_shares, axis=4)
    costate_change = sensor_forcings(thermal_state_solution, measured_sensor_line, sensor_cell_slot, sensor_gridsite_slot) - interval_length * conductive_outflow
    return costate_solution + assemble(costate_change)

def reference(adjoint_end, temp_early, temp_late, mass_inverse, thermal_transport_coefficient, jacobian_quadrature_scales, measured, sensor_cell_slot, sensor_gridsite_slot, face_weight, panel_owner):
    collocation_differentiator = gll_derivative()
    late_scaled = mass_inverse * adjoint_end
    middle = backward_march_update(adjoint_end, late_scaled, temp_late, measured[1], thermal_transport_coefficient, jacobian_quadrature_scales, sensor_cell_slot, sensor_gridsite_slot, collocation_differentiator)
    early_scaled = mass_inverse * middle
    adjoint_start = backward_march_update(middle, early_scaled, temp_early, measured[0], thermal_transport_coefficient, jacobian_quadrature_scales, sensor_cell_slot, sensor_gridsite_slot, collocation_differentiator)
    outer_face = late_scaled[0, :, :, 0] + early_scaled[0, :, :, 0]
    inner_face = late_scaled[NP - 1, :, :, D_TOT - 1] + early_scaled[NP - 1, :, :, D_TOT - 1]
    surface = jnp.stack([outer_face, inner_face])
    strip_grad = interval_length * lax.optimization_barrier(jnp.sum(face_weight * surface, axis=(1, 2)))
    running = jnp.flip(jnp.cumsum(jnp.flip(strip_grad, 2), axis=2), 2)
    panel_grad = jax.ops.segment_sum(running.reshape(-1), panel_owner.reshape(-1).astype(jnp.int32), num_segments=NPANEL)
    return (adjoint_start, panel_grad)
```

```python
import math

import jax
import jax.numpy as jnp
import numpy as np
from jax import lax
from jax.experimental import pallas as pl
from jax.experimental.pallas import tpu as pltpu
from jax.sharding import PartitionSpec as P

N_AZ, N_MER, N_DEP = 4, 32, 2
MER_Y, MER_Z = 4, 8
ROWS = 1728
PLANE = 288
PAN_DEV = 16
SENSORS = 16
STEP = 0.1
F32 = jnp.float32
MESH = pl.DeviceIdType.MESH


def gll_derivative():
    root_seven = math.sqrt(7.0)
    inner_near = math.sqrt((7.0 - 2.0 * root_seven) / 21.0)
    inner_far = math.sqrt((7.0 + 2.0 * root_seven) / 21.0)
    points = np.array([-1.0, -inner_far, -inner_near, inner_near, inner_far, 1.0])
    legendre = (63.0 * points**5 - 70.0 * points**3 + 15.0 * points) / 8.0
    entries = np.zeros((6, 6))
    for i in range(6):
        for j in range(6):
            if i != j:
                entries[i, j] = legendre[i] / (legendre[j] * (points[i] - points[j]))
    entries[0, 0] = -7.5
    entries[5, 5] = 7.5
    return entries


DER = gll_derivative()
FLIP = DER[:, ::-1]
GRAD_EVEN = (0.5 * (DER + FLIP))[:3, :3]
GRAD_ODD = (0.5 * (DER - FLIP))[:3, :3]
TRA = DER.T
DIV_EVEN = (0.5 * (TRA + TRA[:, ::-1]))[:3, :3]
DIV_ODD = (0.5 * (TRA - TRA[:, ::-1]))[:3, :3]


def grad_line(x):
    e = [x[j] + x[5 - j] for j in range(3)]
    o = [x[j] - x[5 - j] for j in range(3)]
    e1, e2 = e[1] - e[0], e[2] - e[0]
    p = [float(GRAD_EVEN[i, 1]) * e1 + float(GRAD_EVEN[i, 2]) * e2 for i in range(3)]
    q = [
        float(GRAD_ODD[i, 0]) * o[0] + float(GRAD_ODD[i, 1]) * o[1] + float(GRAD_ODD[i, 2]) * o[2]
        for i in range(3)
    ]
    return [q[i] + p[i] for i in range(3)] + [q[i] - p[i] for i in (2, 1, 0)]


def div_line(f):
    e = [f[j] + f[5 - j] for j in range(3)]
    o = [f[j] - f[5 - j] for j in range(3)]
    p = [
        float(DIV_EVEN[i, 0]) * e[0] + float(DIV_EVEN[i, 1]) * e[1] + float(DIV_EVEN[i, 2]) * e[2]
        for i in range(3)
    ]
    q1, q2 = [
        float(DIV_ODD[i, 0]) * o[0] + float(DIV_ODD[i, 1]) * o[1] + float(DIV_ODD[i, 2]) * o[2]
        for i in (1, 2)
    ]
    q0 = -(q1 + q2)
    q = [q0, q1, q2]
    return [q[i] + p[i] for i in range(3)] + [q[i] - p[i] for i in (2, 1, 0)]


def rows(start, size, multiple=8):
    if isinstance(start, int):
        return pl.ds(start, size)
    return pl.ds(pl.multiple_of(start, multiple), size)


def line_rows(direction, outer, inner):
    if direction == 0:
        return [rows(j * PLANE + outer * 48 + inner * 16, 16, 16) for j in range(6)]
    if direction == 1:
        return [rows(outer * PLANE + j * 48 + inner * 16, 16, 16) for j in range(6)]
    return [rows(outer * PLANE + inner * 48 + j * 8, 8, 8) for j in range(6)]


def inner_count(direction):
    return 6 if direction == 2 else 3


def kernel(
    adj_hbm,
    early_hbm,
    late_hbm,
    mass_hbm,
    cond_hbm,
    metric_hbm,
    measured,
    cell,
    site,
    face_weight,
    owner,
    out,
    panels,
    adj,
    temp,
    mass,
    cond,
    metric,
    heat,
    kap,
    slope,
    flux_c,
    cross_c,
    source,
    scaled,
    upd,
    mid,
    picks,
    az_out,
    az_in,
    dep_out,
    dep_in,
    ad_out,
    ad_in,
    mer_out,
    mer_in,
    tot_out,
    tot_y,
    ysum_out,
    tot_z,
    pan_out,
    pan_in,
    load_sem,
    face_send,
    face_recv,
    tot_send,
    tot_recv,
    pan_send,
    pan_recv,
):
    az = lax.axis_index("azimuth")
    mer = lax.axis_index("meridian")
    dep = lax.axis_index("depth")
    mer_y = lax.rem(mer, MER_Y)
    mer_z = lax.div(mer, MER_Y)

    def at(da, dm, dd):
        return {
            "azimuth": lax.rem(az + (da + N_AZ), N_AZ),
            "meridian": lax.rem(mer + (dm + N_MER), N_MER),
            "depth": lax.rem(dep + dd, N_DEP),
        }

    def y_peer(k):
        return {"azimuth": az, "meridian": mer_z * MER_Y + lax.rem(mer_y + k, MER_Y), "depth": dep}

    def z_peer(k):
        return {"azimuth": az, "meridian": lax.rem(mer_z + k, MER_Z) * MER_Y + mer_y, "depth": dep}

    loads = [
        (late_hbm, temp.at[1]),
        (metric_hbm, metric),
        (cond_hbm, cond),
        (mass_hbm, mass),
        (adj_hbm, adj),
        (early_hbm, temp.at[0]),
    ]
    loads = [pltpu.make_async_copy(s, d, load_sem.at[i]) for i, (s, d) in enumerate(loads)]
    for copy in loads:
        copy.start()

    barrier = pltpu.get_barrier_semaphore()
    offsets = [
        (da, dm, dd) for dd in (0, 1) for dm in (-1, 0, 1) for da in (-1, 0, 1) if (da, dm, dd) != (0, 0, 0)
    ]
    peers = [at(*o) for o in offsets]
    peers += [y_peer(k) for k in range(1, MER_Y)] + [z_peer(k) for k in range(1, MER_Z)]
    for peer in peers:
        pl.semaphore_signal(barrier, inc=1, device_id=peer, device_id_type=MESH)

    row8 = lax.broadcasted_iota(jnp.int32, (8, 128), 0)
    lane = lax.broadcasted_iota(jnp.int32, (8, 128), 1)
    row_az = lax.rem(row8, 4)
    row_dep = lax.div(row8, 4)
    zero = jnp.zeros((8, 128), F32)

    lane1 = lax.broadcasted_iota(jnp.int32, (1, 128), 1)
    row16 = lax.broadcasted_iota(jnp.int32, (SENSORS, 128), 0)
    lane16 = lax.broadcasted_iota(jnp.int32, (SENSORS, 128), 1)
    code = jnp.full((1, 128), -1, jnp.int32)
    code_column = jnp.zeros((SENSORS, 128), jnp.int32)
    band_column = jnp.zeros((SENSORS, 128), jnp.int32)
    for q in range(SENSORS):
        word = site[q] * 8 + lax.shift_right_logical(cell[q], 7)
        code = jnp.where(jnp.logical_and(lax.rem(lane1, SENSORS) == q, lane1 < 3 * SENSORS), word, code)
        code_column = jnp.where(row16 == q, word, code_column)
        band_column = jnp.where(row16 == q, jnp.bitwise_and(cell[q], 127), band_column)
    for first in range(0, ROWS, 128):
        width = min(128, ROWS - first)
        hot = jnp.where(lane16 + first == code_column, 1.0, 0.0).astype(jnp.bfloat16)
        picks[:, first : first + width] = hot[:, 0:width]

    def sources(k):
        reading = jnp.zeros((SENSORS, 128), F32)
        for q in range(SENSORS):
            reading = jnp.where(row16 == q, measured[k, q], reading)
        felt = jnp.dot(picks[...], temp[k], preferred_element_type=F32)
        value = jnp.where(lane16 == band_column, felt - reading, 0.0)
        high = value.astype(jnp.bfloat16).astype(F32)
        rest = value - high
        middle = rest.astype(jnp.bfloat16).astype(F32)
        low = rest - middle
        table = jnp.concatenate([high, middle, low, jnp.zeros((80, 128), F32)], axis=0).astype(jnp.bfloat16)

        def block(a, _):
            base = lax.broadcasted_iota(jnp.int32, (PLANE, 128), 0) + a * PLANE
            hot = jnp.where(base == code, 1.0, 0.0).astype(jnp.bfloat16)
            source[rows(a * PLANE, PLANE), :] = jnp.dot(hot, table, preferred_element_type=F32)
            return 0

        lax.fori_loop(0, 6, block, 0)

    def coefficients(k):
        def plane(a, _):
            here = rows(a * PLANE, PLANE, 16)
            h = temp[k, here, :].astype(F32)
            heat[here, :] = h
            c = (-STEP) * cond[here, :]
            kap[here, :] = c * (1.0 + 0.5 * h * h)
            slope[here, :] = c * h
            return 0

        lax.fori_loop(0, 6, plane, 0)

        def direction(d):
            def body(outer, _):
                for inner in range(inner_count(d)):
                    at_rows = line_rows(d, outer, inner)
                    g = grad_line([heat[r, :] for r in at_rows])
                    if d == 2:
                        w = metric[rows(2 * ROWS + outer * PLANE + inner * 48, 48, 16), :].astype(F32)
                        w = [w[8 * j : 8 * j + 8] for j in range(6)]
                    else:
                        first = (0, outer * 48 + inner * 16)[d == 0] if d == 0 else outer * PLANE + inner * 16
                        stride = PLANE if d == 0 else 48
                        w = [
                            metric[rows(d * ROWS + first + j * stride, 16, 16), :].astype(F32)
                            for j in range(6)
                        ]
                    for j, r in enumerate(at_rows):
                        flux_c[d, r, :] = kap[r, :] * w[j]
                        cross_c[d, r, :] = slope[r, :] * w[j] * g[j]
                return 0

            lax.fori_loop(0, 6, body, 0)

        for d in range(3):
            direction(d)
        sources(k)

    def update():
        def direction(d):
            def body(outer, _):
                for inner in range(inner_count(d)):
                    at_rows = line_rows(d, outer, inner)
                    g = grad_line([scaled[r, :] for r in at_rows])
                    flux = [flux_c[d, r, :] * g[j] for j, r in enumerate(at_rows)]
                    spread = div_line(flux)
                    for j, r in enumerate(at_rows):
                        total = spread[j] + cross_c[d, r, :] * g[j]
                        before = source if d == 1 else upd
                        upd[r, :] = before[r, :] + total
                return 0

            lax.fori_loop(0, 6, body, 0)

        for d in (1, 2, 0):
            direction(d)

    def assemble_here():
        def azimuth(a, _):
            for c in range(6):
                lo, hi = (rows(a * PLANE + b * 48 + c * 8, 8) for b in (0, 5))
                low, high = upd[lo, :], upd[hi, :]
                upd[hi, :] = high + jnp.where(row_az < 3, pltpu.roll(low, 7, 0), zero)
                upd[lo, :] = low + jnp.where(row_az > 0, pltpu.roll(high, 1, 0), zero)
            return 0

        lax.fori_loop(0, 6, azimuth, 0)

        def meridian(a, _):
            for b in range(6):
                lo, hi = (rows(a * PLANE + b * 48 + c * 8, 8) for c in (0, 5))
                low, high = upd[lo, :], upd[hi, :]
                upd[hi, :] = high + jnp.where(lane < 127, pltpu.roll(low, 127, 1), zero)
                upd[lo, :] = low + jnp.where(lane > 0, pltpu.roll(high, 1, 1), zero)
            return 0

        lax.fori_loop(0, 6, meridian, 0)

        def depth(b, _):
            for c in range(6):
                lo, hi = (rows(a * PLANE + b * 48 + c * 8, 8) for a in (0, 5))
                low, high = upd[lo, :], upd[hi, :]
                upd[hi, :] = high + jnp.where(row_dep == 0, pltpu.roll(low, 4, 0), zero)
                upd[lo, :] = low + jnp.where(row_dep == 1, pltpu.roll(high, 4, 0), zero)
            return 0

        lax.fori_loop(0, 6, depth, 0)

    def face_copies(k):
        copies = []

        def add(offset, src, dst):
            n = len(copies)
            copies.append(
                pltpu.make_async_remote_copy(
                    src_ref=src,
                    dst_ref=dst,
                    send_sem=face_send.at[k, n],
                    recv_sem=face_recv.at[k, n],
                    device_id=at(*offset),
                    device_id_type=MESH,
                )
            )

        for s, da in enumerate((-1, 1)):
            add((da, 0, 0), az_out.at[k, s], az_in.at[k, s])
        add((0, 0, 1), dep_out.at[k], dep_in.at[k])
        for s, da in enumerate((-1, 1)):
            add((da, 0, 1), ad_out.at[k, s], ad_in.at[k, s])
        for s, dm in enumerate((-1, 1)):
            for i, da in enumerate((-1, 0, 1)):
                for dd in (0, 1):
                    add((da, dm, dd), mer_out.at[k, s], mer_in.at[k, (s * 3 + i) * 2 + dd])
        return copies

    def pack_and_start(k, copies):
        for s, (b, e) in enumerate(((0, 0), (5, 3))):
            for a in range(6):
                first = a * PLANE + b * 48 + e
                az_out[k, s, a * 12 : a * 12 + 8, :] = upd[pl.ds(first, 8, stride=4), :]
                az_out[k, s, a * 12 + 8 : a * 12 + 12, :] = upd[pl.ds(first + 32, 4, stride=4), :]
            copies[s].start()

        for d in (0, 1):
            a, r = ((5, 4), (0, 0))[d]

            @pl.when(dep == d)
            def _():
                for n in range(36):
                    first = a * PLANE + n * 8 + r
                    dep_out[k, n * 4 : n * 4 + 4, :] = upd[first : first + 4, :]
                for s, (b, e) in enumerate(((0, 0), (5, 3))):
                    first = a * PLANE + b * 48 + r + e
                    ad_out[k, s, 0:6, :] = upd[pl.ds(first, 6, stride=8), :]

        copies[2].start()
        copies[3].start()
        copies[4].start()
        packed = [zero, zero]
        for n in range(36):
            for s, (c, shift) in enumerate(((0, n), (5, (n + 1) % 128))):
                moved = pltpu.roll(upd[n * 48 + c * 8 : n * 48 + c * 8 + 8, :], shift, 1)
                packed[s] = jnp.where(lane == n, moved, packed[s])
        for s in (0, 1):
            mer_out[k, s] = packed[s]
        for copy in copies[5:]:
            copy.start()

    def add_halo(k, field):
        for s, (b, e) in enumerate(((5, 3), (0, 0))):
            for a in range(6):
                first = a * PLANE + b * 48 + e
                for skip, count in ((0, 8), (8, 4)):
                    r = pl.ds(first + 4 * skip, count, stride=4)
                    field[r, :] = field[r, :] + az_in[k, s, a * 12 + skip : a * 12 + skip + count, :]

        for d in (0, 1):
            a, r = ((5, 4), (0, 0))[d]

            @pl.when(dep == d)
            def _():
                for n in range(36):
                    first = a * PLANE + n * 8 + r
                    field[first : first + 4, :] = (
                        field[first : first + 4, :] + dep_in[k, n * 4 : n * 4 + 4, :]
                    )
                for s, (b, e) in enumerate(((5, 3), (0, 0))):
                    there = pl.ds(a * PLANE + b * 48 + r + e, 6, stride=8)
                    field[there, :] = field[there, :] + ad_in[k, s, 0:6, :]

        node_a, node_b = lax.div(lane, 6), lax.rem(lane, 6)
        on_dep = jnp.logical_and(node_a == 5 * (1 - dep), row_dep == 1 - dep)
        valid = (mer < N_MER - 1, mer > 0)
        for s, (c, to_lane) in enumerate(((5, 127), (0, 0))):
            sides = []
            for dd in (0, 1):
                base = mer_in[k, (s * 3 + 1) * 2 + dd]
                from_high = pltpu.roll(pltpu.roll(mer_in[k, (s * 3 + 0) * 2 + dd], 5, 1), 3, 0)
                from_low = pltpu.roll(pltpu.roll(mer_in[k, (s * 3 + 2) * 2 + dd], 123, 1), 5, 0)
                base = base + jnp.where(jnp.logical_and(node_b == 5, row_az == 3), from_high, zero)
                base = base + jnp.where(jnp.logical_and(node_b == 0, row_az == 0), from_low, zero)
                sides.append(base)
            up = pltpu.roll(pltpu.roll(sides[1], 30, 1), 4, 0)
            down = pltpu.roll(pltpu.roll(sides[1], 98, 1), 4, 0)
            other = jnp.where(dep == 0, up, down)
            total = sides[0] + jnp.where(on_dep, other, zero)
            total = jnp.where(valid[s], total, zero)
            for n in range(36):
                moved = pltpu.roll(total, (to_lane - n) % 128, 1)
                r = slice(n * 48 + c * 8, n * 48 + c * 8 + 8)
                field[r, :] = field[r, :] + jnp.where(lane == to_lane, moved, zero)

    def strip():
        total = jnp.zeros((4, 128), F32)
        out_strip = []
        for d in (0, 1):
            a, r = ((0, 0), (5, 4))[d]
            total = jnp.zeros((4, 128), F32)
            for n in range(36):
                first = a * PLANE + n * 8 + r
                total = total + face_weight[n * 4 : n * 4 + 4, :] * scaled[first : first + 4, :]
            out_strip.append(total)
        return jnp.where(dep == 0, out_strip[0], out_strip[1])

    loads[0].wait()
    loads[1].wait()
    loads[2].wait()
    coefficients(1)
    loads[3].wait()
    loads[4].wait()

    def scale_late(a, _):
        here = rows(a * PLANE, PLANE)
        scaled[here, :] = mass[here, :] * adj[here, :]
        return 0

    lax.fori_loop(0, 6, scale_late, 0)
    strip_late = strip()
    update()
    assemble_here()
    pl.semaphore_wait(barrier, len(peers))
    first_copies = face_copies(0)
    pack_and_start(0, first_copies)

    def add_mid(a, _):
        here = rows(a * PLANE, PLANE)
        mid[here, :] = adj[here, :] + upd[here, :]
        return 0

    lax.fori_loop(0, 6, add_mid, 0)
    loads[5].wait()
    coefficients(0)
    for copy in first_copies:
        copy.wait()
    add_halo(0, mid)

    def scale_early(a, _):
        here = rows(a * PLANE, PLANE)
        scaled[here, :] = mass[here, :] * mid[here, :]
        return 0

    lax.fori_loop(0, 6, scale_early, 0)
    strip_grad = STEP * (strip_late + strip())
    lane4 = lax.broadcasted_iota(jnp.int32, (4, 128), 1)
    suffix = strip_grad
    for shift in (1, 2, 4, 8, 16, 32, 64):
        suffix = suffix + jnp.where(lane4 < 128 - shift, pltpu.roll(suffix, 128 - shift, 1), 0.0)
    total = jnp.sum(strip_grad, axis=1, keepdims=True)
    tot_out[0:4, :] = jnp.broadcast_to(total, (4, 128))
    tot_out[4:8, :] = jnp.zeros((4, 128), F32)
    y_copies = []
    for k in range(1, MER_Y):
        y_copies.append(
            pltpu.make_async_remote_copy(
                src_ref=tot_out,
                dst_ref=tot_y.at[k],
                send_sem=tot_send.at[k],
                recv_sem=tot_recv.at[k],
                device_id=y_peer(k),
                device_id_type=MESH,
            )
        )
    for copy in y_copies:
        copy.start()
    update()
    assemble_here()
    second_copies = face_copies(1)
    pack_and_start(1, second_copies)

    for copy in y_copies:
        copy.wait()
    own_total = tot_out[...]
    carried = zero
    group = own_total
    for k in range(1, MER_Y):
        piece = tot_y[k]
        sender = lax.rem(mer_y - k + MER_Y, MER_Y)
        group = group + piece
        carried = carried + jnp.where(sender > mer_y, piece, zero)
    ysum_out[...] = group
    z_copies = []
    for k in range(1, MER_Z):
        z_copies.append(
            pltpu.make_async_remote_copy(
                src_ref=ysum_out,
                dst_ref=tot_z.at[k],
                send_sem=tot_send.at[MER_Y + k],
                recv_sem=tot_recv.at[MER_Y + k],
                device_id=z_peer(k),
                device_id_type=MESH,
            )
        )
    for copy in z_copies:
        copy.start()

    def add_out(a, _):
        here = rows(a * PLANE, PLANE)
        out[here, :] = mid[here, :] + upd[here, :]
        return 0

    lax.fori_loop(0, 6, add_out, 0)
    for copy in z_copies:
        copy.wait()
    for k in range(1, MER_Z):
        sender = lax.rem(mer_z - k + MER_Z, MER_Z)
        carried = carried + jnp.where(sender > mer_z, tot_z[k], zero)
    running = suffix + carried[0:4, :]

    flat = (az * N_MER + mer) * N_DEP + dep
    before = (lax.rem(az + N_AZ - 1, N_AZ) * N_MER + mer) * N_DEP + dep
    owners = owner[...]
    own = owners - flat * PAN_DEV
    prev = owners - before * PAN_DEV
    slot = jnp.where(
        jnp.logical_and(own >= 0, own < PAN_DEV),
        own,
        jnp.where(jnp.logical_and(prev >= 0, prev < PAN_DEV), prev + PAN_DEV, -1),
    )
    lines = [
        jnp.sum(jnp.where(slot == p, running, 0.0), axis=0, keepdims=True) for p in range(2 * PAN_DEV)
    ]
    lines = jnp.concatenate(lines + [jnp.zeros((128 - 2 * PAN_DEV, 128), F32)], axis=0)
    parts = lax.dot_general(
        jnp.ones((8, 128), F32),
        lines,
        (((1,), (1,)), ((), ())),
        precision=lax.Precision.HIGHEST,
        preferred_element_type=F32,
    )
    pan_out[...] = parts
    pan_copy = pltpu.make_async_remote_copy(
        src_ref=pan_out,
        dst_ref=pan_in,
        send_sem=pan_send,
        recv_sem=pan_recv,
        device_id=at(-1, 0, 0),
        device_id_type=MESH,
    )
    pan_copy.start()
    for copy in second_copies:
        copy.wait()
    add_halo(1, out)
    pan_copy.wait()
    whole = parts + pltpu.roll(pan_in[...], 128 - PAN_DEV, 1)
    panels[...] = whole[0:1, 0:PAN_DEV]


def shards(
    adjoint_end,
    temp_early,
    temp_late,
    mass_inverse,
    thermal_transport_coefficient,
    jacobian_quadrature_scales,
    measured,
    sensor_cell_slot,
    sensor_gridsite_slot,
    face_weight,
    panel_owner,
):
    shape = adjoint_end.shape

    def flat(array):
        return array.reshape(-1, 128)

    hbm = pl.BlockSpec(memory_space=pltpu.HBM)
    smem = pl.BlockSpec(memory_space=pltpu.SMEM)
    vmem = pl.BlockSpec(memory_space=pltpu.VMEM)
    field = pltpu.VMEM((ROWS, 128), F32)
    small = pltpu.VMEM((8, 128), F32)
    start, panel_grad = pl.pallas_call(
        kernel,
        out_shape=(
            jax.ShapeDtypeStruct((ROWS, 128), F32),
            jax.ShapeDtypeStruct((1, PAN_DEV), F32),
        ),
        in_specs=[hbm] * 6 + [smem] * 3 + [vmem] * 2,
        out_specs=(vmem, vmem),
        scratch_shapes=[
            field,
            pltpu.VMEM((2, ROWS, 128), jnp.bfloat16),
            field,
            field,
            pltpu.VMEM((3 * ROWS, 128), jnp.bfloat16),
            field,
            field,
            field,
            pltpu.VMEM((3, ROWS, 128), F32),
            pltpu.VMEM((3, ROWS, 128), F32),
            field,
            field,
            field,
            field,
            pltpu.VMEM((SENSORS, ROWS), jnp.bfloat16),
            pltpu.VMEM((2, 2, 72, 128), F32),
            pltpu.VMEM((2, 2, 72, 128), F32),
            pltpu.VMEM((2, 144, 128), F32),
            pltpu.VMEM((2, 144, 128), F32),
            pltpu.VMEM((2, 2, 8, 128), F32),
            pltpu.VMEM((2, 2, 8, 128), F32),
            pltpu.VMEM((2, 2, 8, 128), F32),
            pltpu.VMEM((2, 12, 8, 128), F32),
            small,
            pltpu.VMEM((MER_Y, 8, 128), F32),
            small,
            pltpu.VMEM((MER_Z, 8, 128), F32),
            small,
            small,
            pltpu.SemaphoreType.DMA((6,)),
            pltpu.SemaphoreType.DMA((2, 17)),
            pltpu.SemaphoreType.DMA((2, 17)),
            pltpu.SemaphoreType.DMA((MER_Y + MER_Z,)),
            pltpu.SemaphoreType.DMA((MER_Y + MER_Z,)),
            pltpu.SemaphoreType.DMA,
            pltpu.SemaphoreType.DMA,
        ],
        compiler_params=pltpu.CompilerParams(
            collective_id=0, has_side_effects=True, vmem_limit_bytes=48 * 1024 * 1024
        ),
        name="adjoint_steps",
    )(
        flat(adjoint_end),
        flat(temp_early),
        flat(temp_late),
        flat(mass_inverse),
        flat(thermal_transport_coefficient),
        flat(jacobian_quadrature_scales),
        measured,
        sensor_cell_slot,
        sensor_gridsite_slot,
        flat(face_weight),
        flat(panel_owner),
    )
    return start.reshape(shape), panel_grad.reshape(PAN_DEV)


def solution(mesh):
    field = P(None, None, None, "depth", "azimuth", "meridian")
    line = P(("azimuth", "meridian", "depth"))
    placed = (
        field,
        field,
        field,
        field,
        field,
        P(None, None, None, None, "depth", "azimuth", "meridian"),
        P(None, ("azimuth", "meridian", "depth")),
        line,
        line,
        P("depth", None, None, "azimuth", "meridian"),
        P("depth", "azimuth", "meridian"),
    )
    return jax.shard_map(shards, mesh=mesh, in_specs=placed, out_specs=(field, line), check_vma=False)
```

```python
import math

import jax
import jax.numpy as jnp
import numpy as np
from jax import lax
from jax.experimental import pallas as pl
from jax.experimental.pallas import tpu as pltpu
from jax.sharding import PartitionSpec as P

N_AZ, N_MER, N_DEP = 4, 32, 2
MER_Y, MER_Z = 4, 8
ROWS = 1728
PLANE = 288
PAN_DEV = 16
SENSORS = 16
STEP = 0.1
F32 = jnp.float32
MESH = pl.DeviceIdType.MESH


def gll_derivative():
    root_seven = math.sqrt(7.0)
    inner_near = math.sqrt((7.0 - 2.0 * root_seven) / 21.0)
    inner_far = math.sqrt((7.0 + 2.0 * root_seven) / 21.0)
    points = np.array([-1.0, -inner_far, -inner_near, inner_near, inner_far, 1.0])
    legendre = (63.0 * points**5 - 70.0 * points**3 + 15.0 * points) / 8.0
    entries = np.zeros((6, 6))
    for i in range(6):
        for j in range(6):
            if i != j:
                entries[i, j] = legendre[i] / (legendre[j] * (points[i] - points[j]))
    entries[0, 0] = -7.5
    entries[5, 5] = 7.5
    return entries


DER = gll_derivative()
FLIP = DER[:, ::-1]
GRAD_EVEN = (0.5 * (DER + FLIP))[:3, :3]
GRAD_ODD = (0.5 * (DER - FLIP))[:3, :3]
TRA = DER.T
DIV_EVEN = (0.5 * (TRA + TRA[:, ::-1]))[:3, :3]
DIV_ODD = (0.5 * (TRA - TRA[:, ::-1]))[:3, :3]


def grad_line(x):
    e = [x[j] + x[5 - j] for j in range(3)]
    o = [x[j] - x[5 - j] for j in range(3)]
    e1, e2 = e[1] - e[0], e[2] - e[0]
    p = [float(GRAD_EVEN[i, 1]) * e1 + float(GRAD_EVEN[i, 2]) * e2 for i in range(3)]
    q = [
        float(GRAD_ODD[i, 0]) * o[0] + float(GRAD_ODD[i, 1]) * o[1] + float(GRAD_ODD[i, 2]) * o[2]
        for i in range(3)
    ]
    return [q[i] + p[i] for i in range(3)] + [q[i] - p[i] for i in (2, 1, 0)]


def div_line(f):
    e = [f[j] + f[5 - j] for j in range(3)]
    o = [f[j] - f[5 - j] for j in range(3)]
    p = [
        float(DIV_EVEN[i, 0]) * e[0] + float(DIV_EVEN[i, 1]) * e[1] + float(DIV_EVEN[i, 2]) * e[2]
        for i in range(3)
    ]
    q1, q2 = [
        float(DIV_ODD[i, 0]) * o[0] + float(DIV_ODD[i, 1]) * o[1] + float(DIV_ODD[i, 2]) * o[2]
        for i in (1, 2)
    ]
    q0 = -(q1 + q2)
    q = [q0, q1, q2]
    return [q[i] + p[i] for i in range(3)] + [q[i] - p[i] for i in (2, 1, 0)]


def rows(start, size, multiple=8):
    if isinstance(start, int):
        return pl.ds(start, size)
    return pl.ds(pl.multiple_of(start, multiple), size)


def line_rows(direction, outer, inner):
    if direction == 0:
        return [rows(j * PLANE + outer * 48 + inner * 16, 16, 16) for j in range(6)]
    if direction == 1:
        return [rows(outer * PLANE + j * 48 + inner * 16, 16, 16) for j in range(6)]
    return [rows(outer * PLANE + inner * 48 + j * 8, 8, 8) for j in range(6)]


def inner_count(direction):
    return 6 if direction == 2 else 3


def kernel(
    adj_hbm,
    early_hbm,
    late_hbm,
    mass_hbm,
    cond_hbm,
    metric_hbm,
    measured_hbm,
    cell_hbm,
    site_hbm,
    face_weight_hbm,
    owner_hbm,
    out,
    panels,
    measured,
    cell,
    site,
    face_weight,
    owner,
    adj,
    temp,
    mass,
    cond,
    metric,
    heat,
    kap,
    slope,
    flux_c,
    cross_c,
    source,
    scaled,
    upd,
    mid,
    spots,
    az_out,
    az_in,
    dep_out,
    dep_in,
    ad_out,
    ad_in,
    mer_out,
    mer_in,
    tot_out,
    tot_y,
    ysum_out,
    tot_z,
    pan_out,
    pan_in,
    carry,
    load_sem,
    face_send,
    face_recv,
    tot_send,
    tot_recv,
    pan_send,
    pan_recv,
):
    az = lax.axis_index("azimuth")
    mer = lax.axis_index("meridian")
    dep = lax.axis_index("depth")
    mer_y = lax.rem(mer, MER_Y)
    mer_z = lax.div(mer, MER_Y)

    def at(da, dm, dd):
        return {
            "azimuth": lax.rem(az + (da + N_AZ), N_AZ),
            "meridian": mer + dm,
            "depth": lax.rem(dep + dd, N_DEP),
        }

    def y_peer(k):
        return {"azimuth": az, "meridian": mer_z * MER_Y + lax.rem(mer_y + k, MER_Y), "depth": dep}

    def z_peer(da, k):
        return {"azimuth": lax.rem(az + (da + N_AZ), N_AZ), "meridian": mer + k * MER_Y, "depth": dep}

    has_low, has_high = mer > 0, mer < N_MER - 1

    loads = [
        (late_hbm, temp.at[pl.ds(108, 108)]),
        (metric_hbm, metric),
        (cond_hbm, cond),
        (mass_hbm, mass),
        (adj_hbm, adj),
        (early_hbm, temp.at[pl.ds(0, 108)]),
        (site_hbm, site),
        (cell_hbm, cell),
        (measured_hbm, measured),
        (face_weight_hbm, face_weight),
        (owner_hbm, owner),
    ]
    loads = [pltpu.make_async_copy(s, d, load_sem.at[i]) for i, (s, d) in enumerate(loads)]
    for n in (6, 7, 8, 0, 5, 1, 2, 3, 4, 9, 10):
        loads[n].start()

    barrier = pltpu.get_barrier_semaphore()
    def greet(peer):
        pl.semaphore_signal(barrier, inc=1, device_id=peer, device_id_type=MESH)

    around = [(da, dd) for dd in (0, 1) for da in (-1, 0, 1)]
    for da, dd in around:
        if (da, dd) != (0, 0):
            greet(at(da, 0, dd))
    for there, dm in ((has_low, -1), (has_high, 1)):

        @pl.when(there)
        def _():
            for da, dd in around:
                greet(at(da, dm, dd))

    for k in range(1, MER_Y):
        greet(y_peer(k))
    for k in range(1, MER_Z):

        @pl.when(mer_z + k < MER_Z)
        def _():
            for da in (0, 1):
                greet(z_peer(da, k))

    greeted = 5 + 3 + 6 * (has_low.astype(jnp.int32) + has_high.astype(jnp.int32)) + 2 * mer_z

    row8 = lax.broadcasted_iota(jnp.int32, (8, 128), 0)
    lane = lax.broadcasted_iota(jnp.int32, (8, 128), 1)
    row_az = lax.rem(row8, 4)
    row_dep = lax.div(row8, 4)
    zero = jnp.zeros((8, 128), F32)

    lane1 = lax.broadcasted_iota(jnp.int32, (1, 128), 1)
    row16 = lax.broadcasted_iota(jnp.int32, (16, 128), 0)
    lane16 = lax.broadcasted_iota(jnp.int32, (16, 128), 1)
    for n in (6, 7, 8):
        loads[n].wait()
    code = jnp.full((1, 128), -1, jnp.int32)
    for q in range(SENSORS):
        word = site[q] * 8 + lax.shift_right_logical(cell[q], 7)
        code = jnp.where(jnp.logical_and(lax.rem(lane1, SENSORS) == q, lane1 < 3 * SENSORS), word, code)
    loads[0].wait()
    loads[5].wait()
    tables = []
    for k in (0, 1):
        for q in range(SENSORS):
            tile_row = jnp.bitwise_and(site[q], 1) * 8 + lax.shift_right_logical(cell[q], 7)
            there = jnp.logical_and(row16 == tile_row, lane16 == jnp.bitwise_and(cell[q], 127))
            felt = temp[k * 108 + lax.shift_right_logical(site[q], 1)].astype(F32)
            value = jnp.where(there, felt - measured[k, q], 0.0)
            spots[k, q : q + 1, :] = jnp.sum(value, axis=0, keepdims=True)
        value = spots[k]
        high = value.astype(jnp.bfloat16).astype(F32)
        rest = value - high
        middle = rest.astype(jnp.bfloat16).astype(F32)
        low = rest - middle
        tables.append(jnp.concatenate([high, middle, low, jnp.zeros((80, 128), F32)], axis=0).astype(jnp.bfloat16))
    table = jnp.concatenate(tables, axis=1)

    def place(a, _):
        base = lax.broadcasted_iota(jnp.int32, (PLANE, 128), 0) + a * PLANE
        hot = jnp.where(base == code, 1.0, 0.0).astype(jnp.bfloat16)
        both = jnp.dot(hot, table, preferred_element_type=F32)
        source[0, rows(a * PLANE, PLANE), :] = both[:, 0:128]
        source[1, rows(a * PLANE, PLANE), :] = both[:, 128:256]
        return 0

    lax.fori_loop(0, 6, place, 0)

    def coefficients(k):
        def plane(a, _):
            here = rows(a * PLANE, PLANE, 16)
            h = temp[pl.ds(k * 108 + a * 18, 18)].astype(F32).reshape(PLANE, 128)
            heat[here, :] = h
            c = (-STEP) * cond[here, :]
            kap[here, :] = c * (1.0 + 0.5 * h * h)
            slope[here, :] = c * h
            return 0

        lax.fori_loop(0, 6, plane, 0)

        def direction(d):
            def body(outer, _):
                for inner in range(inner_count(d)):
                    at_rows = line_rows(d, outer, inner)
                    g = grad_line([heat[r, :] for r in at_rows])
                    if d == 2:
                        w = metric[rows(2 * ROWS + outer * PLANE + inner * 48, 48, 16), :].astype(F32)
                        w = [w[8 * j : 8 * j + 8] for j in range(6)]
                    else:
                        first = (0, outer * 48 + inner * 16)[d == 0] if d == 0 else outer * PLANE + inner * 16
                        stride = PLANE if d == 0 else 48
                        w = [
                            metric[rows(d * ROWS + first + j * stride, 16, 16), :].astype(F32)
                            for j in range(6)
                        ]
                    for j, r in enumerate(at_rows):
                        flux_c[d, r, :] = kap[r, :] * w[j]
                        cross_c[d, r, :] = slope[r, :] * w[j] * g[j]
                return 0

            lax.fori_loop(0, 6, body, 0)

        for d in range(3):
            direction(d)

    def update(k, between=None):
        def direction(d):
            def body(outer, _):
                for inner in range(inner_count(d)):
                    at_rows = line_rows(d, outer, inner)
                    g = grad_line([scaled[r, :] for r in at_rows])
                    flux = [flux_c[d, r, :] * g[j] for j, r in enumerate(at_rows)]
                    spread = div_line(flux)
                    for j, r in enumerate(at_rows):
                        total = spread[j] + cross_c[d, r, :] * g[j]
                        before = source[k, r, :] if d == 1 else upd[r, :]
                        upd[r, :] = before + total
                return 0

            lax.fori_loop(0, 6, body, 0)

        direction(1)
        direction(2)
        if between is not None:
            between()
        direction(0)

    def assemble_here():
        def azimuth(a, _):
            for c in range(6):
                lo, hi = (rows(a * PLANE + b * 48 + c * 8, 8) for b in (0, 5))
                low, high = upd[lo, :], upd[hi, :]
                upd[hi, :] = high + jnp.where(row_az < 3, pltpu.roll(low, 7, 0), zero)
                upd[lo, :] = low + jnp.where(row_az > 0, pltpu.roll(high, 1, 0), zero)
            return 0

        lax.fori_loop(0, 6, azimuth, 0)

        def meridian(a, _):
            for b in range(6):
                lo, hi = (rows(a * PLANE + b * 48 + c * 8, 8) for c in (0, 5))
                low, high = upd[lo, :], upd[hi, :]
                upd[hi, :] = high + jnp.where(lane < 127, pltpu.roll(low, 127, 1), zero)
                upd[lo, :] = low + jnp.where(lane > 0, pltpu.roll(high, 1, 1), zero)
            return 0

        lax.fori_loop(0, 6, meridian, 0)

        def depth(b, _):
            for c in range(6):
                lo, hi = (rows(a * PLANE + b * 48 + c * 8, 8) for a in (0, 5))
                low, high = upd[lo, :], upd[hi, :]
                upd[hi, :] = high + jnp.where(row_dep == 0, pltpu.roll(low, 4, 0), zero)
                upd[lo, :] = low + jnp.where(row_dep == 1, pltpu.roll(high, 4, 0), zero)
            return 0

        lax.fori_loop(0, 6, depth, 0)

    def face_copies(k):
        copies = []

        def add(offset, src, dst):
            n = len(copies)
            copies.append(
                pltpu.make_async_remote_copy(
                    src_ref=src,
                    dst_ref=dst,
                    send_sem=face_send.at[k, n],
                    recv_sem=face_recv.at[k, n],
                    device_id=at(*offset),
                    device_id_type=MESH,
                )
            )

        for s, da in enumerate((-1, 1)):
            add((da, 0, 0), az_out.at[k, s], az_in.at[k, s])
        add((0, 0, 1), dep_out.at[k], dep_in.at[k])
        for s, da in enumerate((-1, 1)):
            add((da, 0, 1), ad_out.at[k, s], ad_in.at[k, s])
        for s, dm in enumerate((-1, 1)):
            for i, da in enumerate((-1, 0, 1)):
                for dd in (0, 1):
                    add((da, dm, dd), mer_out.at[k, s], mer_in.at[k, (s * 3 + i) * 2 + dd])
        return copies

    def pack_and_start(k, copies):
        for s, (b, e) in enumerate(((0, 0), (5, 3))):
            for a in range(6):
                first = a * PLANE + b * 48 + e
                az_out[k, s, a * 12 : a * 12 + 8, :] = upd[pl.ds(first, 8, stride=4), :]
                az_out[k, s, a * 12 + 8 : a * 12 + 12, :] = upd[pl.ds(first + 32, 4, stride=4), :]
            copies[s].start()

        for d in (0, 1):
            a, r = ((5, 4), (0, 0))[d]

            @pl.when(dep == d)
            def _():
                for n in range(36):
                    first = a * PLANE + n * 8 + r
                    dep_out[k, n * 4 : n * 4 + 4, :] = upd[first : first + 4, :]
                for s, (b, e) in enumerate(((0, 0), (5, 3))):
                    first = a * PLANE + b * 48 + r + e
                    ad_out[k, s, 0:6, :] = upd[pl.ds(first, 6, stride=8), :]

        copies[2].start()
        copies[3].start()
        copies[4].start()
        packed = [zero, zero]
        for n in range(36):
            for s, (c, shift) in enumerate(((0, n), (5, (n + 1) % 128))):
                moved = pltpu.roll(upd[n * 48 + c * 8 : n * 48 + c * 8 + 8, :], shift, 1)
                packed[s] = jnp.where(lane == n, moved, packed[s])
        for s in (0, 1):
            mer_out[k, s] = packed[s]
        for s, there in enumerate((has_low, has_high)):

            @pl.when(there)
            def _():
                for copy in copies[5 + 6 * s : 11 + 6 * s]:
                    copy.start()

    def finish(copies):
        for copy in copies[:5]:
            copy.wait()
        for s, (to, came) in enumerate(((has_low, has_high), (has_high, has_low))):

            @pl.when(to)
            def _():
                for copy in copies[5 + 6 * s : 11 + 6 * s]:
                    copy.wait_send()

            @pl.when(came)
            def _():
                for copy in copies[5 + 6 * s : 11 + 6 * s]:
                    copy.wait_recv()

    def add_halo(k, field):
        for s, (b, e) in enumerate(((5, 3), (0, 0))):
            for a in range(6):
                first = a * PLANE + b * 48 + e
                for skip, count in ((0, 8), (8, 4)):
                    r = pl.ds(first + 4 * skip, count, stride=4)
                    field[r, :] = field[r, :] + az_in[k, s, a * 12 + skip : a * 12 + skip + count, :]

        for d in (0, 1):
            a, r = ((5, 4), (0, 0))[d]

            @pl.when(dep == d)
            def _():
                for n in range(36):
                    first = a * PLANE + n * 8 + r
                    field[first : first + 4, :] = (
                        field[first : first + 4, :] + dep_in[k, n * 4 : n * 4 + 4, :]
                    )
                for s, (b, e) in enumerate(((5, 3), (0, 0))):
                    there = pl.ds(a * PLANE + b * 48 + r + e, 6, stride=8)
                    field[there, :] = field[there, :] + ad_in[k, s, 0:6, :]

        node_a, node_b = lax.div(lane, 6), lax.rem(lane, 6)
        on_dep = jnp.logical_and(node_a == 5 * (1 - dep), row_dep == 1 - dep)
        for s, (c, to_lane, there) in enumerate(((5, 127, has_high), (0, 0, has_low))):

            @pl.when(there)
            def _():
                sides = []
                for dd in (0, 1):
                    base = mer_in[k, (s * 3 + 1) * 2 + dd]
                    from_high = pltpu.roll(pltpu.roll(mer_in[k, (s * 3 + 0) * 2 + dd], 5, 1), 3, 0)
                    from_low = pltpu.roll(pltpu.roll(mer_in[k, (s * 3 + 2) * 2 + dd], 123, 1), 5, 0)
                    base = base + jnp.where(jnp.logical_and(node_b == 5, row_az == 3), from_high, zero)
                    base = base + jnp.where(jnp.logical_and(node_b == 0, row_az == 0), from_low, zero)
                    sides.append(base)
                up = pltpu.roll(pltpu.roll(sides[1], 30, 1), 4, 0)
                down = pltpu.roll(pltpu.roll(sides[1], 98, 1), 4, 0)
                other = jnp.where(dep == 0, up, down)
                total = sides[0] + jnp.where(on_dep, other, zero)
                for n in range(36):
                    moved = pltpu.roll(total, (to_lane - n) % 128, 1)
                    r = slice(n * 48 + c * 8, n * 48 + c * 8 + 8)
                    field[r, :] = field[r, :] + jnp.where(lane == to_lane, moved, zero)

    def strip():
        total = jnp.zeros((4, 128), F32)
        out_strip = []
        for d in (0, 1):
            a, r = ((0, 0), (5, 4))[d]
            total = jnp.zeros((4, 128), F32)
            for n in range(36):
                first = a * PLANE + n * 8 + r
                total = total + face_weight[n * 4 : n * 4 + 4, :] * scaled[first : first + 4, :]
            out_strip.append(total)
        return jnp.where(dep == 0, out_strip[0], out_strip[1])

    loads[1].wait()
    loads[2].wait()
    coefficients(1)
    loads[3].wait()
    loads[4].wait()

    def scale_late(a, _):
        here = rows(a * PLANE, PLANE)
        scaled[here, :] = mass[here, :] * adj[here, :]
        return 0

    lax.fori_loop(0, 6, scale_late, 0)
    loads[9].wait()
    strip_late = strip()
    update(1)
    assemble_here()
    pl.semaphore_wait(barrier, greeted)
    first_copies = face_copies(0)
    pack_and_start(0, first_copies)

    def add_mid(a, _):
        here = rows(a * PLANE, PLANE)
        mid[here, :] = adj[here, :] + upd[here, :]
        return 0

    lax.fori_loop(0, 6, add_mid, 0)
    coefficients(0)
    finish(first_copies)
    add_halo(0, mid)

    def scale_early(a, _):
        here = rows(a * PLANE, PLANE)
        scaled[here, :] = mass[here, :] * mid[here, :]
        return 0

    lax.fori_loop(0, 6, scale_early, 0)
    strip_grad = STEP * (strip_late + strip())
    lane4 = lax.broadcasted_iota(jnp.int32, (4, 128), 1)
    suffix = strip_grad
    for shift in (1, 2, 4, 8, 16, 32, 64):
        suffix = suffix + jnp.where(lane4 < 128 - shift, pltpu.roll(suffix, 128 - shift, 1), 0.0)
    total = jnp.broadcast_to(jnp.sum(strip_grad, axis=1, keepdims=True), (4, 128))
    group_of = lax.div(lane1, 2 * PAN_DEV)
    mine = jnp.zeros((1, 128), F32)
    for e in range(4):
        mine = jnp.where(group_of == e, total[e : e + 1, :], mine)
    tot_out[...] = jnp.broadcast_to(mine, (8, 128))

    def tot_copy(src, dst, n, peer):
        return pltpu.make_async_remote_copy(
            src_ref=src,
            dst_ref=dst,
            send_sem=tot_send.at[n],
            recv_sem=tot_recv.at[n],
            device_id=peer,
            device_id_type=MESH,
        )

    y_copies = [tot_copy(tot_out, tot_y.at[k], k, y_peer(k)) for k in range(1, MER_Y)]
    for copy in y_copies:
        copy.start()
    z_copies = [
        [tot_copy(ysum_out, tot_z.at[-da, k], MER_Y + MER_Z * -da + k, z_peer(da, -k)) for da in (0, -1)]
        for k in range(1, MER_Z)
    ]

    def pass_totals():
        for copy in y_copies:
            copy.wait()
        group = tot_out[...]
        above = zero
        for k in range(1, MER_Y):
            piece = tot_y[k]
            sender = lax.rem(mer_y - k + MER_Y, MER_Y)
            group = group + piece
            above = above + jnp.where(sender > mer_y, piece, zero)
        ysum_out[...] = group
        carry[0] = above
        pan_out[2] = above
        for k in range(1, MER_Z):

            @pl.when(mer_z >= k)
            def _():
                for copy in z_copies[k - 1]:
                    copy.start()

    update(0, pass_totals)
    assemble_here()
    second_copies = face_copies(1)
    pack_and_start(1, second_copies)

    flat = (az * N_MER + mer) * N_DEP + dep
    before = (lax.rem(az + N_AZ - 1, N_AZ) * N_MER + mer) * N_DEP + dep
    loads[10].wait()
    owners = owner[...]
    own = owners - flat * PAN_DEV
    prev = owners - before * PAN_DEV
    slot = jnp.where(
        jnp.logical_and(own >= 0, own < PAN_DEV),
        own,
        jnp.where(jnp.logical_and(prev >= 0, prev < PAN_DEV), prev + PAN_DEV, -1),
    )
    panel = lax.broadcasted_iota(jnp.int32, (2 * PAN_DEV, 128), 0)
    hits = [jnp.broadcast_to(slot[e : e + 1, :], (2 * PAN_DEV, 128)) == panel for e in range(4)]
    counts = jnp.concatenate([jnp.where(hit, 1.0, 0.0) for hit in hits], axis=0)
    parts = jnp.concatenate(
        [jnp.where(hits[e], jnp.broadcast_to(suffix[e : e + 1, :], (2 * PAN_DEV, 128)), 0.0) for e in range(4)], axis=0
    )

    def lane_sums(values, precision):
        return lax.dot_general(
            jnp.ones((8, 128), values.dtype),
            values,
            (((1,), (1,)), ((), ())),
            precision=precision,
            preferred_element_type=F32,
        )

    counts = lane_sums(counts.astype(jnp.bfloat16), None)
    parts = lane_sums(parts, lax.Precision.HIGHEST)
    pan_out[0] = parts
    pan_out[1] = counts
    pan_copy = pltpu.make_async_remote_copy(
        src_ref=pan_out,
        dst_ref=pan_in,
        send_sem=pan_send,
        recv_sem=pan_recv,
        device_id=at(-1, 0, 0),
        device_id_type=MESH,
    )
    pan_copy.start()

    def add_out(a, _):
        here = rows(a * PLANE, PLANE)
        out[here, :] = mid[here, :] + upd[here, :]
        return 0

    lax.fori_loop(0, 6, add_out, 0)
    finish(second_copies)
    add_halo(1, out)

    pan_copy.wait()
    carry[1] = pan_in[2]
    for k in range(1, MER_Z):

        @pl.when(mer_z >= k)
        def _():
            for copy in z_copies[k - 1]:
                copy.wait_send()

        @pl.when(mer_z + k < MER_Z)
        def _():
            for s, copy in enumerate(z_copies[k - 1]):
                copy.wait_recv()
                carry[s] = carry[s] + tot_z[s, k]

    whole = parts + counts * carry[0]
    other = pan_in[0] + pan_in[1] * carry[1]
    whole = whole + pltpu.roll(other, 128 - PAN_DEV, 1)
    whole = whole + pltpu.roll(whole, 64, 1)
    whole = whole + pltpu.roll(whole, 96, 1)
    panels[...] = whole[0:1, 0:PAN_DEV]


def shards(
    adjoint_end,
    temp_early,
    temp_late,
    mass_inverse,
    thermal_transport_coefficient,
    jacobian_quadrature_scales,
    measured,
    sensor_cell_slot,
    sensor_gridsite_slot,
    face_weight,
    panel_owner,
):
    shape = adjoint_end.shape

    def flat(array):
        return array.reshape(-1, 128)

    hbm = pl.BlockSpec(memory_space=pltpu.HBM)
    vmem = pl.BlockSpec(memory_space=pltpu.VMEM)
    field = pltpu.VMEM((ROWS, 128), F32)
    small = pltpu.VMEM((8, 128), F32)
    start, panel_grad = pl.pallas_call(
        kernel,
        out_shape=(
            pltpu.VMEM((ROWS, 128), F32),
            pltpu.VMEM((1, PAN_DEV), F32),
        ),
        in_specs=[hbm] * 11,
        out_specs=(vmem, vmem),
        scratch_shapes=[
            pltpu.SMEM((2, SENSORS), F32),
            pltpu.SMEM((SENSORS,), jnp.int32),
            pltpu.SMEM((SENSORS,), jnp.int32),
            pltpu.VMEM((144, 128), F32),
            pltpu.VMEM((4, 128), jnp.int32),
            field,
            pltpu.VMEM((216, 16, 128), jnp.bfloat16),
            field,
            field,
            pltpu.VMEM((3 * ROWS, 128), jnp.bfloat16),
            field,
            field,
            field,
            pltpu.VMEM((3, ROWS, 128), F32),
            pltpu.VMEM((3, ROWS, 128), F32),
            pltpu.VMEM((2, ROWS, 128), F32),
            field,
            field,
            field,
            pltpu.VMEM((2, SENSORS, 128), F32),
            pltpu.VMEM((2, 2, 72, 128), F32),
            pltpu.VMEM((2, 2, 72, 128), F32),
            pltpu.VMEM((2, 144, 128), F32),
            pltpu.VMEM((2, 144, 128), F32),
            pltpu.VMEM((2, 2, 8, 128), F32),
            pltpu.VMEM((2, 2, 8, 128), F32),
            pltpu.VMEM((2, 2, 8, 128), F32),
            pltpu.VMEM((2, 12, 8, 128), F32),
            small,
            pltpu.VMEM((MER_Y, 8, 128), F32),
            small,
            pltpu.VMEM((2, MER_Z, 8, 128), F32),
            pltpu.VMEM((3, 8, 128), F32),
            pltpu.VMEM((3, 8, 128), F32),
            pltpu.VMEM((2, 8, 128), F32),
            pltpu.SemaphoreType.DMA((11,)),
            pltpu.SemaphoreType.DMA((2, 17)),
            pltpu.SemaphoreType.DMA((2, 17)),
            pltpu.SemaphoreType.DMA((MER_Y + 2 * MER_Z,)),
            pltpu.SemaphoreType.DMA((MER_Y + 2 * MER_Z,)),
            pltpu.SemaphoreType.DMA,
            pltpu.SemaphoreType.DMA,
        ],
        compiler_params=pltpu.CompilerParams(
            collective_id=0, has_side_effects=True, vmem_limit_bytes=60 * 1024 * 1024
        ),
        name="adjoint_steps",
    )(
        flat(adjoint_end),
        temp_early.reshape(108, 16, 128),
        temp_late.reshape(108, 16, 128),
        flat(mass_inverse),
        flat(thermal_transport_coefficient),
        flat(jacobian_quadrature_scales),
        measured,
        sensor_cell_slot,
        sensor_gridsite_slot,
        flat(face_weight),
        flat(panel_owner),
    )
    return start.reshape(shape), panel_grad.reshape(PAN_DEV)


def solution(mesh):
    field = P(None, None, None, "depth", "azimuth", "meridian")
    line = P(("azimuth", "meridian", "depth"))
    placed = (
        field,
        field,
        field,
        field,
        field,
        P(None, None, None, None, "depth", "azimuth", "meridian"),
        P(None, ("azimuth", "meridian", "depth")),
        line,
        line,
        P("depth", None, None, "azimuth", "meridian"),
        P("depth", "azimuth", "meridian"),
    )
    return jax.shard_map(shards, mesh=mesh, in_specs=placed, out_specs=(field, line), check_vma=False)
```

```python
import math

import jax
import jax.numpy as jnp
import numpy as np
from jax import lax
from jax.experimental import pallas as pl
from jax.experimental.pallas import tpu as pltpu
from jax.sharding import PartitionSpec as P

N_AZ, N_MER, N_DEP = 4, 32, 2
MER_Y, MER_Z = 4, 8
ROWS = 1728
PLANE = 288
PAN_DEV = 16
SENSORS = 16
STEP = 0.1
F32 = jnp.float32
MESH = pl.DeviceIdType.MESH


def gll_derivative():
    root_seven = math.sqrt(7.0)
    inner_near = math.sqrt((7.0 - 2.0 * root_seven) / 21.0)
    inner_far = math.sqrt((7.0 + 2.0 * root_seven) / 21.0)
    points = np.array([-1.0, -inner_far, -inner_near, inner_near, inner_far, 1.0])
    legendre = (63.0 * points**5 - 70.0 * points**3 + 15.0 * points) / 8.0
    entries = np.zeros((6, 6))
    for i in range(6):
        for j in range(6):
            if i != j:
                entries[i, j] = legendre[i] / (legendre[j] * (points[i] - points[j]))
    entries[0, 0] = -7.5
    entries[5, 5] = 7.5
    return entries


DER = gll_derivative()
FLIP = DER[:, ::-1]
GRAD_EVEN = (0.5 * (DER + FLIP))[:3, :3]
GRAD_ODD = (0.5 * (DER - FLIP))[:3, :3]
TRA = DER.T
DIV_EVEN = (0.5 * (TRA + TRA[:, ::-1]))[:3, :3]
DIV_ODD = (0.5 * (TRA - TRA[:, ::-1]))[:3, :3]


def grad_line(x):
    e = [x[j] + x[5 - j] for j in range(3)]
    o = [x[j] - x[5 - j] for j in range(3)]
    e1, e2 = e[1] - e[0], e[2] - e[0]
    p = [float(GRAD_EVEN[i, 1]) * e1 + float(GRAD_EVEN[i, 2]) * e2 for i in range(3)]
    q = [
        float(GRAD_ODD[i, 0]) * o[0] + float(GRAD_ODD[i, 1]) * o[1] + float(GRAD_ODD[i, 2]) * o[2]
        for i in range(3)
    ]
    return [q[i] + p[i] for i in range(3)] + [q[i] - p[i] for i in (2, 1, 0)]


def div_line(f):
    e = [f[j] + f[5 - j] for j in range(3)]
    o = [f[j] - f[5 - j] for j in range(3)]
    p = [
        float(DIV_EVEN[i, 0]) * e[0] + float(DIV_EVEN[i, 1]) * e[1] + float(DIV_EVEN[i, 2]) * e[2]
        for i in range(3)
    ]
    q1, q2 = [
        float(DIV_ODD[i, 0]) * o[0] + float(DIV_ODD[i, 1]) * o[1] + float(DIV_ODD[i, 2]) * o[2]
        for i in (1, 2)
    ]
    q0 = -(q1 + q2)
    q = [q0, q1, q2]
    return [q[i] + p[i] for i in range(3)] + [q[i] - p[i] for i in (2, 1, 0)]


def rows(start, size, multiple=8):
    if isinstance(start, int):
        return pl.ds(start, size)
    return pl.ds(pl.multiple_of(start, multiple), size)


def line_rows(direction, outer, inner):
    if direction == 0:
        return [rows(j * PLANE + outer * 48 + inner * 16, 16, 16) for j in range(6)]
    if direction == 1:
        return [rows(outer * PLANE + j * 48 + inner * 16, 16, 16) for j in range(6)]
    return [rows(outer * PLANE + inner * 48 + j * 8, 8, 8) for j in range(6)]


def inner_count(direction):
    return 6 if direction == 2 else 3


def kernel(
    adj_hbm,
    early_hbm,
    late_hbm,
    mass_hbm,
    cond_hbm,
    metric_hbm,
    measured_hbm,
    cell_hbm,
    site_hbm,
    face_weight_hbm,
    owner_hbm,
    out,
    panels,
    measured,
    cell,
    site,
    face_weight,
    owner,
    adj,
    temp_early,
    temp_late,
    mass,
    cond,
    metric,
    heat,
    flux_c,
    cross_c,
    source,
    hot,
    scaled,
    upd,
    mid,
    spots,
    az_out,
    az_in,
    dep_out,
    dep_in,
    mer_out,
    mer_in,
    tot_out,
    tot_y,
    ysum_out,
    tot_z,
    pan_out,
    pan_in,
    carry,
    load_sem,
    face_send,
    face_recv,
    tot_send,
    tot_recv,
    pan_send,
    pan_recv,
):
    az = lax.axis_index("azimuth")
    mer = lax.axis_index("meridian")
    dep = lax.axis_index("depth")
    mer_y = lax.rem(mer, MER_Y)
    mer_z = lax.div(mer, MER_Y)

    def at(da, dm, dd):
        return {
            "azimuth": lax.rem(az + (da + N_AZ), N_AZ),
            "meridian": mer + dm,
            "depth": lax.rem(dep + dd, N_DEP),
        }

    def y_peer(k):
        return {"azimuth": az, "meridian": mer_z * MER_Y + lax.rem(mer_y + k, MER_Y), "depth": dep}

    def z_peer(da, k):
        return {"azimuth": lax.rem(az + (da + N_AZ), N_AZ), "meridian": mer + k * MER_Y, "depth": dep}

    has_low, has_high = mer > 0, mer < N_MER - 1

    loads = [
        (late_hbm, temp_late),
        (metric_hbm, metric),
        (cond_hbm, cond),
        (mass_hbm, mass),
        (adj_hbm, adj),
        (early_hbm, temp_early),
        (site_hbm, site),
        (cell_hbm, cell),
        (measured_hbm, measured),
        (face_weight_hbm, face_weight),
        (owner_hbm, owner),
    ]
    loads = [pltpu.make_async_copy(s, d, load_sem.at[i]) for i, (s, d) in enumerate(loads)]
    for n in (6, 7, 0, 8, 1, 2, 3, 4, 9, 5, 10):
        loads[n].start()

    barrier = pltpu.get_barrier_semaphore()
    def greet(peer):
        pl.semaphore_signal(barrier, inc=1, device_id=peer, device_id_type=MESH)

    greet(at(0, 0, 1))
    greet(at(-1, 0, 0))
    greet(at(1, 0, 0))
    for there, dm in ((has_low, -1), (has_high, 1)):

        @pl.when(there)
        def _():
            for da in (-1, 0, 1):
                greet(at(da, dm, 0))

    for k in range(1, MER_Y):
        greet(y_peer(k))
    for k in range(1, MER_Z):

        @pl.when(mer_z + k < MER_Z)
        def _():
            for da in (0, 1):
                greet(z_peer(da, k))

    greeted = 3 + 3 + 3 * (has_low.astype(jnp.int32) + has_high.astype(jnp.int32)) + 2 * mer_z

    row8 = lax.broadcasted_iota(jnp.int32, (8, 128), 0)
    lane = lax.broadcasted_iota(jnp.int32, (8, 128), 1)
    row_az = lax.rem(row8, 4)
    row_dep = lax.div(row8, 4)
    zero = jnp.zeros((8, 128), F32)

    lane1 = lax.broadcasted_iota(jnp.int32, (1, 128), 1)
    row16 = lax.broadcasted_iota(jnp.int32, (16, 128), 0)
    lane16 = lax.broadcasted_iota(jnp.int32, (16, 128), 1)
    for n in (6, 7):
        loads[n].wait()
    code = jnp.full((1, 128), -1, jnp.int32)
    for q in range(SENSORS):
        word = site[q] * 8 + lax.shift_right_logical(cell[q], 7)
        code = jnp.where(jnp.logical_and(lax.rem(lane1, SENSORS) == q, lane1 < 3 * SENSORS), word, code)

    def place(a, _):
        base = lax.broadcasted_iota(jnp.int32, (PLANE, 128), 0) + a * PLANE
        hot[rows(a * PLANE, PLANE, 16), :] = jnp.where(base == code, 1.0, 0.0).astype(jnp.bfloat16)
        return 0

    lax.fori_loop(0, 6, place, 0)

    temps = (temp_early, temp_late)

    def felt_table(k):
        for q in range(SENSORS):
            tile_row = jnp.bitwise_and(site[q], 1) * 8 + lax.shift_right_logical(cell[q], 7)
            there = jnp.logical_and(row16 == tile_row, lane16 == jnp.bitwise_and(cell[q], 127))
            felt = temps[k][lax.shift_right_logical(site[q], 1)].astype(F32)
            value = jnp.where(there, felt - measured[k, q], 0.0)
            spots[k, q : q + 1, :] = jnp.sum(value, axis=0, keepdims=True)
        value = spots[k]
        high = value.astype(jnp.bfloat16).astype(F32)
        rest = value - high
        middle = rest.astype(jnp.bfloat16).astype(F32)
        low = rest - middle
        return jnp.concatenate([high, middle, low, jnp.zeros((80, 128), F32)], axis=0).astype(jnp.bfloat16)

    def heat_gradients(k):
        def plane(a, _):
            h = temps[k][pl.ds(a * 18, 18)].astype(F32).reshape(PLANE, 128)
            heat[rows(a * PLANE, PLANE), :] = h
            return 0

        lax.fori_loop(0, 6, plane, 0)

        def direction(d):
            def body(outer, _):
                for inner in range(inner_count(d)):
                    at_rows = line_rows(d, outer, inner)
                    for r, g in zip(at_rows, grad_line([heat[r, :] for r in at_rows])):
                        cross_c[d, r, :] = g
                return 0

            lax.fori_loop(0, 6, body, 0)

        for d in range(3):
            direction(d)

    def coefficients(table):
        def plane(a, _):
            for part in range(6):
                first = a * PLANE + part * 48
                r = rows(first, 48, 16)
                h = heat[r, :]
                c = (-STEP) * cond[r, :]
                kap = c * (1.0 + 0.5 * h * h)
                slope = c * h
                for d in range(3):
                    w = metric[rows(d * ROWS + first, 48, 16), :].astype(F32)
                    flux_c[d, r, :] = kap * w
                    cross_c[d, r, :] = slope * w * cross_c[d, r, :]
            here = rows(a * PLANE, PLANE, 16)
            source[here, :] = jnp.dot(hot[here, :], table, preferred_element_type=F32)
            return 0

        lax.fori_loop(0, 6, plane, 0)

    def update(between=None):
        def direction(d):
            def body(outer, _):
                for inner in range(inner_count(d)):
                    at_rows = line_rows(d, outer, inner)
                    g = grad_line([scaled[r, :] for r in at_rows])
                    flux = [flux_c[d, r, :] * g[j] for j, r in enumerate(at_rows)]
                    spread = div_line(flux)
                    for j, r in enumerate(at_rows):
                        total = spread[j] + cross_c[d, r, :] * g[j]
                        before = source[r, :] if d == 1 else upd[r, :]
                        upd[r, :] = before + total
                return 0

            lax.fori_loop(0, 6, body, 0)

        direction(1)
        direction(2)
        if between is not None:
            between()
        direction(0)

    row7_az = row_az[0:7]

    def assemble_azimuth_depth():
        for a in range(6):
            for c in range(6):
                lo, hi = (a * PLANE + b * 48 + c * 8 for b in (0, 5))
                low, high = upd[lo + 1 : lo + 8, :], upd[hi : hi + 7, :]
                both = low + high
                upd[hi : hi + 7, :] = jnp.where(row7_az < 3, both, high)
                upd[lo + 1 : lo + 8, :] = jnp.where(row7_az < 3, both, low)
        for n in range(36):
            lo, hi = n * 8 + 4, 5 * PLANE + n * 8
            both = upd[lo : lo + 4, :] + upd[hi : hi + 4, :]
            upd[lo : lo + 4, :] = both
            upd[hi : hi + 4, :] = both

    def assemble_meridian(planes, packed):
        for a in planes:
            for b in range(0, 6, 2):
                ends = []
                for n in (a * 6 + b, a * 6 + b + 1):
                    lo, hi = slice(n * 48, n * 48 + 8), slice(n * 48 + 40, n * 48 + 48)
                    low, high = upd[lo, :], upd[hi, :]
                    low_moved, high_moved = pltpu.roll(low, 127, 1), pltpu.roll(high, 1, 1)
                    upd[hi, :] = high + jnp.where(lane < 127, low_moved, zero)
                    upd[lo, :] = low + jnp.where(lane > 0, high_moved, zero)
                    ends.append((low, low_moved, high, high_moved))
                n = a * 6 + b
                pairs = (
                    jnp.where(lane == 127, ends[0][1], ends[1][0]),
                    jnp.where(lane == 127, ends[0][2], ends[1][3]),
                )
                for s in (0, 1):
                    moved = pltpu.roll(pairs[s], n + 1, 1)
                    packed[s] = jnp.where(jnp.logical_or(lane == n, lane == n + 1), moved, packed[s])
        return packed

    def remote(src, dst, k, n, peer):
        return pltpu.make_async_remote_copy(
            src_ref=src,
            dst_ref=dst,
            send_sem=face_send.at[k, n],
            recv_sem=face_recv.at[k, n],
            device_id=peer,
            device_id_type=MESH,
        )

    def face_copies(k):
        copies = [remote(dep_out.at[k], dep_in.at[k], k, 0, at(0, 0, 1))]
        for s, da in enumerate((-1, 1)):
            copies.append(remote(az_out.at[k, s], az_in.at[k, s], k, 1 + s, at(da, 0, 0)))
        for s, dm in enumerate((-1, 1)):
            for i, da in enumerate((-1, 0, 1)):
                n = 3 + s * 3 + i
                copies.append(remote(mer_out.at[k, s], mer_in.at[k, s * 3 + i], k, n, at(da, dm, 0)))
        return copies

    def exchange(k, copies):
        assemble_azimuth_depth()
        for d in (0, 1):
            first = (5 * PLANE + 4, 0)[d]

            @pl.when(dep == d)
            def _():
                for n in range(36):
                    r = first + n * 8
                    dep_out[k, n * 4 : n * 4 + 4, :] = upd[r : r + 4, :]

        if k == 0:
            pl.semaphore_wait(barrier, greeted)
        copies[0].start()
        packed = assemble_meridian((1, 2, 3, 4), [zero, zero])
        copies[0].wait()
        for d in (0, 1):
            first = (5 * PLANE + 4, 0)[d]

            @pl.when(dep == d)
            def _():
                for n in range(36):
                    r = first + n * 8
                    upd[r : r + 4, :] = upd[r : r + 4, :] + dep_in[k, n * 4 : n * 4 + 4, :]

        packed = assemble_meridian((0, 5), packed)
        for s, there in enumerate((has_low, has_high)):
            mer_out[k, s] = packed[s]

            @pl.when(there)
            def _():
                for copy in copies[3 + 3 * s : 6 + 3 * s]:
                    copy.start()

        for s, (b, e) in enumerate(((0, 0), (5, 3))):
            for a in range(6):
                first = a * PLANE + b * 48 + e
                az_out[k, s, a * 12 : a * 12 + 8, :] = upd[pl.ds(first, 8, stride=4), :]
                az_out[k, s, a * 12 + 8 : a * 12 + 12, :] = upd[pl.ds(first + 32, 4, stride=4), :]
            copies[1 + s].start()

    def finish(copies):
        for copy in copies[1:3]:
            copy.wait()
        for s, (to, came) in enumerate(((has_low, has_high), (has_high, has_low))):

            @pl.when(to)
            def _():
                for copy in copies[3 + 3 * s : 6 + 3 * s]:
                    copy.wait_send()

            @pl.when(came)
            def _():
                for copy in copies[3 + 3 * s : 6 + 3 * s]:
                    copy.wait_recv()

    def add_halo(k, field):
        for s, (b, e) in enumerate(((5, 3), (0, 0))):
            for a in range(6):
                first = a * PLANE + b * 48 + e
                for skip, count in ((0, 8), (8, 4)):
                    r = pl.ds(first + 4 * skip, count, stride=4)
                    field[r, :] = field[r, :] + az_in[k, s, a * 12 + skip : a * 12 + skip + count, :]

        for s, (c, to_lane, there) in enumerate(((5, 127, has_high), (0, 0, has_low))):

            @pl.when(there)
            def _():
                from_high, direct, from_low = (mer_in[k, s * 3 + i] for i in range(3))
                for n in range(36):
                    moved = pltpu.roll(direct, (to_lane - n) % 128, 1)
                    r = slice(n * 48 + c * 8, n * 48 + c * 8 + 8)
                    field[r, :] = field[r, :] + jnp.where(lane == to_lane, moved, zero)
                for a in range(6):
                    moved = pltpu.roll(from_high, (to_lane - a * 6) % 128, 1)
                    moved = jnp.where(jnp.logical_and(lane == to_lane, row_az == 0), moved, zero)
                    r = a * PLANE + 5 * 48 + c * 8 + 3
                    field[r : r + 5, :] = field[r : r + 5, :] + moved[0:5]
                    moved = pltpu.roll(from_low, (to_lane - a * 6 - 5) % 128, 1)
                    moved = jnp.where(jnp.logical_and(lane == to_lane, row_az == 3), moved, zero)
                    r = a * PLANE + c * 8
                    field[r : r + 5, :] = field[r : r + 5, :] + moved[3:8]

    def strip(field):
        sums = []
        for first in (0, 5 * PLANE + 4):
            total = jnp.zeros((4, 128), F32)
            for n in range(36):
                r = slice(first + n * 8, first + n * 8 + 4)
                total = total + face_weight[n * 4 : n * 4 + 4, :] * (mass[r, :] * field[r, :])
            sums.append(total)
        return jnp.where(dep == 0, sums[0], sums[1])

    loads[0].wait()
    heat_gradients(1)
    loads[8].wait()
    late_table = felt_table(1)
    loads[1].wait()
    loads[2].wait()
    coefficients(late_table)
    loads[3].wait()
    loads[4].wait()

    def scale_late(a, _):
        here = rows(a * PLANE, PLANE)
        scaled[here, :] = mass[here, :] * adj[here, :]
        return 0

    lax.fori_loop(0, 6, scale_late, 0)
    loads[9].wait()
    strip_late = strip(adj)
    update()
    first_copies = face_copies(0)
    exchange(0, first_copies)

    def add_mid(a, _):
        here = rows(a * PLANE, PLANE)
        mid[here, :] = adj[here, :] + upd[here, :]
        return 0

    lax.fori_loop(0, 6, add_mid, 0)
    loads[5].wait()
    heat_gradients(0)
    coefficients(felt_table(0))
    finish(first_copies)
    add_halo(0, mid)

    strip_grad = STEP * (strip_late + strip(mid))
    total = jnp.broadcast_to(jnp.sum(strip_grad, axis=1, keepdims=True), (4, 128))
    group_of = lax.div(lane1, 2 * PAN_DEV)
    mine = jnp.zeros((1, 128), F32)
    for e in range(4):
        mine = jnp.where(group_of == e, total[e : e + 1, :], mine)
    tot_out[...] = jnp.broadcast_to(mine, (8, 128))

    def tot_copy(src, dst, n, peer):
        return pltpu.make_async_remote_copy(
            src_ref=src,
            dst_ref=dst,
            send_sem=tot_send.at[n],
            recv_sem=tot_recv.at[n],
            device_id=peer,
            device_id_type=MESH,
        )

    y_copies = [tot_copy(tot_out, tot_y.at[k], k, y_peer(k)) for k in range(1, MER_Y)]
    for copy in y_copies:
        copy.start()
    z_copies = [
        [tot_copy(ysum_out, tot_z.at[-da, k], MER_Y + MER_Z * -da + k, z_peer(da, -k)) for da in (0, -1)]
        for k in range(1, MER_Z)
    ]

    def pass_totals():
        for copy in y_copies:
            copy.wait()
        group = tot_out[...]
        above = zero
        for k in range(1, MER_Y):
            piece = tot_y[k]
            sender = lax.rem(mer_y - k + MER_Y, MER_Y)
            group = group + piece
            above = above + jnp.where(sender > mer_y, piece, zero)
        ysum_out[...] = group
        carry[0] = above
        pan_out[2] = above
        for k in range(1, MER_Z):

            @pl.when(mer_z >= k)
            def _():
                for copy in z_copies[k - 1]:
                    copy.start()

    def scale_early(a, _):
        here = rows(a * PLANE, PLANE)
        scaled[here, :] = mass[here, :] * mid[here, :]
        return 0

    lax.fori_loop(0, 6, scale_early, 0)
    update(pass_totals)
    second_copies = face_copies(1)
    exchange(1, second_copies)

    lane4 = lax.broadcasted_iota(jnp.int32, (4, 128), 1)
    suffix = strip_grad
    for shift in (1, 2, 4, 8, 16, 32, 64):
        suffix = suffix + jnp.where(lane4 < 128 - shift, pltpu.roll(suffix, 128 - shift, 1), 0.0)

    flat = (az * N_MER + mer) * N_DEP + dep
    before = (lax.rem(az + N_AZ - 1, N_AZ) * N_MER + mer) * N_DEP + dep
    loads[10].wait()
    owners = owner[...]
    own = owners - flat * PAN_DEV
    prev = owners - before * PAN_DEV
    slot = jnp.where(
        jnp.logical_and(own >= 0, own < PAN_DEV),
        own,
        jnp.where(jnp.logical_and(prev >= 0, prev < PAN_DEV), prev + PAN_DEV, -1),
    )
    panel = lax.broadcasted_iota(jnp.int32, (2 * PAN_DEV, 128), 0)
    hits = [jnp.broadcast_to(slot[e : e + 1, :], (2 * PAN_DEV, 128)) == panel for e in range(4)]
    counts = jnp.concatenate([jnp.where(hit, 1.0, 0.0) for hit in hits], axis=0)
    parts = jnp.concatenate(
        [jnp.where(hits[e], jnp.broadcast_to(suffix[e : e + 1, :], (2 * PAN_DEV, 128)), 0.0) for e in range(4)], axis=0
    )

    def lane_sums(values, precision):
        return lax.dot_general(
            jnp.ones((8, 128), values.dtype),
            values,
            (((1,), (1,)), ((), ())),
            precision=precision,
            preferred_element_type=F32,
        )

    counts = lane_sums(counts.astype(jnp.bfloat16), None)
    parts = lane_sums(parts, lax.Precision.HIGHEST)
    pan_out[0] = parts
    pan_out[1] = counts
    pan_copy = pltpu.make_async_remote_copy(
        src_ref=pan_out,
        dst_ref=pan_in,
        send_sem=pan_send,
        recv_sem=pan_recv,
        device_id=at(-1, 0, 0),
        device_id_type=MESH,
    )
    pan_copy.start()

    def add_out(a, _):
        here = rows(a * PLANE, PLANE)
        out[here, :] = mid[here, :] + upd[here, :]
        return 0

    lax.fori_loop(0, 6, add_out, 0)
    finish(second_copies)
    add_halo(1, out)

    pan_copy.wait()
    carry[1] = pan_in[2]
    for k in range(1, MER_Z):

        @pl.when(mer_z >= k)
        def _():
            for copy in z_copies[k - 1]:
                copy.wait_send()

        @pl.when(mer_z + k < MER_Z)
        def _():
            for s, copy in enumerate(z_copies[k - 1]):
                copy.wait_recv()
                carry[s] = carry[s] + tot_z[s, k]

    whole = parts + counts * carry[0]
    other = pan_in[0] + pan_in[1] * carry[1]
    whole = whole + pltpu.roll(other, 128 - PAN_DEV, 1)
    whole = whole + pltpu.roll(whole, 64, 1)
    whole = whole + pltpu.roll(whole, 96, 1)
    panels[...] = whole[0:1, 0:PAN_DEV]


def shards(
    adjoint_end,
    temp_early,
    temp_late,
    mass_inverse,
    thermal_transport_coefficient,
    jacobian_quadrature_scales,
    measured,
    sensor_cell_slot,
    sensor_gridsite_slot,
    face_weight,
    panel_owner,
):
    shape = adjoint_end.shape

    def flat(array):
        return array.reshape(-1, 128)

    hbm = pl.BlockSpec(memory_space=pltpu.HBM)
    vmem = pl.BlockSpec(memory_space=pltpu.VMEM)
    field = pltpu.VMEM((ROWS, 128), F32)
    small = pltpu.VMEM((8, 128), F32)
    start, panel_grad = pl.pallas_call(
        kernel,
        out_shape=(
            pltpu.VMEM((ROWS, 128), F32),
            pltpu.VMEM((1, PAN_DEV), F32),
        ),
        in_specs=[hbm] * 11,
        out_specs=(vmem, vmem),
        scratch_shapes=[
            pltpu.SMEM((2, SENSORS), F32),
            pltpu.SMEM((SENSORS,), jnp.int32),
            pltpu.SMEM((SENSORS,), jnp.int32),
            pltpu.VMEM((144, 128), F32),
            pltpu.VMEM((4, 128), jnp.int32),
            field,
            pltpu.VMEM((108, 16, 128), jnp.bfloat16),
            pltpu.VMEM((108, 16, 128), jnp.bfloat16),
            field,
            field,
            pltpu.VMEM((3 * ROWS, 128), jnp.bfloat16),
            field,
            pltpu.VMEM((3, ROWS, 128), F32),
            pltpu.VMEM((3, ROWS, 128), F32),
            field,
            pltpu.VMEM((ROWS, 128), jnp.bfloat16),
            field,
            field,
            field,
            pltpu.VMEM((2, SENSORS, 128), F32),
            pltpu.VMEM((2, 2, 72, 128), F32),
            pltpu.VMEM((2, 2, 72, 128), F32),
            pltpu.VMEM((2, 144, 128), F32),
            pltpu.VMEM((2, 144, 128), F32),
            pltpu.VMEM((2, 2, 8, 128), F32),
            pltpu.VMEM((2, 6, 8, 128), F32),
            small,
            pltpu.VMEM((MER_Y, 8, 128), F32),
            small,
            pltpu.VMEM((2, MER_Z, 8, 128), F32),
            pltpu.VMEM((3, 8, 128), F32),
            pltpu.VMEM((3, 8, 128), F32),
            pltpu.VMEM((2, 8, 128), F32),
            pltpu.SemaphoreType.DMA((11,)),
            pltpu.SemaphoreType.DMA((2, 9)),
            pltpu.SemaphoreType.DMA((2, 9)),
            pltpu.SemaphoreType.DMA((MER_Y + 2 * MER_Z,)),
            pltpu.SemaphoreType.DMA((MER_Y + 2 * MER_Z,)),
            pltpu.SemaphoreType.DMA,
            pltpu.SemaphoreType.DMA,
        ],
        compiler_params=pltpu.CompilerParams(
            collective_id=0, has_side_effects=True, vmem_limit_bytes=60 * 1024 * 1024
        ),
        name="adjoint_steps",
    )(
        flat(adjoint_end),
        temp_early.reshape(108, 16, 128),
        temp_late.reshape(108, 16, 128),
        flat(mass_inverse),
        flat(thermal_transport_coefficient),
        flat(jacobian_quadrature_scales),
        measured,
        sensor_cell_slot,
        sensor_gridsite_slot,
        flat(face_weight),
        flat(panel_owner),
    )
    return start.reshape(shape), panel_grad.reshape(PAN_DEV)


def solution(mesh):
    field = P(None, None, None, "depth", "azimuth", "meridian")
    line = P(("azimuth", "meridian", "depth"))
    placed = (
        field,
        field,
        field,
        field,
        field,
        P(None, None, None, None, "depth", "azimuth", "meridian"),
        P(None, ("azimuth", "meridian", "depth")),
        line,
        line,
        P("depth", None, None, "azimuth", "meridian"),
        P("depth", "azimuth", "meridian"),
    )
    return jax.shard_map(shards, mesh=mesh, in_specs=placed, out_specs=(field, line), check_vma=False)
```

```python
import math

import jax
import jax.numpy as jnp
import numpy as np
from jax import lax
from jax.experimental import pallas as pl
from jax.experimental.pallas import tpu as pltpu
from jax.sharding import PartitionSpec as P

N_AZ, N_MER, N_DEP = 4, 32, 2
MER_Y, MER_Z = 4, 8
ROWS = 1728
PLANE = 288
PAN_DEV = 16
SENSORS = 16
STEP = 0.1
F32 = jnp.float32
MESH = pl.DeviceIdType.MESH


def gll_derivative():
    root_seven = math.sqrt(7.0)
    inner_near = math.sqrt((7.0 - 2.0 * root_seven) / 21.0)
    inner_far = math.sqrt((7.0 + 2.0 * root_seven) / 21.0)
    points = np.array([-1.0, -inner_far, -inner_near, inner_near, inner_far, 1.0])
    legendre = (63.0 * points**5 - 70.0 * points**3 + 15.0 * points) / 8.0
    entries = np.zeros((6, 6))
    for i in range(6):
        for j in range(6):
            if i != j:
                entries[i, j] = legendre[i] / (legendre[j] * (points[i] - points[j]))
    entries[0, 0] = -7.5
    entries[5, 5] = 7.5
    return entries


DER = gll_derivative()
FLIP = DER[:, ::-1]
GRAD_EVEN = (0.5 * (DER + FLIP))[:3, :3]
GRAD_ODD = (0.5 * (DER - FLIP))[:3, :3]
TRA = DER.T
DIV_EVEN = (0.5 * (TRA + TRA[:, ::-1]))[:3, :3]
DIV_ODD = (0.5 * (TRA - TRA[:, ::-1]))[:3, :3]


def grad_line(x):
    e = [x[j] + x[5 - j] for j in range(3)]
    o = [x[j] - x[5 - j] for j in range(3)]
    e1, e2 = e[1] - e[0], e[2] - e[0]
    p = [float(GRAD_EVEN[i, 1]) * e1 + float(GRAD_EVEN[i, 2]) * e2 for i in range(3)]
    q = [
        float(GRAD_ODD[i, 0]) * o[0] + float(GRAD_ODD[i, 1]) * o[1] + float(GRAD_ODD[i, 2]) * o[2]
        for i in range(3)
    ]
    return [q[i] + p[i] for i in range(3)] + [q[i] - p[i] for i in (2, 1, 0)]


def div_line(f):
    e = [f[j] + f[5 - j] for j in range(3)]
    o = [f[j] - f[5 - j] for j in range(3)]
    p = [
        float(DIV_EVEN[i, 0]) * e[0] + float(DIV_EVEN[i, 1]) * e[1] + float(DIV_EVEN[i, 2]) * e[2]
        for i in range(3)
    ]
    q1, q2 = [
        float(DIV_ODD[i, 0]) * o[0] + float(DIV_ODD[i, 1]) * o[1] + float(DIV_ODD[i, 2]) * o[2]
        for i in (1, 2)
    ]
    q0 = -(q1 + q2)
    q = [q0, q1, q2]
    return [q[i] + p[i] for i in range(3)] + [q[i] - p[i] for i in (2, 1, 0)]


def rows(start, size, multiple=8):
    if isinstance(start, int):
        return pl.ds(start, size)
    return pl.ds(pl.multiple_of(start, multiple), size)


def line_rows(direction, outer, inner):
    if direction == 0:
        return [rows(j * PLANE + outer * 48 + inner * 16, 16, 16) for j in range(6)]
    if direction == 1:
        return [rows(outer * PLANE + j * 48 + inner * 16, 16, 16) for j in range(6)]
    return [rows(outer * PLANE + inner * 48 + j * 8, 8, 8) for j in range(6)]


def inner_count(direction):
    return 6 if direction == 2 else 3


def kernel(
    adj_hbm,
    early_hbm,
    late_hbm,
    mass_hbm,
    cond_hbm,
    metric_hbm,
    measured_hbm,
    cell_hbm,
    site_hbm,
    face_weight_hbm,
    owner_hbm,
    out,
    panels,
    measured,
    cell,
    site,
    face_weight,
    owner,
    adj,
    temp_early,
    temp_late,
    mass,
    cond,
    metric,
    heat,
    flux_c,
    cross_c,
    source,
    hot,
    scaled,
    upd,
    mid,
    spots,
    az_out,
    az_in,
    dep_out,
    dep_in,
    mer_out,
    mer_in,
    tot_out,
    tot_y,
    ysum_out,
    tot_z,
    pan_out,
    pan_in,
    carry,
    load_sem,
    face_send,
    face_recv,
    tot_send,
    tot_recv,
    pan_send,
    pan_recv,
):
    az = lax.axis_index("azimuth")
    mer = lax.axis_index("meridian")
    dep = lax.axis_index("depth")
    mer_y = lax.rem(mer, MER_Y)
    mer_z = lax.div(mer, MER_Y)

    def at(da, dm, dd):
        return {
            "azimuth": lax.rem(az + (da + N_AZ), N_AZ),
            "meridian": mer + dm,
            "depth": lax.rem(dep + dd, N_DEP),
        }

    def y_peer(k):
        return {"azimuth": az, "meridian": mer_z * MER_Y + lax.rem(mer_y + k, MER_Y), "depth": dep}

    def z_peer(da, k):
        return {"azimuth": lax.rem(az + (da + N_AZ), N_AZ), "meridian": mer + k * MER_Y, "depth": dep}

    has_low, has_high = mer > 0, mer < N_MER - 1

    loads = [
        (late_hbm, temp_late),
        (metric_hbm, metric),
        (cond_hbm, cond),
        (mass_hbm, mass),
        (adj_hbm, adj),
        (early_hbm, temp_early),
        (site_hbm, site),
        (cell_hbm, cell),
        (measured_hbm, measured),
        (face_weight_hbm, face_weight),
        (owner_hbm, owner),
    ]
    loads = [pltpu.make_async_copy(s, d, load_sem.at[i]) for i, (s, d) in enumerate(loads)]
    for n in (6, 7, 0, 8, 1, 2, 3, 4, 9, 5, 10):
        loads[n].start()

    barrier = pltpu.get_barrier_semaphore()
    def greet(peer):
        pl.semaphore_signal(barrier, inc=1, device_id=peer, device_id_type=MESH)

    greet(at(0, 0, 1))
    greet(at(-1, 0, 0))
    greet(at(1, 0, 0))
    for there, dm in ((has_low, -1), (has_high, 1)):

        @pl.when(there)
        def _():
            for da in (-1, 0, 1):
                greet(at(da, dm, 0))

    for k in range(1, MER_Y):
        greet(y_peer(k))
    for k in range(1, MER_Z):

        @pl.when(mer_z + k < MER_Z)
        def _():
            for da in (0, 1):
                greet(z_peer(da, k))

    greeted = 3 + 3 + 3 * (has_low.astype(jnp.int32) + has_high.astype(jnp.int32)) + 2 * mer_z

    row8 = lax.broadcasted_iota(jnp.int32, (8, 128), 0)
    lane = lax.broadcasted_iota(jnp.int32, (8, 128), 1)
    row_az = lax.rem(row8, 4)
    row_dep = lax.div(row8, 4)
    zero = jnp.zeros((8, 128), F32)

    lane1 = lax.broadcasted_iota(jnp.int32, (1, 128), 1)
    row16 = lax.broadcasted_iota(jnp.int32, (16, 128), 0)
    lane16 = lax.broadcasted_iota(jnp.int32, (16, 128), 1)
    for n in (6, 7):
        loads[n].wait()
    code = jnp.full((1, 128), -1, jnp.int32)
    for q in range(SENSORS):
        word = site[q] * 8 + lax.shift_right_logical(cell[q], 7)
        code = jnp.where(jnp.logical_and(lax.rem(lane1, SENSORS) == q, lane1 < 3 * SENSORS), word, code)

    def place(a, _):
        base = lax.broadcasted_iota(jnp.int32, (PLANE, 128), 0) + a * PLANE
        hot[rows(a * PLANE, PLANE, 16), :] = jnp.where(base == code, 1.0, 0.0).astype(jnp.bfloat16)
        return 0

    lax.fori_loop(0, 6, place, 0)

    temps = (temp_early, temp_late)

    def felt_table(k):
        for q in range(SENSORS):
            tile_row = jnp.bitwise_and(site[q], 1) * 8 + lax.shift_right_logical(cell[q], 7)
            there = jnp.logical_and(row16 == tile_row, lane16 == jnp.bitwise_and(cell[q], 127))
            felt = temps[k][lax.shift_right_logical(site[q], 1)].astype(F32)
            value = jnp.where(there, felt - measured[k, q], 0.0)
            spots[k, q : q + 1, :] = jnp.sum(value, axis=0, keepdims=True)
        value = spots[k]
        high = value.astype(jnp.bfloat16).astype(F32)
        rest = value - high
        middle = rest.astype(jnp.bfloat16).astype(F32)
        low = rest - middle
        return jnp.concatenate([high, middle, low, jnp.zeros((80, 128), F32)], axis=0).astype(jnp.bfloat16)

    def heat_gradients(k):
        def plane(a, _):
            h = temps[k][pl.ds(a * 18, 18)].astype(F32).reshape(PLANE, 128)
            heat[rows(a * PLANE, PLANE), :] = h
            return 0

        lax.fori_loop(0, 6, plane, 0)

        def direction(d):
            def body(outer, _):
                for inner in range(inner_count(d)):
                    at_rows = line_rows(d, outer, inner)
                    for r, g in zip(at_rows, grad_line([heat[r, :] for r in at_rows])):
                        cross_c[d, r, :] = g
                return 0

            lax.fori_loop(0, 6, body, 0)

        for d in range(3):
            direction(d)

    def coefficients(table):
        def plane(a, _):
            for part in range(6):
                first = a * PLANE + part * 48
                r = rows(first, 48, 16)
                h = heat[r, :]
                c = (-STEP) * cond[r, :]
                kap = c * (1.0 + 0.5 * h * h)
                slope = c * h
                for d in range(3):
                    w = metric[rows(d * ROWS + first, 48, 16), :].astype(F32)
                    flux_c[d, r, :] = kap * w
                    cross_c[d, r, :] = slope * w * cross_c[d, r, :]
            here = rows(a * PLANE, PLANE, 16)
            source[here, :] = jnp.dot(hot[here, :], table, preferred_element_type=F32)
            return 0

        lax.fori_loop(0, 6, plane, 0)

    def update(field, k, depth_copy):
        def add_lines(d, outer):
            for inner in range(inner_count(d)):
                at_rows = line_rows(d, outer, inner)
                if d == 0:
                    values = [mass[r, :] * field[r, :] for r in at_rows]
                    for r, value in zip(at_rows, values):
                        scaled[r, :] = value
                else:
                    values = [scaled[r, :] for r in at_rows]
                g = grad_line(values)
                flux = [flux_c[d, r, :] * g[j] for j, r in enumerate(at_rows)]
                spread = div_line(flux)
                for j, r in enumerate(at_rows):
                    total = spread[j] + cross_c[d, r, :] * g[j]
                    upd[r, :] = (source if d == 0 else upd)[r, :] + total

        def depth_lines(b, _):
            add_lines(0, b)
            return 0

        def plane(i, _):
            a = jnp.where(i == 0, 5 * (1 - dep), i - 1 + dep)
            add_lines(1, a)
            add_lines(2, a)
            return 0

        lax.fori_loop(0, 6, depth_lines, 0)
        lax.fori_loop(0, 1, plane, 0)
        for d in (0, 1):
            first = (5 * PLANE + 4, 0)[d]

            @pl.when(dep == d)
            def _():
                for n in range(36):
                    r = first + n * 8
                    dep_out[k, n * 4 : n * 4 + 4, :] = upd[r : r + 4, :]

        if k == 0:
            pl.semaphore_wait(barrier, greeted)
        depth_copy.start()
        lax.fori_loop(1, 6, plane, 0)

    row7_az = row_az[0:7]

    def assemble_azimuth_depth():
        for a in range(6):
            for c in range(6):
                lo, hi = (a * PLANE + b * 48 + c * 8 for b in (0, 5))
                low, high = upd[lo + 1 : lo + 8, :], upd[hi : hi + 7, :]
                both = low + high
                upd[hi : hi + 7, :] = jnp.where(row7_az < 3, both, high)
                upd[lo + 1 : lo + 8, :] = jnp.where(row7_az < 3, both, low)
        for n in range(36):
            lo, hi = n * 8 + 4, 5 * PLANE + n * 8
            both = upd[lo : lo + 4, :] + upd[hi : hi + 4, :]
            upd[lo : lo + 4, :] = both
            upd[hi : hi + 4, :] = both

    def assemble_meridian(planes, packed):
        for a in planes:
            for b in range(0, 6, 2):
                ends = []
                for n in (a * 6 + b, a * 6 + b + 1):
                    lo, hi = slice(n * 48, n * 48 + 8), slice(n * 48 + 40, n * 48 + 48)
                    low, high = upd[lo, :], upd[hi, :]
                    low_moved, high_moved = pltpu.roll(low, 127, 1), pltpu.roll(high, 1, 1)
                    upd[hi, :] = high + jnp.where(lane < 127, low_moved, zero)
                    upd[lo, :] = low + jnp.where(lane > 0, high_moved, zero)
                    ends.append((low, low_moved, high, high_moved))
                n = a * 6 + b
                pairs = (
                    jnp.where(lane == 127, ends[0][1], ends[1][0]),
                    jnp.where(lane == 127, ends[0][2], ends[1][3]),
                )
                for s in (0, 1):
                    moved = pltpu.roll(pairs[s], n + 1, 1)
                    packed[s] = jnp.where(jnp.logical_or(lane == n, lane == n + 1), moved, packed[s])
        return packed

    def remote(src, dst, k, n, peer):
        return pltpu.make_async_remote_copy(
            src_ref=src,
            dst_ref=dst,
            send_sem=face_send.at[k, n],
            recv_sem=face_recv.at[k, n],
            device_id=peer,
            device_id_type=MESH,
        )

    def face_copies(k):
        copies = [remote(dep_out.at[k], dep_in.at[k], k, 0, at(0, 0, 1))]
        for s, da in enumerate((-1, 1)):
            copies.append(remote(az_out.at[k, s], az_in.at[k, s], k, 1 + s, at(da, 0, 0)))
        for s, dm in enumerate((-1, 1)):
            for i, da in enumerate((-1, 0, 1)):
                n = 3 + s * 3 + i
                copies.append(remote(mer_out.at[k, s], mer_in.at[k, s * 3 + i], k, n, at(da, dm, 0)))
        return copies

    def exchange(k, copies):
        copies[0].wait()
        for d in (0, 1):
            first = (5 * PLANE + 4, 0)[d]

            @pl.when(dep == d)
            def _():
                for n in range(36):
                    r = first + n * 8
                    upd[r : r + 4, :] = upd[r : r + 4, :] + dep_in[k, n * 4 : n * 4 + 4, :]

        assemble_azimuth_depth()
        packed = assemble_meridian(range(6), [zero, zero])
        for s, there in enumerate((has_low, has_high)):
            mer_out[k, s] = packed[s]

            @pl.when(there)
            def _():
                for copy in copies[3 + 3 * s : 6 + 3 * s]:
                    copy.start()

        for s, (b, e) in enumerate(((0, 0), (5, 3))):
            for a in range(6):
                first = a * PLANE + b * 48 + e
                az_out[k, s, a * 12 : a * 12 + 8, :] = upd[pl.ds(first, 8, stride=4), :]
                az_out[k, s, a * 12 + 8 : a * 12 + 12, :] = upd[pl.ds(first + 32, 4, stride=4), :]
            copies[1 + s].start()

    def finish(copies):
        for copy in copies[1:3]:
            copy.wait()
        for s, (to, came) in enumerate(((has_low, has_high), (has_high, has_low))):

            @pl.when(to)
            def _():
                for copy in copies[3 + 3 * s : 6 + 3 * s]:
                    copy.wait_send()

            @pl.when(came)
            def _():
                for copy in copies[3 + 3 * s : 6 + 3 * s]:
                    copy.wait_recv()

    def add_halo(k, field):
        for s, (b, e) in enumerate(((5, 3), (0, 0))):
            for a in range(6):
                first = a * PLANE + b * 48 + e
                for skip, count in ((0, 8), (8, 4)):
                    r = pl.ds(first + 4 * skip, count, stride=4)
                    field[r, :] = field[r, :] + az_in[k, s, a * 12 + skip : a * 12 + skip + count, :]

        for s, (c, to_lane, there) in enumerate(((5, 127, has_high), (0, 0, has_low))):

            @pl.when(there)
            def _():
                from_high, direct, from_low = (mer_in[k, s * 3 + i] for i in range(3))
                for n in range(36):
                    moved = pltpu.roll(direct, (to_lane - n) % 128, 1)
                    r = slice(n * 48 + c * 8, n * 48 + c * 8 + 8)
                    field[r, :] = field[r, :] + jnp.where(lane == to_lane, moved, zero)
                for a in range(6):
                    moved = pltpu.roll(from_high, (to_lane - a * 6) % 128, 1)
                    moved = jnp.where(jnp.logical_and(lane == to_lane, row_az == 0), moved, zero)
                    r = a * PLANE + 5 * 48 + c * 8 + 3
                    field[r : r + 5, :] = field[r : r + 5, :] + moved[0:5]
                    moved = pltpu.roll(from_low, (to_lane - a * 6 - 5) % 128, 1)
                    moved = jnp.where(jnp.logical_and(lane == to_lane, row_az == 3), moved, zero)
                    r = a * PLANE + c * 8
                    field[r : r + 5, :] = field[r : r + 5, :] + moved[3:8]

    def strip(field):
        sums = []
        for first in (0, 5 * PLANE + 4):
            total = jnp.zeros((4, 128), F32)
            for n in range(36):
                r = slice(first + n * 8, first + n * 8 + 4)
                total = total + face_weight[n * 4 : n * 4 + 4, :] * (mass[r, :] * field[r, :])
            sums.append(total)
        return jnp.where(dep == 0, sums[0], sums[1])

    loads[0].wait()
    heat_gradients(1)
    loads[8].wait()
    late_table = felt_table(1)
    loads[1].wait()
    loads[2].wait()
    coefficients(late_table)
    loads[3].wait()
    loads[4].wait()

    loads[9].wait()
    strip_late = strip(adj)
    first_copies = face_copies(0)
    update(adj, 0, first_copies[0])
    exchange(0, first_copies)

    def add_mid(a, _):
        here = rows(a * PLANE, PLANE)
        mid[here, :] = adj[here, :] + upd[here, :]
        return 0

    lax.fori_loop(0, 6, add_mid, 0)
    loads[5].wait()
    heat_gradients(0)
    coefficients(felt_table(0))
    finish(first_copies)
    add_halo(0, mid)

    strip_grad = STEP * (strip_late + strip(mid))
    total = jnp.broadcast_to(jnp.sum(strip_grad, axis=1, keepdims=True), (4, 128))
    group_of = lax.div(lane1, 2 * PAN_DEV)
    mine = jnp.zeros((1, 128), F32)
    for e in range(4):
        mine = jnp.where(group_of == e, total[e : e + 1, :], mine)
    tot_out[...] = jnp.broadcast_to(mine, (8, 128))

    def tot_copy(src, dst, n, peer):
        return pltpu.make_async_remote_copy(
            src_ref=src,
            dst_ref=dst,
            send_sem=tot_send.at[n],
            recv_sem=tot_recv.at[n],
            device_id=peer,
            device_id_type=MESH,
        )

    y_copies = [tot_copy(tot_out, tot_y.at[k], k, y_peer(k)) for k in range(1, MER_Y)]
    for copy in y_copies:
        copy.start()
    z_copies = [
        [tot_copy(ysum_out, tot_z.at[-da, k], MER_Y + MER_Z * -da + k, z_peer(da, -k)) for da in (0, -1)]
        for k in range(1, MER_Z)
    ]

    def pass_totals():
        for copy in y_copies:
            copy.wait()
        group = tot_out[...]
        above = zero
        for k in range(1, MER_Y):
            piece = tot_y[k]
            sender = lax.rem(mer_y - k + MER_Y, MER_Y)
            group = group + piece
            above = above + jnp.where(sender > mer_y, piece, zero)
        ysum_out[...] = group
        carry[0] = above
        pan_out[2] = above
        for k in range(1, MER_Z):

            @pl.when(mer_z >= k)
            def _():
                for copy in z_copies[k - 1]:
                    copy.start()

    second_copies = face_copies(1)
    update(mid, 1, second_copies[0])
    exchange(1, second_copies)
    pass_totals()

    lane4 = lax.broadcasted_iota(jnp.int32, (4, 128), 1)
    suffix = strip_grad
    for shift in (1, 2, 4, 8, 16, 32, 64):
        suffix = suffix + jnp.where(lane4 < 128 - shift, pltpu.roll(suffix, 128 - shift, 1), 0.0)

    flat = (az * N_MER + mer) * N_DEP + dep
    before = (lax.rem(az + N_AZ - 1, N_AZ) * N_MER + mer) * N_DEP + dep
    loads[10].wait()
    owners = owner[...]
    own = owners - flat * PAN_DEV
    prev = owners - before * PAN_DEV
    slot = jnp.where(
        jnp.logical_and(own >= 0, own < PAN_DEV),
        own,
        jnp.where(jnp.logical_and(prev >= 0, prev < PAN_DEV), prev + PAN_DEV, -1),
    )
    panel = lax.broadcasted_iota(jnp.int32, (2 * PAN_DEV, 128), 0)
    hits = [jnp.broadcast_to(slot[e : e + 1, :], (2 * PAN_DEV, 128)) == panel for e in range(4)]
    counts = jnp.concatenate([jnp.where(hit, 1.0, 0.0) for hit in hits], axis=0)
    parts = jnp.concatenate(
        [jnp.where(hits[e], jnp.broadcast_to(suffix[e : e + 1, :], (2 * PAN_DEV, 128)), 0.0) for e in range(4)], axis=0
    )

    def lane_sums(values, precision):
        return lax.dot_general(
            jnp.ones((8, 128), values.dtype),
            values,
            (((1,), (1,)), ((), ())),
            precision=precision,
            preferred_element_type=F32,
        )

    counts = lane_sums(counts.astype(jnp.bfloat16), None)
    parts = lane_sums(parts, lax.Precision.HIGHEST)
    pan_out[0] = parts
    pan_out[1] = counts
    pan_copy = pltpu.make_async_remote_copy(
        src_ref=pan_out,
        dst_ref=pan_in,
        send_sem=pan_send,
        recv_sem=pan_recv,
        device_id=at(-1, 0, 0),
        device_id_type=MESH,
    )
    pan_copy.start()

    def add_out(a, _):
        here = rows(a * PLANE, PLANE)
        out[here, :] = mid[here, :] + upd[here, :]
        return 0

    lax.fori_loop(0, 6, add_out, 0)
    finish(second_copies)
    add_halo(1, out)

    pan_copy.wait()
    carry[1] = pan_in[2]
    for k in range(1, MER_Z):

        @pl.when(mer_z >= k)
        def _():
            for copy in z_copies[k - 1]:
                copy.wait_send()

        @pl.when(mer_z + k < MER_Z)
        def _():
            for s, copy in enumerate(z_copies[k - 1]):
                copy.wait_recv()
                carry[s] = carry[s] + tot_z[s, k]

    whole = parts + counts * carry[0]
    other = pan_in[0] + pan_in[1] * carry[1]
    whole = whole + pltpu.roll(other, 128 - PAN_DEV, 1)
    whole = whole + pltpu.roll(whole, 64, 1)
    whole = whole + pltpu.roll(whole, 96, 1)
    panels[...] = whole[0:1, 0:PAN_DEV]


def shards(
    adjoint_end,
    temp_early,
    temp_late,
    mass_inverse,
    thermal_transport_coefficient,
    jacobian_quadrature_scales,
    measured,
    sensor_cell_slot,
    sensor_gridsite_slot,
    face_weight,
    panel_owner,
):
    shape = adjoint_end.shape

    def flat(array):
        return array.reshape(-1, 128)

    hbm = pl.BlockSpec(memory_space=pltpu.HBM)
    vmem = pl.BlockSpec(memory_space=pltpu.VMEM)
    field = pltpu.VMEM((ROWS, 128), F32)
    small = pltpu.VMEM((8, 128), F32)
    start, panel_grad = pl.pallas_call(
        kernel,
        out_shape=(
            pltpu.VMEM((ROWS, 128), F32),
            pltpu.VMEM((1, PAN_DEV), F32),
        ),
        in_specs=[hbm] * 11,
        out_specs=(vmem, vmem),
        scratch_shapes=[
            pltpu.SMEM((2, SENSORS), F32),
            pltpu.SMEM((SENSORS,), jnp.int32),
            pltpu.SMEM((SENSORS,), jnp.int32),
            pltpu.VMEM((144, 128), F32),
            pltpu.VMEM((4, 128), jnp.int32),
            field,
            pltpu.VMEM((108, 16, 128), jnp.bfloat16),
            pltpu.VMEM((108, 16, 128), jnp.bfloat16),
            field,
            field,
            pltpu.VMEM((3 * ROWS, 128), jnp.bfloat16),
            field,
            pltpu.VMEM((3, ROWS, 128), F32),
            pltpu.VMEM((3, ROWS, 128), F32),
            field,
            pltpu.VMEM((ROWS, 128), jnp.bfloat16),
            field,
            field,
            field,
            pltpu.VMEM((2, SENSORS, 128), F32),
            pltpu.VMEM((2, 2, 72, 128), F32),
            pltpu.VMEM((2, 2, 72, 128), F32),
            pltpu.VMEM((2, 144, 128), F32),
            pltpu.VMEM((2, 144, 128), F32),
            pltpu.VMEM((2, 2, 8, 128), F32),
            pltpu.VMEM((2, 6, 8, 128), F32),
            small,
            pltpu.VMEM((MER_Y, 8, 128), F32),
            small,
            pltpu.VMEM((2, MER_Z, 8, 128), F32),
            pltpu.VMEM((3, 8, 128), F32),
            pltpu.VMEM((3, 8, 128), F32),
            pltpu.VMEM((2, 8, 128), F32),
            pltpu.SemaphoreType.DMA((11,)),
            pltpu.SemaphoreType.DMA((2, 9)),
            pltpu.SemaphoreType.DMA((2, 9)),
            pltpu.SemaphoreType.DMA((MER_Y + 2 * MER_Z,)),
            pltpu.SemaphoreType.DMA((MER_Y + 2 * MER_Z,)),
            pltpu.SemaphoreType.DMA,
            pltpu.SemaphoreType.DMA,
        ],
        compiler_params=pltpu.CompilerParams(
            collective_id=0, has_side_effects=True, vmem_limit_bytes=60 * 1024 * 1024
        ),
        name="adjoint_steps",
    )(
        flat(adjoint_end),
        temp_early.reshape(108, 16, 128),
        temp_late.reshape(108, 16, 128),
        flat(mass_inverse),
        flat(thermal_transport_coefficient),
        flat(jacobian_quadrature_scales),
        measured,
        sensor_cell_slot,
        sensor_gridsite_slot,
        flat(face_weight),
        flat(panel_owner),
    )
    return start.reshape(shape), panel_grad.reshape(PAN_DEV)


def solution(mesh):
    field = P(None, None, None, "depth", "azimuth", "meridian")
    line = P(("azimuth", "meridian", "depth"))
    placed = (
        field,
        field,
        field,
        field,
        field,
        P(None, None, None, None, "depth", "azimuth", "meridian"),
        P(None, ("azimuth", "meridian", "depth")),
        line,
        line,
        P("depth", None, None, "azimuth", "meridian"),
        P("depth", "azimuth", "meridian"),
    )
    return jax.shard_map(shards, mesh=mesh, in_specs=placed, out_specs=(field, line), check_vma=False)
```

```python
import math

import jax
import jax.numpy as jnp
import numpy as np
from jax import lax
from jax.experimental import pallas as pl
from jax.experimental.pallas import tpu as pltpu
from jax.sharding import PartitionSpec as P

N_AZ, N_MER, N_DEP = 4, 32, 2
ROWS = 1728
PLANE = 288
PAN_DEV = 16
SENSORS = 16
STEP = 0.1
F32 = jnp.float32
MESH = pl.DeviceIdType.MESH


def gll_derivative():
    root_seven = math.sqrt(7.0)
    inner_near = math.sqrt((7.0 - 2.0 * root_seven) / 21.0)
    inner_far = math.sqrt((7.0 + 2.0 * root_seven) / 21.0)
    points = np.array([-1.0, -inner_far, -inner_near, inner_near, inner_far, 1.0])
    legendre = (63.0 * points**5 - 70.0 * points**3 + 15.0 * points) / 8.0
    entries = np.zeros((6, 6))
    for i in range(6):
        for j in range(6):
            if i != j:
                entries[i, j] = legendre[i] / (legendre[j] * (points[i] - points[j]))
    entries[0, 0] = -7.5
    entries[5, 5] = 7.5
    return entries


DER = gll_derivative()
FLIP = DER[:, ::-1]
GRAD_EVEN = (0.5 * (DER + FLIP))[:3, :3]
GRAD_ODD = (0.5 * (DER - FLIP))[:3, :3]
TRA = DER.T
DIV_EVEN = (0.5 * (TRA + TRA[:, ::-1]))[:3, :3]
DIV_ODD = (0.5 * (TRA - TRA[:, ::-1]))[:3, :3]


def grad_line(x):
    e = [x[j] + x[5 - j] for j in range(3)]
    o = [x[j] - x[5 - j] for j in range(3)]
    e1, e2 = e[1] - e[0], e[2] - e[0]
    p = [float(GRAD_EVEN[i, 1]) * e1 + float(GRAD_EVEN[i, 2]) * e2 for i in range(3)]
    q = [
        float(GRAD_ODD[i, 0]) * o[0] + float(GRAD_ODD[i, 1]) * o[1] + float(GRAD_ODD[i, 2]) * o[2]
        for i in range(3)
    ]
    return [q[i] + p[i] for i in range(3)] + [q[i] - p[i] for i in (2, 1, 0)]


def div_line(f):
    e = [f[j] + f[5 - j] for j in range(3)]
    o = [f[j] - f[5 - j] for j in range(3)]
    p = [
        float(DIV_EVEN[i, 0]) * e[0] + float(DIV_EVEN[i, 1]) * e[1] + float(DIV_EVEN[i, 2]) * e[2]
        for i in range(3)
    ]
    q1, q2 = [
        float(DIV_ODD[i, 0]) * o[0] + float(DIV_ODD[i, 1]) * o[1] + float(DIV_ODD[i, 2]) * o[2]
        for i in (1, 2)
    ]
    q0 = -(q1 + q2)
    q = [q0, q1, q2]
    return [q[i] + p[i] for i in range(3)] + [q[i] - p[i] for i in (2, 1, 0)]


def rows(start, size, multiple=8):
    if isinstance(start, int):
        return pl.ds(start, size)
    return pl.ds(pl.multiple_of(start, multiple), size)


def line_rows(direction, outer, inner):
    if direction == 0:
        return [rows(j * PLANE + outer * 48 + inner * 16, 16, 16) for j in range(6)]
    if direction == 1:
        return [rows(outer * PLANE + j * 48 + inner * 16, 16, 16) for j in range(6)]
    return [rows(outer * PLANE + inner * 48 + j * 8, 8, 8) for j in range(6)]


def inner_count(direction):
    return 6 if direction == 2 else 3


def kernel(
    adj_hbm,
    early_hbm,
    late_hbm,
    mass_hbm,
    cond_hbm,
    metric_hbm,
    measured_hbm,
    cell_hbm,
    site_hbm,
    face_weight_hbm,
    owner_hbm,
    out,
    panels,
    measured,
    cell,
    site,
    face_weight,
    owner,
    adj,
    temp_early,
    temp_late,
    mass,
    cond,
    metric,
    heat,
    flux_c,
    cross_c,
    source,
    hot,
    scaled,
    upd,
    mid,
    spots,
    az_out,
    az_in,
    dep_out,
    dep_in,
    mer_out,
    mer_in,
    tot_out,
    tot_in,
    pan_out,
    pan_in,
    load_sem,
    face_send,
    face_recv,
    tot_send,
    tot_recv,
    pan_send,
    pan_recv,
):
    az = lax.axis_index("azimuth")
    mer = lax.axis_index("meridian")
    dep = lax.axis_index("depth")

    def at(da, dm, dd):
        return {
            "azimuth": lax.rem(az + (da + N_AZ), N_AZ),
            "meridian": mer + dm,
            "depth": lax.rem(dep + dd, N_DEP),
        }

    def column(da, position):
        return {"azimuth": lax.rem(az + (da + N_AZ), N_AZ), "meridian": position, "depth": dep}

    has_low, has_high = mer > 0, mer < N_MER - 1

    loads = [
        (late_hbm, temp_late),
        (metric_hbm, metric),
        (cond_hbm, cond),
        (mass_hbm, mass),
        (adj_hbm, adj),
        (early_hbm, temp_early),
        (site_hbm, site),
        (cell_hbm, cell),
        (measured_hbm, measured),
        (face_weight_hbm, face_weight),
        (owner_hbm, owner),
    ]
    loads = [pltpu.make_async_copy(s, d, load_sem.at[i]) for i, (s, d) in enumerate(loads)]
    for n in (6, 7, 0, 8, 1, 2, 3, 4, 9, 5, 10):
        loads[n].start()

    barrier = pltpu.get_barrier_semaphore()
    def greet(peer):
        pl.semaphore_signal(barrier, inc=1, device_id=peer, device_id_type=MESH)

    greet(at(0, 0, 1))
    greet(at(-1, 0, 0))
    greet(at(1, 0, 0))
    for there, dm in ((has_low, -1), (has_high, 1)):

        @pl.when(there)
        def _():
            for da in (-1, 0, 1):
                greet(at(da, dm, 0))

    def greet_higher(position, _):
        for da in (0, 1):
            greet(column(da, position))
        return 0

    lax.fori_loop(mer + 1, N_MER, greet_higher, 0)
    greeted = 3 + 3 * (has_low.astype(jnp.int32) + has_high.astype(jnp.int32)) + 2 * mer

    row8 = lax.broadcasted_iota(jnp.int32, (8, 128), 0)
    lane = lax.broadcasted_iota(jnp.int32, (8, 128), 1)
    row_az = lax.rem(row8, 4)
    row_dep = lax.div(row8, 4)
    zero = jnp.zeros((8, 128), F32)

    lane1 = lax.broadcasted_iota(jnp.int32, (1, 128), 1)
    row16 = lax.broadcasted_iota(jnp.int32, (16, 128), 0)
    lane16 = lax.broadcasted_iota(jnp.int32, (16, 128), 1)
    for n in (6, 7):
        loads[n].wait()
    code = jnp.full((1, 128), -1, jnp.int32)
    for q in range(SENSORS):
        word = site[q] * 8 + lax.shift_right_logical(cell[q], 7)
        code = jnp.where(jnp.logical_and(lax.rem(lane1, SENSORS) == q, lane1 < 3 * SENSORS), word, code)

    def place(a, _):
        base = lax.broadcasted_iota(jnp.int32, (PLANE, 128), 0) + a * PLANE
        hot[rows(a * PLANE, PLANE, 16), :] = jnp.where(base == code, 1.0, 0.0).astype(jnp.bfloat16)
        return 0

    lax.fori_loop(0, 6, place, 0)

    temps = (temp_early, temp_late)

    def felt_table(k):
        for q in range(SENSORS):
            tile_row = jnp.bitwise_and(site[q], 1) * 8 + lax.shift_right_logical(cell[q], 7)
            there = jnp.logical_and(row16 == tile_row, lane16 == jnp.bitwise_and(cell[q], 127))
            felt = temps[k][lax.shift_right_logical(site[q], 1)].astype(F32)
            value = jnp.where(there, felt - measured[k, q], 0.0)
            spots[k, q : q + 1, :] = jnp.sum(value, axis=0, keepdims=True)
        value = spots[k]
        high = value.astype(jnp.bfloat16).astype(F32)
        rest = value - high
        middle = rest.astype(jnp.bfloat16).astype(F32)
        low = rest - middle
        return jnp.concatenate([high, middle, low, jnp.zeros((80, 128), F32)], axis=0).astype(jnp.bfloat16)

    def heat_gradients(k):
        def plane(a, _):
            h = temps[k][pl.ds(a * 18, 18)].astype(F32).reshape(PLANE, 128)
            heat[rows(a * PLANE, PLANE), :] = h
            return 0

        lax.fori_loop(0, 6, plane, 0)

        def direction(d):
            def body(outer, _):
                for inner in range(inner_count(d)):
                    at_rows = line_rows(d, outer, inner)
                    for r, g in zip(at_rows, grad_line([heat[r, :] for r in at_rows])):
                        cross_c[d, r, :] = g
                return 0

            lax.fori_loop(0, 6, body, 0)

        for d in range(3):
            direction(d)

    def coefficients(table):
        def plane(a, _):
            for part in range(6):
                first = a * PLANE + part * 48
                r = rows(first, 48, 16)
                h = heat[r, :]
                c = (-STEP) * cond[r, :]
                kap = c * (1.0 + 0.5 * h * h)
                slope = c * h
                for d in range(3):
                    w = metric[rows(d * ROWS + first, 48, 16), :].astype(F32)
                    flux_c[d, r, :] = kap * w
                    cross_c[d, r, :] = slope * w * cross_c[d, r, :]
            here = rows(a * PLANE, PLANE, 16)
            source[here, :] = jnp.dot(hot[here, :], table, preferred_element_type=F32)
            return 0

        lax.fori_loop(0, 6, plane, 0)

    def update(field, k, depth_copy):
        def add_lines(d, outer):
            for inner in range(inner_count(d)):
                at_rows = line_rows(d, outer, inner)
                if d == 0:
                    values = [mass[r, :] * field[r, :] for r in at_rows]
                    for r, value in zip(at_rows, values):
                        scaled[r, :] = value
                else:
                    values = [scaled[r, :] for r in at_rows]
                g = grad_line(values)
                flux = [flux_c[d, r, :] * g[j] for j, r in enumerate(at_rows)]
                spread = div_line(flux)
                for j, r in enumerate(at_rows):
                    total = spread[j] + cross_c[d, r, :] * g[j]
                    upd[r, :] = (source if d == 0 else upd)[r, :] + total

        def depth_lines(b, _):
            add_lines(0, b)
            return 0

        def plane(i, _):
            a = jnp.where(i == 0, 5 * (1 - dep), i - 1 + dep)
            add_lines(1, a)
            add_lines(2, a)
            return 0

        lax.fori_loop(0, 6, depth_lines, 0)
        lax.fori_loop(0, 1, plane, 0)
        for d in (0, 1):
            first = (5 * PLANE + 4, 0)[d]

            @pl.when(dep == d)
            def _():
                for n in range(36):
                    r = first + n * 8
                    dep_out[k, n * 4 : n * 4 + 4, :] = upd[r : r + 4, :]

        if k == 0:
            pl.semaphore_wait(barrier, greeted)
        depth_copy.start()
        lax.fori_loop(1, 6, plane, 0)

    row7_az = row_az[0:7]

    def assemble_azimuth_depth():
        for a in range(6):
            for c in range(6):
                lo, hi = (a * PLANE + b * 48 + c * 8 for b in (0, 5))
                low, high = upd[lo + 1 : lo + 8, :], upd[hi : hi + 7, :]
                both = low + high
                upd[hi : hi + 7, :] = jnp.where(row7_az < 3, both, high)
                upd[lo + 1 : lo + 8, :] = jnp.where(row7_az < 3, both, low)
        for n in range(36):
            lo, hi = n * 8 + 4, 5 * PLANE + n * 8
            both = upd[lo : lo + 4, :] + upd[hi : hi + 4, :]
            upd[lo : lo + 4, :] = both
            upd[hi : hi + 4, :] = both

    def assemble_meridian(planes, packed):
        for a in planes:
            for b in range(0, 6, 2):
                ends = []
                for n in (a * 6 + b, a * 6 + b + 1):
                    lo, hi = slice(n * 48, n * 48 + 8), slice(n * 48 + 40, n * 48 + 48)
                    low, high = upd[lo, :], upd[hi, :]
                    low_moved, high_moved = pltpu.roll(low, 127, 1), pltpu.roll(high, 1, 1)
                    upd[hi, :] = high + jnp.where(lane < 127, low_moved, zero)
                    upd[lo, :] = low + jnp.where(lane > 0, high_moved, zero)
                    ends.append((low, low_moved, high, high_moved))
                n = a * 6 + b
                pairs = (
                    jnp.where(lane == 127, ends[0][1], ends[1][0]),
                    jnp.where(lane == 127, ends[0][2], ends[1][3]),
                )
                for s in (0, 1):
                    moved = pltpu.roll(pairs[s], n + 1, 1)
                    packed[s] = jnp.where(jnp.logical_or(lane == n, lane == n + 1), moved, packed[s])
        return packed

    def remote(src, dst, k, n, peer):
        return pltpu.make_async_remote_copy(
            src_ref=src,
            dst_ref=dst,
            send_sem=face_send.at[k, n],
            recv_sem=face_recv.at[k, n],
            device_id=peer,
            device_id_type=MESH,
        )

    def face_copies(k):
        copies = [remote(dep_out.at[k], dep_in.at[k], k, 0, at(0, 0, 1))]
        for s, da in enumerate((-1, 1)):
            copies.append(remote(az_out.at[k, s], az_in.at[k, s], k, 1 + s, at(da, 0, 0)))
        for s, dm in enumerate((-1, 1)):
            for i, da in enumerate((-1, 0, 1)):
                n = 3 + s * 3 + i
                copies.append(remote(mer_out.at[k, s], mer_in.at[k, s * 3 + i], k, n, at(da, dm, 0)))
        return copies

    def exchange(k, copies):
        copies[0].wait_recv()
        for d in (0, 1):
            first = (5 * PLANE + 4, 0)[d]

            @pl.when(dep == d)
            def _():
                for n in range(36):
                    r = first + n * 8
                    upd[r : r + 4, :] = upd[r : r + 4, :] + dep_in[k, n * 4 : n * 4 + 4, :]

        assemble_azimuth_depth()
        packed = assemble_meridian(range(6), [zero, zero])
        for s, there in enumerate((has_low, has_high)):
            mer_out[k, s] = packed[s]

            @pl.when(there)
            def _():
                for copy in copies[3 + 3 * s : 6 + 3 * s]:
                    copy.start()

        for s, (b, e) in enumerate(((0, 0), (5, 3))):
            for a in range(6):
                first = a * PLANE + b * 48 + e
                az_out[k, s, a * 12 : a * 12 + 8, :] = upd[pl.ds(first, 8, stride=4), :]
                az_out[k, s, a * 12 + 8 : a * 12 + 12, :] = upd[pl.ds(first + 32, 4, stride=4), :]
            copies[1 + s].start()

    def finish(copies):
        for copy in copies[1:3]:
            copy.wait_recv()
        for s, came in enumerate((has_high, has_low)):

            @pl.when(came)
            def _():
                for copy in copies[3 + 3 * s : 6 + 3 * s]:
                    copy.wait_recv()

    def finish_sends(copies):
        for copy in copies[:3]:
            copy.wait_send()
        for s, to in enumerate((has_low, has_high)):

            @pl.when(to)
            def _():
                for copy in copies[3 + 3 * s : 6 + 3 * s]:
                    copy.wait_send()

    def add_halo(k, field):
        for s, (b, e) in enumerate(((5, 3), (0, 0))):
            for a in range(6):
                first = a * PLANE + b * 48 + e
                for skip, count in ((0, 8), (8, 4)):
                    r = pl.ds(first + 4 * skip, count, stride=4)
                    field[r, :] = field[r, :] + az_in[k, s, a * 12 + skip : a * 12 + skip + count, :]

        for s, (c, to_lane, there) in enumerate(((5, 127, has_high), (0, 0, has_low))):

            @pl.when(there)
            def _():
                from_high, direct, from_low = (mer_in[k, s * 3 + i] for i in range(3))
                for n in range(36):
                    moved = pltpu.roll(direct, (to_lane - n) % 128, 1)
                    r = slice(n * 48 + c * 8, n * 48 + c * 8 + 8)
                    field[r, :] = field[r, :] + jnp.where(lane == to_lane, moved, zero)
                for a in range(6):
                    moved = pltpu.roll(from_high, (to_lane - a * 6) % 128, 1)
                    moved = jnp.where(jnp.logical_and(lane == to_lane, row_az == 0), moved, zero)
                    r = a * PLANE + 5 * 48 + c * 8 + 3
                    field[r : r + 5, :] = field[r : r + 5, :] + moved[0:5]
                    moved = pltpu.roll(from_low, (to_lane - a * 6 - 5) % 128, 1)
                    moved = jnp.where(jnp.logical_and(lane == to_lane, row_az == 3), moved, zero)
                    r = a * PLANE + c * 8
                    field[r : r + 5, :] = field[r : r + 5, :] + moved[3:8]

    def strip(field):
        sums = []
        for first in (0, 5 * PLANE + 4):
            total = jnp.zeros((4, 128), F32)
            for n in range(36):
                r = slice(first + n * 8, first + n * 8 + 4)
                total = total + face_weight[n * 4 : n * 4 + 4, :] * (mass[r, :] * field[r, :])
            sums.append(total)
        return jnp.where(dep == 0, sums[0], sums[1])

    loads[0].wait()
    heat_gradients(1)
    loads[8].wait()
    late_table = felt_table(1)
    loads[1].wait()
    loads[2].wait()
    coefficients(late_table)
    loads[3].wait()
    loads[4].wait()

    loads[9].wait()
    first_copies = face_copies(0)
    update(adj, 0, first_copies[0])
    exchange(0, first_copies)

    strip_late = strip(adj)

    def add_mid(a, _):
        here = rows(a * PLANE, PLANE)
        mid[here, :] = adj[here, :] + upd[here, :]
        return 0

    lax.fori_loop(0, 6, add_mid, 0)
    loads[5].wait()
    heat_gradients(0)
    coefficients(felt_table(0))
    finish(first_copies)
    add_halo(0, mid)

    strip_grad = STEP * (strip_late + strip(mid))
    total = jnp.broadcast_to(jnp.sum(strip_grad, axis=1, keepdims=True), (4, 128))
    group_of = lax.div(lane1, 2 * PAN_DEV)
    mine = jnp.zeros((1, 128), F32)
    for e in range(4):
        mine = jnp.where(group_of == e, total[e : e + 1, :], mine)
    tot_out[...] = mine

    def tot_copies(to, slot):
        return [
            pltpu.make_async_remote_copy(
                src_ref=tot_out,
                dst_ref=tot_in.at[s, slot],
                send_sem=tot_send.at[s, to],
                recv_sem=tot_recv.at[s, slot],
                device_id=column(-s, to),
                device_id_type=MESH,
            )
            for s in (0, 1)
        ]

    def send_totals(position, _):
        for copy in tot_copies(position, mer):
            copy.start()
        return 0

    lax.fori_loop(0, mer, send_totals, 0)
    second_copies = face_copies(1)
    update(mid, 1, second_copies[0])
    exchange(1, second_copies)

    lane4 = lax.broadcasted_iota(jnp.int32, (4, 128), 1)
    suffix = strip_grad
    for shift in (1, 2, 4, 8, 16, 32, 64):
        suffix = suffix + jnp.where(lane4 < 128 - shift, pltpu.roll(suffix, 128 - shift, 1), 0.0)

    flat = (az * N_MER + mer) * N_DEP + dep
    before = (lax.rem(az + N_AZ - 1, N_AZ) * N_MER + mer) * N_DEP + dep
    loads[10].wait()
    owners = owner[...]
    own = owners - flat * PAN_DEV
    prev = owners - before * PAN_DEV
    slot = jnp.where(
        jnp.logical_and(own >= 0, own < PAN_DEV),
        own,
        jnp.where(jnp.logical_and(prev >= 0, prev < PAN_DEV), prev + PAN_DEV, -1),
    )
    panel = lax.broadcasted_iota(jnp.int32, (2 * PAN_DEV, 128), 0)
    hits = [jnp.broadcast_to(slot[e : e + 1, :], (2 * PAN_DEV, 128)) == panel for e in range(4)]
    counts = jnp.concatenate([jnp.where(hit, 1.0, 0.0) for hit in hits], axis=0)
    parts = jnp.concatenate(
        [jnp.where(hits[e], jnp.broadcast_to(suffix[e : e + 1, :], (2 * PAN_DEV, 128)), 0.0) for e in range(4)], axis=0
    )

    def lane_sums(values, precision):
        return lax.dot_general(
            jnp.ones((8, 128), values.dtype),
            values,
            (((1,), (1,)), ((), ())),
            precision=precision,
            preferred_element_type=F32,
        )

    counts = lane_sums(counts.astype(jnp.bfloat16), None)
    parts = lane_sums(parts, lax.Precision.HIGHEST)
    pan_out[0] = parts
    pan_out[1] = counts
    pan_copy = pltpu.make_async_remote_copy(
        src_ref=pan_out,
        dst_ref=pan_in,
        send_sem=pan_send,
        recv_sem=pan_recv,
        device_id=at(-1, 0, 0),
        device_id_type=MESH,
    )
    pan_copy.start()

    def add_out(a, _):
        here = rows(a * PLANE, PLANE)
        out[here, :] = mid[here, :] + upd[here, :]
        return 0

    lax.fori_loop(0, 6, add_out, 0)
    finish(second_copies)
    add_halo(1, out)

    pan_copy.wait_recv()
    def receive_totals(position, sums):
        for copy in tot_copies(0, position):
            copy.wait_recv()
        return tuple(total + tot_in[s, position] for s, total in enumerate(sums))

    none = jnp.zeros((1, 128), F32)
    carried = lax.fori_loop(mer + 1, N_MER, receive_totals, (none, none))

    def finish_totals(position, _):
        for copy in tot_copies(position, mer):
            copy.wait_send()
        return 0

    lax.fori_loop(0, mer, finish_totals, 0)
    finish_sends(first_copies)
    finish_sends(second_copies)
    pan_copy.wait_send()

    whole = parts + counts * carried[0]
    other = pan_in[0] + pan_in[1] * carried[1]
    whole = whole + pltpu.roll(other, 128 - PAN_DEV, 1)
    whole = whole + pltpu.roll(whole, 64, 1)
    whole = whole + pltpu.roll(whole, 96, 1)
    panels[...] = whole[0:1, 0:PAN_DEV]


def shards(
    adjoint_end,
    temp_early,
    temp_late,
    mass_inverse,
    thermal_transport_coefficient,
    jacobian_quadrature_scales,
    measured,
    sensor_cell_slot,
    sensor_gridsite_slot,
    face_weight,
    panel_owner,
):
    shape = adjoint_end.shape

    def flat(array):
        return array.reshape(-1, 128)

    hbm = pl.BlockSpec(memory_space=pltpu.HBM)
    vmem = pl.BlockSpec(memory_space=pltpu.VMEM)
    field = pltpu.VMEM((ROWS, 128), F32)
    small = pltpu.VMEM((8, 128), F32)
    start, panel_grad = pl.pallas_call(
        kernel,
        out_shape=(
            pltpu.VMEM((ROWS, 128), F32),
            pltpu.VMEM((1, PAN_DEV), F32),
        ),
        in_specs=[hbm] * 11,
        out_specs=(vmem, vmem),
        scratch_shapes=[
            pltpu.SMEM((2, SENSORS), F32),
            pltpu.SMEM((SENSORS,), jnp.int32),
            pltpu.SMEM((SENSORS,), jnp.int32),
            pltpu.VMEM((144, 128), F32),
            pltpu.VMEM((4, 128), jnp.int32),
            field,
            pltpu.VMEM((108, 16, 128), jnp.bfloat16),
            pltpu.VMEM((108, 16, 128), jnp.bfloat16),
            field,
            field,
            pltpu.VMEM((3 * ROWS, 128), jnp.bfloat16),
            field,
            pltpu.VMEM((3, ROWS, 128), F32),
            pltpu.VMEM((3, ROWS, 128), F32),
            field,
            pltpu.VMEM((ROWS, 128), jnp.bfloat16),
            field,
            field,
            field,
            pltpu.VMEM((2, SENSORS, 128), F32),
            pltpu.VMEM((2, 2, 72, 128), F32),
            pltpu.VMEM((2, 2, 72, 128), F32),
            pltpu.VMEM((2, 144, 128), F32),
            pltpu.VMEM((2, 144, 128), F32),
            pltpu.VMEM((2, 2, 8, 128), F32),
            pltpu.VMEM((2, 6, 8, 128), F32),
            pltpu.VMEM((1, 128), F32),
            pltpu.VMEM((2, N_MER, 1, 128), F32),
            pltpu.VMEM((2, 8, 128), F32),
            pltpu.VMEM((2, 8, 128), F32),
            pltpu.SemaphoreType.DMA((11,)),
            pltpu.SemaphoreType.DMA((2, 9)),
            pltpu.SemaphoreType.DMA((2, 9)),
            pltpu.SemaphoreType.DMA((2, N_MER)),
            pltpu.SemaphoreType.DMA((2, N_MER)),
            pltpu.SemaphoreType.DMA,
            pltpu.SemaphoreType.DMA,
        ],
        compiler_params=pltpu.CompilerParams(
            collective_id=0, has_side_effects=True, vmem_limit_bytes=60 * 1024 * 1024
        ),
        name="adjoint_steps",
    )(
        flat(adjoint_end),
        temp_early.reshape(108, 16, 128),
        temp_late.reshape(108, 16, 128),
        flat(mass_inverse),
        flat(thermal_transport_coefficient),
        flat(jacobian_quadrature_scales),
        measured,
        sensor_cell_slot,
        sensor_gridsite_slot,
        flat(face_weight),
        flat(panel_owner),
    )
    return start.reshape(shape), panel_grad.reshape(PAN_DEV)


def solution(mesh):
    field = P(None, None, None, "depth", "azimuth", "meridian")
    line = P(("azimuth", "meridian", "depth"))
    placed = (
        field,
        field,
        field,
        field,
        field,
        P(None, None, None, None, "depth", "azimuth", "meridian"),
        P(None, ("azimuth", "meridian", "depth")),
        line,
        line,
        P("depth", None, None, "azimuth", "meridian"),
        P("depth", "azimuth", "meridian"),
    )
    return jax.shard_map(shards, mesh=mesh, in_specs=placed, out_specs=(field, line), check_vma=False)
```

```python
import math

import jax
import jax.numpy as jnp
import numpy as np
from jax import lax
from jax.experimental import pallas as pl
from jax.experimental.pallas import tpu as pltpu
from jax.sharding import PartitionSpec as P

N_AZ, N_MER, N_DEP = 4, 32, 2
ROWS = 1728
PLANE = 288
PAN_DEV = 16
SENSORS = 16
STEP = 0.1
F32 = jnp.float32
MESH = pl.DeviceIdType.MESH


def gll_derivative():
    root_seven = math.sqrt(7.0)
    inner_near = math.sqrt((7.0 - 2.0 * root_seven) / 21.0)
    inner_far = math.sqrt((7.0 + 2.0 * root_seven) / 21.0)
    points = np.array([-1.0, -inner_far, -inner_near, inner_near, inner_far, 1.0])
    legendre = (63.0 * points**5 - 70.0 * points**3 + 15.0 * points) / 8.0
    entries = np.zeros((6, 6))
    for i in range(6):
        for j in range(6):
            if i != j:
                entries[i, j] = legendre[i] / (legendre[j] * (points[i] - points[j]))
    entries[0, 0] = -7.5
    entries[5, 5] = 7.5
    return entries


DER = gll_derivative()
FLIP = DER[:, ::-1]
GRAD_EVEN = (0.5 * (DER + FLIP))[:3, :3]
GRAD_ODD = (0.5 * (DER - FLIP))[:3, :3]
TRA = DER.T
DIV_EVEN = (0.5 * (TRA + TRA[:, ::-1]))[:3, :3]
DIV_ODD = (0.5 * (TRA - TRA[:, ::-1]))[:3, :3]


def grad_line(x):
    e = [x[j] + x[5 - j] for j in range(3)]
    o = [x[j] - x[5 - j] for j in range(3)]
    e1, e2 = e[1] - e[0], e[2] - e[0]
    p = [float(GRAD_EVEN[i, 1]) * e1 + float(GRAD_EVEN[i, 2]) * e2 for i in range(3)]
    q = [
        float(GRAD_ODD[i, 0]) * o[0] + float(GRAD_ODD[i, 1]) * o[1] + float(GRAD_ODD[i, 2]) * o[2]
        for i in range(3)
    ]
    return [q[i] + p[i] for i in range(3)] + [q[i] - p[i] for i in (2, 1, 0)]


def div_line(f):
    e = [f[j] + f[5 - j] for j in range(3)]
    o = [f[j] - f[5 - j] for j in range(3)]
    p = [
        float(DIV_EVEN[i, 0]) * e[0] + float(DIV_EVEN[i, 1]) * e[1] + float(DIV_EVEN[i, 2]) * e[2]
        for i in range(3)
    ]
    q1, q2 = [
        float(DIV_ODD[i, 0]) * o[0] + float(DIV_ODD[i, 1]) * o[1] + float(DIV_ODD[i, 2]) * o[2]
        for i in (1, 2)
    ]
    q0 = -(q1 + q2)
    q = [q0, q1, q2]
    return [q[i] + p[i] for i in range(3)] + [q[i] - p[i] for i in (2, 1, 0)]


def rows(start, size, multiple=8):
    if isinstance(start, int):
        return pl.ds(start, size)
    return pl.ds(pl.multiple_of(start, multiple), size)


def line_rows(direction, outer, inner):
    if direction == 0:
        return [rows(j * PLANE + outer * 48 + inner * 16, 16, 16) for j in range(6)]
    if direction == 1:
        return [rows(outer * PLANE + j * 48 + inner * 16, 16, 16) for j in range(6)]
    return [rows(outer * PLANE + inner * 48 + j * 8, 8, 8) for j in range(6)]


def inner_count(direction):
    return 6 if direction == 2 else 3


def kernel(
    adj_hbm,
    early_hbm,
    late_hbm,
    mass_hbm,
    cond_hbm,
    metric_hbm,
    measured_hbm,
    cell_hbm,
    site_hbm,
    face_weight_hbm,
    owner_hbm,
    out,
    panels,
    measured,
    cell,
    site,
    face_weight,
    owner,
    adj,
    temp_early,
    temp_late,
    mass,
    cond,
    metric,
    heat,
    flux_c,
    cross_c,
    source,
    hot,
    scaled,
    upd,
    mid,
    spots,
    az_out,
    az_in,
    dep_out,
    dep_in,
    mer_out,
    mer_in,
    tot_out,
    tot_in,
    pan_out,
    pan_in,
    load_sem,
    face_send,
    face_recv,
    tot_send,
    tot_recv,
    pan_send,
    pan_recv,
):
    az = lax.axis_index("azimuth")
    mer = lax.axis_index("meridian")
    dep = lax.axis_index("depth")

    def at(da, dm, dd):
        return {
            "azimuth": lax.rem(az + (da + N_AZ), N_AZ),
            "meridian": mer + dm,
            "depth": lax.rem(dep + dd, N_DEP),
        }

    def column(da, position):
        return {"azimuth": lax.rem(az + (da + N_AZ), N_AZ), "meridian": position, "depth": dep}

    has_low, has_high = mer > 0, mer < N_MER - 1

    loads = [
        (late_hbm, temp_late),
        (metric_hbm, metric),
        (cond_hbm, cond),
        (mass_hbm, mass),
        (adj_hbm, adj),
        (early_hbm, temp_early),
        (site_hbm, site),
        (cell_hbm, cell),
        (measured_hbm, measured),
        (face_weight_hbm, face_weight),
        (owner_hbm, owner),
    ]
    loads = [pltpu.make_async_copy(s, d, load_sem.at[i]) for i, (s, d) in enumerate(loads)]
    for n in (6, 7, 0, 8, 1, 2, 3, 4, 9, 5, 10):
        loads[n].start()

    barrier = pltpu.get_barrier_semaphore()
    def greet(peer):
        pl.semaphore_signal(barrier, inc=1, device_id=peer, device_id_type=MESH)

    greet(at(0, 0, 1))
    greet(at(-1, 0, 0))
    greet(at(1, 0, 0))
    for there, dm in ((has_low, -1), (has_high, 1)):

        @pl.when(there)
        def _():
            for da in (-1, 0, 1):
                greet(at(da, dm, 0))

    def greet_higher(position, _):
        for da in (0, 1):
            greet(column(da, position))
        return 0

    lax.fori_loop(mer + 1, N_MER, greet_higher, 0)
    greeted = 3 + 3 * (has_low.astype(jnp.int32) + has_high.astype(jnp.int32)) + 2 * mer

    row8 = lax.broadcasted_iota(jnp.int32, (8, 128), 0)
    lane = lax.broadcasted_iota(jnp.int32, (8, 128), 1)
    row_az = lax.rem(row8, 4)
    row_dep = lax.div(row8, 4)
    zero = jnp.zeros((8, 128), F32)

    lane1 = lax.broadcasted_iota(jnp.int32, (1, 128), 1)
    row16 = lax.broadcasted_iota(jnp.int32, (16, 128), 0)
    lane16 = lax.broadcasted_iota(jnp.int32, (16, 128), 1)
    for n in (6, 7):
        loads[n].wait()
    code = jnp.full((1, 128), -1, jnp.int32)
    for q in range(SENSORS):
        word = site[q] * 8 + lax.shift_right_logical(cell[q], 7)
        code = jnp.where(jnp.logical_and(lax.rem(lane1, SENSORS) == q, lane1 < 3 * SENSORS), word, code)

    def place(a, _):
        base = lax.broadcasted_iota(jnp.int32, (PLANE, 128), 0) + a * PLANE
        hot[rows(a * PLANE, PLANE, 16), :] = jnp.where(base == code, 1.0, 0.0).astype(jnp.bfloat16)
        return 0

    lax.fori_loop(0, 6, place, 0)

    temps = (temp_early, temp_late)

    def felt_table(k):
        for q in range(SENSORS):
            tile_row = jnp.bitwise_and(site[q], 1) * 8 + lax.shift_right_logical(cell[q], 7)
            there = jnp.logical_and(row16 == tile_row, lane16 == jnp.bitwise_and(cell[q], 127))
            felt = temps[k][lax.shift_right_logical(site[q], 1)].astype(F32)
            value = jnp.where(there, felt - measured[k, q], 0.0)
            spots[k, q : q + 1, :] = jnp.sum(value, axis=0, keepdims=True)
        value = spots[k]
        high = value.astype(jnp.bfloat16).astype(F32)
        rest = value - high
        middle = rest.astype(jnp.bfloat16).astype(F32)
        low = rest - middle
        return jnp.concatenate([high, middle, low, jnp.zeros((80, 128), F32)], axis=0).astype(jnp.bfloat16)

    def heat_gradients(k):
        def plane(a, _):
            h = temps[k][pl.ds(a * 18, 18)].astype(F32).reshape(PLANE, 128)
            heat[rows(a * PLANE, PLANE), :] = h
            return 0

        lax.fori_loop(0, 6, plane, 0)

        def direction(d):
            def body(outer, _):
                for inner in range(inner_count(d)):
                    at_rows = line_rows(d, outer, inner)
                    for r, g in zip(at_rows, grad_line([heat[r, :] for r in at_rows])):
                        cross_c[d, r, :] = g
                return 0

            lax.fori_loop(0, 6, body, 0)

        for d in range(3):
            direction(d)

    def coefficients(table):
        def plane(a, _):
            for part in range(6):
                first = a * PLANE + part * 48
                r = rows(first, 48, 16)
                h = heat[r, :]
                c = (-STEP) * cond[r, :]
                kap = c * (1.0 + 0.5 * h * h)
                slope = c * h
                for d in range(3):
                    w = metric[rows(d * ROWS + first, 48, 16), :].astype(F32)
                    flux_c[d, r, :] = kap * w
                    cross_c[d, r, :] = slope * w * cross_c[d, r, :]
            here = rows(a * PLANE, PLANE, 16)
            source[here, :] = jnp.dot(hot[here, :], table, preferred_element_type=F32)
            return 0

        lax.fori_loop(0, 6, plane, 0)

    def update(field, k, depth_copy):
        def add_lines(d, outer):
            for inner in range(inner_count(d)):
                at_rows = line_rows(d, outer, inner)
                if d == 0:
                    values = [mass[r, :] * field[r, :] for r in at_rows]
                    for r, value in zip(at_rows, values):
                        scaled[r, :] = value
                else:
                    values = [scaled[r, :] for r in at_rows]
                g = grad_line(values)
                flux = [flux_c[d, r, :] * g[j] for j, r in enumerate(at_rows)]
                spread = div_line(flux)
                for j, r in enumerate(at_rows):
                    total = spread[j] + cross_c[d, r, :] * g[j]
                    upd[r, :] = (source if d == 0 else upd)[r, :] + total

        def depth_lines(b, _):
            add_lines(0, b)
            return 0

        def plane(i, _):
            a = jnp.where(i == 0, 5 * (1 - dep), i - 1 + dep)
            add_lines(1, a)
            add_lines(2, a)
            return 0

        lax.fori_loop(0, 6, depth_lines, 0)
        lax.fori_loop(0, 1, plane, 0)
        for d in (0, 1):
            first = (5 * PLANE + 4, 0)[d]

            @pl.when(dep == d)
            def _():
                for n in range(36):
                    r = first + n * 8
                    dep_out[k, n * 4 : n * 4 + 4, :] = upd[r : r + 4, :]

        if k == 0:
            pl.semaphore_wait(barrier, greeted)
        depth_copy.start()
        lax.fori_loop(1, 6, plane, 0)

    row7_az = row_az[0:7]

    def assemble_azimuth_depth():
        for a in range(6):
            for c in range(6):
                lo, hi = (a * PLANE + b * 48 + c * 8 for b in (0, 5))
                low, high = upd[lo + 1 : lo + 8, :], upd[hi : hi + 7, :]
                both = low + high
                upd[hi : hi + 7, :] = jnp.where(row7_az < 3, both, high)
                upd[lo + 1 : lo + 8, :] = jnp.where(row7_az < 3, both, low)
        for n in range(36):
            lo, hi = n * 8 + 4, 5 * PLANE + n * 8
            both = upd[lo : lo + 4, :] + upd[hi : hi + 4, :]
            upd[lo : lo + 4, :] = both
            upd[hi : hi + 4, :] = both

    def assemble_meridian(planes, packed):
        for a in planes:
            for b in range(0, 6, 2):
                ends = []
                for n in (a * 6 + b, a * 6 + b + 1):
                    lo, hi = slice(n * 48, n * 48 + 8), slice(n * 48 + 40, n * 48 + 48)
                    low, high = upd[lo, :], upd[hi, :]
                    low_moved, high_moved = pltpu.roll(low, 127, 1), pltpu.roll(high, 1, 1)
                    upd[hi, :] = high + jnp.where(lane < 127, low_moved, zero)
                    upd[lo, :] = low + jnp.where(lane > 0, high_moved, zero)
                    ends.append((low, low_moved, high, high_moved))
                n = a * 6 + b
                pairs = (
                    jnp.where(lane == 127, ends[0][1], ends[1][0]),
                    jnp.where(lane == 127, ends[0][2], ends[1][3]),
                )
                for s in (0, 1):
                    moved = pltpu.roll(pairs[s], n + 1, 1)
                    packed[s] = jnp.where(jnp.logical_or(lane == n, lane == n + 1), moved, packed[s])
        return packed

    def remote(src, dst, k, n, peer):
        return pltpu.make_async_remote_copy(
            src_ref=src,
            dst_ref=dst,
            send_sem=face_send.at[k, n],
            recv_sem=face_recv.at[k, n],
            device_id=peer,
            device_id_type=MESH,
        )

    def face_copies(k):
        copies = [remote(dep_out.at[k], dep_in.at[k], k, 0, at(0, 0, 1))]
        for s, da in enumerate((-1, 1)):
            copies.append(remote(az_out.at[k, s], az_in.at[k, s], k, 1 + s, at(da, 0, 0)))
        for s, dm in enumerate((-1, 1)):
            for i, da in enumerate((-1, 0, 1)):
                n = 3 + s * 3 + i
                copies.append(remote(mer_out.at[k, s], mer_in.at[k, s * 3 + i], k, n, at(da, dm, 0)))
        return copies

    def exchange(k, copies):
        copies[0].wait_recv()
        for d in (0, 1):
            first = (5 * PLANE + 4, 0)[d]

            @pl.when(dep == d)
            def _():
                for n in range(36):
                    r = first + n * 8
                    upd[r : r + 4, :] = upd[r : r + 4, :] + dep_in[k, n * 4 : n * 4 + 4, :]

        assemble_azimuth_depth()
        packed = assemble_meridian(range(6), [zero, zero])
        for s, there in enumerate((has_low, has_high)):
            mer_out[k, s] = packed[s]

            @pl.when(there)
            def _():
                for copy in copies[3 + 3 * s : 6 + 3 * s]:
                    copy.start()

        for s, (b, e) in enumerate(((0, 0), (5, 3))):
            for a in range(6):
                first = a * PLANE + b * 48 + e
                az_out[k, s, a * 12 : a * 12 + 8, :] = upd[pl.ds(first, 8, stride=4), :]
                az_out[k, s, a * 12 + 8 : a * 12 + 12, :] = upd[pl.ds(first + 32, 4, stride=4), :]
            copies[1 + s].start()

    def finish(copies):
        for copy in copies[1:3]:
            copy.wait_recv()
        for s, came in enumerate((has_high, has_low)):

            @pl.when(came)
            def _():
                for copy in copies[3 + 3 * s : 6 + 3 * s]:
                    copy.wait_recv()

    def finish_sends(copies):
        for copy in copies[:3]:
            copy.wait_send()
        for s, to in enumerate((has_low, has_high)):

            @pl.when(to)
            def _():
                for copy in copies[3 + 3 * s : 6 + 3 * s]:
                    copy.wait_send()

    def add_halo(k, field, planes):
        for s, (b, e) in enumerate(((5, 3), (0, 0))):
            for a in planes:
                first = a * PLANE + b * 48 + e
                for skip, count in ((0, 8), (8, 4)):
                    r = pl.ds(first + 4 * skip, count, stride=4)
                    field[r, :] = field[r, :] + az_in[k, s, a * 12 + skip : a * 12 + skip + count, :]

        for s, (c, to_lane, there) in enumerate(((5, 127, has_high), (0, 0, has_low))):

            @pl.when(there)
            def _():
                from_high, direct, from_low = (mer_in[k, s * 3 + i] for i in range(3))
                for n in [a * 6 + b for a in planes for b in range(6)]:
                    moved = pltpu.roll(direct, (to_lane - n) % 128, 1)
                    r = slice(n * 48 + c * 8, n * 48 + c * 8 + 8)
                    field[r, :] = field[r, :] + jnp.where(lane == to_lane, moved, zero)
                for a in planes:
                    moved = pltpu.roll(from_high, (to_lane - a * 6) % 128, 1)
                    moved = jnp.where(jnp.logical_and(lane == to_lane, row_az == 0), moved, zero)
                    r = a * PLANE + 5 * 48 + c * 8 + 3
                    field[r : r + 5, :] = field[r : r + 5, :] + moved[0:5]
                    moved = pltpu.roll(from_low, (to_lane - a * 6 - 5) % 128, 1)
                    moved = jnp.where(jnp.logical_and(lane == to_lane, row_az == 3), moved, zero)
                    r = a * PLANE + c * 8
                    field[r : r + 5, :] = field[r : r + 5, :] + moved[3:8]

    def strip(field):
        sums = []
        for first in (0, 5 * PLANE + 4):
            total = jnp.zeros((4, 128), F32)
            for n in range(36):
                r = slice(first + n * 8, first + n * 8 + 4)
                total = total + face_weight[n * 4 : n * 4 + 4, :] * (mass[r, :] * field[r, :])
            sums.append(total)
        return jnp.where(dep == 0, sums[0], sums[1])

    loads[0].wait()
    heat_gradients(1)
    loads[8].wait()
    late_table = felt_table(1)
    loads[1].wait()
    loads[2].wait()
    coefficients(late_table)
    loads[3].wait()
    loads[4].wait()

    loads[9].wait()
    first_copies = face_copies(0)
    update(adj, 0, first_copies[0])
    exchange(0, first_copies)

    strip_late = strip(adj)

    def add_mid(a, _):
        here = rows(a * PLANE, PLANE)
        mid[here, :] = adj[here, :] + upd[here, :]
        return 0

    lax.fori_loop(0, 6, add_mid, 0)
    loads[5].wait()
    heat_gradients(0)
    coefficients(felt_table(0))
    finish(first_copies)
    add_halo(0, mid, (0, 5))

    strip_grad = STEP * (strip_late + strip(mid))
    total = jnp.broadcast_to(jnp.sum(strip_grad, axis=1, keepdims=True), (4, 128))
    group_of = lax.div(lane1, 2 * PAN_DEV)
    mine = jnp.zeros((1, 128), F32)
    for e in range(4):
        mine = jnp.where(group_of == e, total[e : e + 1, :], mine)
    tot_out[...] = mine

    def tot_copies(to, slot):
        return [
            pltpu.make_async_remote_copy(
                src_ref=tot_out,
                dst_ref=tot_in.at[s, slot],
                send_sem=tot_send.at[s, to],
                recv_sem=tot_recv.at[s, slot],
                device_id=column(-s, to),
                device_id_type=MESH,
            )
            for s in (0, 1)
        ]

    def send_totals(position, _):
        for copy in tot_copies(position, mer):
            copy.start()
        return 0

    lax.fori_loop(0, mer, send_totals, 0)
    add_halo(0, mid, (1, 2, 3, 4))
    second_copies = face_copies(1)
    update(mid, 1, second_copies[0])
    exchange(1, second_copies)

    lane4 = lax.broadcasted_iota(jnp.int32, (4, 128), 1)
    suffix = strip_grad
    for shift in (1, 2, 4, 8, 16, 32, 64):
        suffix = suffix + jnp.where(lane4 < 128 - shift, pltpu.roll(suffix, 128 - shift, 1), 0.0)

    flat = (az * N_MER + mer) * N_DEP + dep
    before = (lax.rem(az + N_AZ - 1, N_AZ) * N_MER + mer) * N_DEP + dep
    loads[10].wait()
    owners = owner[...]
    own = owners - flat * PAN_DEV
    prev = owners - before * PAN_DEV
    slot = jnp.where(
        jnp.logical_and(own >= 0, own < PAN_DEV),
        own,
        jnp.where(jnp.logical_and(prev >= 0, prev < PAN_DEV), prev + PAN_DEV, -1),
    )
    panel = lax.broadcasted_iota(jnp.int32, (2 * PAN_DEV, 128), 0)
    hits = [jnp.broadcast_to(slot[e : e + 1, :], (2 * PAN_DEV, 128)) == panel for e in range(4)]
    counts = jnp.concatenate([jnp.where(hit, 1.0, 0.0) for hit in hits], axis=0)
    parts = jnp.concatenate(
        [jnp.where(hits[e], jnp.broadcast_to(suffix[e : e + 1, :], (2 * PAN_DEV, 128)), 0.0) for e in range(4)], axis=0
    )

    def lane_sums(values, precision):
        return lax.dot_general(
            jnp.ones((8, 128), values.dtype),
            values,
            (((1,), (1,)), ((), ())),
            precision=precision,
            preferred_element_type=F32,
        )

    counts = lane_sums(counts.astype(jnp.bfloat16), None)
    parts = lane_sums(parts, lax.Precision.HIGHEST)
    pan_out[0] = parts
    pan_out[1] = counts
    pan_copy = pltpu.make_async_remote_copy(
        src_ref=pan_out,
        dst_ref=pan_in,
        send_sem=pan_send,
        recv_sem=pan_recv,
        device_id=at(-1, 0, 0),
        device_id_type=MESH,
    )
    pan_copy.start()

    def add_out(a, _):
        here = rows(a * PLANE, PLANE)
        out[here, :] = mid[here, :] + upd[here, :]
        return 0

    lax.fori_loop(0, 6, add_out, 0)
    finish(second_copies)
    add_halo(1, out, range(6))

    pan_copy.wait_recv()
    def finish_totals(position, _):
        for copy in tot_copies(position, mer):
            copy.wait_send()
        return 0

    lax.fori_loop(0, mer, finish_totals, 0)
    finish_sends(first_copies)
    finish_sends(second_copies)
    pan_copy.wait_send()
    pan_other = pan_in[...]

    def receive_totals(position, sums):
        for copy in tot_copies(0, position):
            copy.wait_recv()
        return tuple(total + tot_in[s, position] for s, total in enumerate(sums))

    none = jnp.zeros((1, 128), F32)
    carried = lax.fori_loop(mer + 1, N_MER, receive_totals, (none, none))

    whole = parts + counts * carried[0]
    other = pan_other[0] + pan_other[1] * carried[1]
    pieces = [whole] + [pltpu.roll(whole, 128 - 32 * e, 1) for e in (1, 2, 3)]
    pieces += [pltpu.roll(other, 128 - 32 * e - PAN_DEV, 1) for e in (0, 1, 2, 3)]
    while len(pieces) > 1:
        pieces = [pieces[i] + pieces[i + 1] for i in range(0, len(pieces), 2)]
    whole = pieces[0]
    panels[...] = whole[0:1, 0:PAN_DEV]


def shards(
    adjoint_end,
    temp_early,
    temp_late,
    mass_inverse,
    thermal_transport_coefficient,
    jacobian_quadrature_scales,
    measured,
    sensor_cell_slot,
    sensor_gridsite_slot,
    face_weight,
    panel_owner,
):
    shape = adjoint_end.shape

    def flat(array):
        return array.reshape(-1, 128)

    hbm = pl.BlockSpec(memory_space=pltpu.HBM)
    vmem = pl.BlockSpec(memory_space=pltpu.VMEM)
    field = pltpu.VMEM((ROWS, 128), F32)
    small = pltpu.VMEM((8, 128), F32)
    start, panel_grad = pl.pallas_call(
        kernel,
        out_shape=(
            pltpu.VMEM((ROWS, 128), F32),
            pltpu.VMEM((1, PAN_DEV), F32),
        ),
        in_specs=[hbm] * 11,
        out_specs=(vmem, vmem),
        scratch_shapes=[
            pltpu.SMEM((2, SENSORS), F32),
            pltpu.SMEM((SENSORS,), jnp.int32),
            pltpu.SMEM((SENSORS,), jnp.int32),
            pltpu.VMEM((144, 128), F32),
            pltpu.VMEM((4, 128), jnp.int32),
            field,
            pltpu.VMEM((108, 16, 128), jnp.bfloat16),
            pltpu.VMEM((108, 16, 128), jnp.bfloat16),
            field,
            field,
            pltpu.VMEM((3 * ROWS, 128), jnp.bfloat16),
            field,
            pltpu.VMEM((3, ROWS, 128), F32),
            pltpu.VMEM((3, ROWS, 128), F32),
            field,
            pltpu.VMEM((ROWS, 128), jnp.bfloat16),
            field,
            field,
            field,
            pltpu.VMEM((2, SENSORS, 128), F32),
            pltpu.VMEM((2, 2, 72, 128), F32),
            pltpu.VMEM((2, 2, 72, 128), F32),
            pltpu.VMEM((2, 144, 128), F32),
            pltpu.VMEM((2, 144, 128), F32),
            pltpu.VMEM((2, 2, 8, 128), F32),
            pltpu.VMEM((2, 6, 8, 128), F32),
            pltpu.VMEM((1, 128), F32),
            pltpu.VMEM((2, N_MER, 1, 128), F32),
            pltpu.VMEM((2, 8, 128), F32),
            pltpu.VMEM((2, 8, 128), F32),
            pltpu.SemaphoreType.DMA((11,)),
            pltpu.SemaphoreType.DMA((2, 9)),
            pltpu.SemaphoreType.DMA((2, 9)),
            pltpu.SemaphoreType.DMA((2, N_MER)),
            pltpu.SemaphoreType.DMA((2, N_MER)),
            pltpu.SemaphoreType.DMA,
            pltpu.SemaphoreType.DMA,
        ],
        compiler_params=pltpu.CompilerParams(
            collective_id=0, has_side_effects=True, vmem_limit_bytes=60 * 1024 * 1024
        ),
        name="adjoint_steps",
    )(
        flat(adjoint_end),
        temp_early.reshape(108, 16, 128),
        temp_late.reshape(108, 16, 128),
        flat(mass_inverse),
        flat(thermal_transport_coefficient),
        flat(jacobian_quadrature_scales),
        measured,
        sensor_cell_slot,
        sensor_gridsite_slot,
        flat(face_weight),
        flat(panel_owner),
    )
    return start.reshape(shape), panel_grad.reshape(PAN_DEV)


def solution(mesh):
    field = P(None, None, None, "depth", "azimuth", "meridian")
    line = P(("azimuth", "meridian", "depth"))
    placed = (
        field,
        field,
        field,
        field,
        field,
        P(None, None, None, None, "depth", "azimuth", "meridian"),
        P(None, ("azimuth", "meridian", "depth")),
        line,
        line,
        P("depth", None, None, "azimuth", "meridian"),
        P("depth", "azimuth", "meridian"),
    )
    return jax.shard_map(shards, mesh=mesh, in_specs=placed, out_specs=(field, line), check_vma=False)
```

```python
import math

import jax
import jax.numpy as jnp
import numpy as np
from jax import lax
from jax.experimental import pallas as pl
from jax.experimental.pallas import tpu as pltpu
from jax.sharding import PartitionSpec as P

N_AZ, N_MER, N_DEP = 4, 32, 2
ROWS = 1728
PLANE = 288
PAN_DEV = 16
SENSORS = 16
STEP = 0.1
F32 = jnp.float32
MESH = pl.DeviceIdType.MESH


def gll_derivative():
    root_seven = math.sqrt(7.0)
    inner_near = math.sqrt((7.0 - 2.0 * root_seven) / 21.0)
    inner_far = math.sqrt((7.0 + 2.0 * root_seven) / 21.0)
    points = np.array([-1.0, -inner_far, -inner_near, inner_near, inner_far, 1.0])
    legendre = (63.0 * points**5 - 70.0 * points**3 + 15.0 * points) / 8.0
    entries = np.zeros((6, 6))
    for i in range(6):
        for j in range(6):
            if i != j:
                entries[i, j] = legendre[i] / (legendre[j] * (points[i] - points[j]))
    entries[0, 0] = -7.5
    entries[5, 5] = 7.5
    return entries


DER = gll_derivative()
FLIP = DER[:, ::-1]
GRAD_EVEN = (0.5 * (DER + FLIP))[:3, :3]
GRAD_ODD = (0.5 * (DER - FLIP))[:3, :3]
TRA = DER.T
DIV_EVEN = (0.5 * (TRA + TRA[:, ::-1]))[:3, :3]
DIV_ODD = (0.5 * (TRA - TRA[:, ::-1]))[:3, :3]


def grad_line(x):
    e = [x[j] + x[5 - j] for j in range(3)]
    o = [x[j] - x[5 - j] for j in range(3)]
    e1, e2 = e[1] - e[0], e[2] - e[0]
    p = [float(GRAD_EVEN[i, 1]) * e1 + float(GRAD_EVEN[i, 2]) * e2 for i in range(3)]
    q = [
        float(GRAD_ODD[i, 0]) * o[0] + float(GRAD_ODD[i, 1]) * o[1] + float(GRAD_ODD[i, 2]) * o[2]
        for i in range(3)
    ]
    return [q[i] + p[i] for i in range(3)] + [q[i] - p[i] for i in (2, 1, 0)]


def div_line(f):
    e = [f[j] + f[5 - j] for j in range(3)]
    o = [f[j] - f[5 - j] for j in range(3)]
    p = [
        float(DIV_EVEN[i, 0]) * e[0] + float(DIV_EVEN[i, 1]) * e[1] + float(DIV_EVEN[i, 2]) * e[2]
        for i in range(3)
    ]
    q1, q2 = [
        float(DIV_ODD[i, 0]) * o[0] + float(DIV_ODD[i, 1]) * o[1] + float(DIV_ODD[i, 2]) * o[2]
        for i in (1, 2)
    ]
    q0 = -(q1 + q2)
    q = [q0, q1, q2]
    return [q[i] + p[i] for i in range(3)] + [q[i] - p[i] for i in (2, 1, 0)]


def rows(start, size, multiple=8):
    if isinstance(start, int):
        return pl.ds(start, size)
    return pl.ds(pl.multiple_of(start, multiple), size)


def line_rows(direction, outer, inner):
    if direction == 0:
        return [rows(j * PLANE + outer * 48 + inner * 16, 16, 16) for j in range(6)]
    if direction == 1:
        return [rows(outer * PLANE + j * 48 + inner * 16, 16, 16) for j in range(6)]
    return [rows(outer * PLANE + inner * 48 + j * 8, 8, 8) for j in range(6)]


def inner_count(direction):
    return 6 if direction == 2 else 3


def kernel(
    adj_hbm,
    early_hbm,
    late_hbm,
    mass_hbm,
    cond_hbm,
    metric_hbm,
    measured_hbm,
    cell_hbm,
    site_hbm,
    face_weight_hbm,
    owner_hbm,
    out,
    panels,
    measured,
    cell,
    site,
    face_weight,
    owner,
    adj,
    temp_early,
    temp_late,
    mass,
    cond,
    metric,
    heat,
    flux_c,
    cross_c,
    source,
    hot,
    scaled,
    upd,
    mid,
    spots,
    az_out,
    az_in,
    dep_out,
    dep_in,
    mer_out,
    mer_in,
    tot_out,
    tot_in,
    pan_out,
    pan_in,
    load_sem,
    face_send,
    face_recv,
    tot_send,
    tot_recv,
    pan_send,
    pan_recv,
):
    az = lax.axis_index("azimuth")
    mer = lax.axis_index("meridian")
    dep = lax.axis_index("depth")

    def at(da, dm, dd):
        return {
            "azimuth": lax.rem(az + (da + N_AZ), N_AZ),
            "meridian": mer + dm,
            "depth": lax.rem(dep + dd, N_DEP),
        }

    def column(da, position):
        return {"azimuth": lax.rem(az + (da + N_AZ), N_AZ), "meridian": position, "depth": dep}

    has_low, has_high = mer > 0, mer < N_MER - 1

    loads = [
        (late_hbm, temp_late),
        (metric_hbm, metric),
        (cond_hbm, cond),
        (mass_hbm, mass),
        (adj_hbm, adj),
        (early_hbm, temp_early),
        (site_hbm, site),
        (cell_hbm, cell),
        (measured_hbm, measured),
        (face_weight_hbm, face_weight),
        (owner_hbm, owner),
    ]
    loads = [pltpu.make_async_copy(s, d, load_sem.at[i]) for i, (s, d) in enumerate(loads)]
    for n in (6, 7, 0, 8, 1, 2, 3, 4, 9, 5, 10):
        loads[n].start()

    barrier = pltpu.get_barrier_semaphore()
    def greet(peer):
        pl.semaphore_signal(barrier, inc=1, device_id=peer, device_id_type=MESH)

    greet(at(0, 0, 1))
    greet(at(-1, 0, 0))
    greet(at(1, 0, 0))
    for there, dm in ((has_low, -1), (has_high, 1)):

        @pl.when(there)
        def _():
            for da in (-1, 0, 1):
                greet(at(da, dm, 0))

    def greet_higher(position, _):
        for da in (0, 1):
            greet(column(da, position))
        return 0

    lax.fori_loop(mer + 1, N_MER, greet_higher, 0)
    greeted = 3 + 3 * (has_low.astype(jnp.int32) + has_high.astype(jnp.int32)) + 2 * mer

    row8 = lax.broadcasted_iota(jnp.int32, (8, 128), 0)
    lane = lax.broadcasted_iota(jnp.int32, (8, 128), 1)
    row_az = lax.rem(row8, 4)
    row_dep = lax.div(row8, 4)
    zero = jnp.zeros((8, 128), F32)

    lane1 = lax.broadcasted_iota(jnp.int32, (1, 128), 1)
    row16 = lax.broadcasted_iota(jnp.int32, (16, 128), 0)
    lane16 = lax.broadcasted_iota(jnp.int32, (16, 128), 1)
    for n in (6, 7):
        loads[n].wait()
    code = jnp.full((1, 128), -1, jnp.int32)
    for q in range(SENSORS):
        word = site[q] * 8 + lax.shift_right_logical(cell[q], 7)
        code = jnp.where(jnp.logical_and(lax.rem(lane1, SENSORS) == q, lane1 < 3 * SENSORS), word, code)

    def place(a, _):
        base = lax.broadcasted_iota(jnp.int32, (PLANE, 128), 0) + a * PLANE
        hot[rows(a * PLANE, PLANE, 16), :] = jnp.where(base == code, 1.0, 0.0).astype(jnp.bfloat16)
        return 0

    lax.fori_loop(0, 6, place, 0)

    temps = (temp_early, temp_late)

    def felt_table(k):
        for q in range(SENSORS):
            tile_row = jnp.bitwise_and(site[q], 1) * 8 + lax.shift_right_logical(cell[q], 7)
            there = jnp.logical_and(row16 == tile_row, lane16 == jnp.bitwise_and(cell[q], 127))
            felt = temps[k][lax.shift_right_logical(site[q], 1)].astype(F32)
            value = jnp.where(there, felt - measured[k, q], 0.0)
            spots[k, q : q + 1, :] = jnp.sum(value, axis=0, keepdims=True)
        value = spots[k]
        high = value.astype(jnp.bfloat16).astype(F32)
        rest = value - high
        middle = rest.astype(jnp.bfloat16).astype(F32)
        low = rest - middle
        return jnp.concatenate([high, middle, low, jnp.zeros((80, 128), F32)], axis=0).astype(jnp.bfloat16)

    def heat_gradients(k):
        def plane(a, _):
            h = temps[k][pl.ds(a * 18, 18)].astype(F32).reshape(PLANE, 128)
            heat[rows(a * PLANE, PLANE), :] = h
            return 0

        lax.fori_loop(0, 6, plane, 0)

        def direction(d):
            def body(outer, _):
                for inner in range(inner_count(d)):
                    at_rows = line_rows(d, outer, inner)
                    for r, g in zip(at_rows, grad_line([heat[r, :] for r in at_rows])):
                        cross_c[d, r, :] = g
                return 0

            lax.fori_loop(0, 6, body, 0)

        for d in range(3):
            direction(d)

    def coefficients(table):
        def plane(a, _):
            for part in range(6):
                first = a * PLANE + part * 48
                r = rows(first, 48, 16)
                h = heat[r, :]
                c = (-STEP) * cond[r, :]
                kap = c * (1.0 + 0.5 * h * h)
                slope = c * h
                for d in range(3):
                    w = metric[rows(d * ROWS + first, 48, 16), :].astype(F32)
                    flux_c[d, r, :] = kap * w
                    cross_c[d, r, :] = slope * w * cross_c[d, r, :]
            here = rows(a * PLANE, PLANE, 16)
            source[here, :] = jnp.dot(hot[here, :], table, preferred_element_type=F32)
            return 0

        lax.fori_loop(0, 6, plane, 0)

    def update(field, k, depth_copy):
        def add_lines(d, outer):
            for inner in range(inner_count(d)):
                at_rows = line_rows(d, outer, inner)
                if d == 0:
                    values = [mass[r, :] * field[r, :] for r in at_rows]
                    for r, value in zip(at_rows, values):
                        scaled[r, :] = value
                else:
                    values = [scaled[r, :] for r in at_rows]
                g = grad_line(values)
                flux = [flux_c[d, r, :] * g[j] for j, r in enumerate(at_rows)]
                spread = div_line(flux)
                for j, r in enumerate(at_rows):
                    total = spread[j] + cross_c[d, r, :] * g[j]
                    upd[r, :] = (source if d == 0 else upd)[r, :] + total

        def depth_lines(b, _):
            add_lines(0, b)
            return 0

        def plane(i, _):
            a = jnp.where(i == 0, 5 * (1 - dep), i - 1 + dep)
            add_lines(1, a)
            add_lines(2, a)
            return 0

        lax.fori_loop(0, 6, depth_lines, 0)
        lax.fori_loop(0, 1, plane, 0)
        for d in (0, 1):
            first = (5 * PLANE + 4, 0)[d]

            @pl.when(dep == d)
            def _():
                for n in range(36):
                    r = first + n * 8
                    dep_out[k, n * 4 : n * 4 + 4, :] = upd[r : r + 4, :]

        if k == 0:
            pl.semaphore_wait(barrier, greeted)
        depth_copy.start()
        lax.fori_loop(1, 6, plane, 0)

    row7_az = row_az[0:7]

    def assemble_azimuth_depth():
        for a in range(6):
            for c in range(6):
                lo, hi = (a * PLANE + b * 48 + c * 8 for b in (0, 5))
                low, high = upd[lo + 1 : lo + 8, :], upd[hi : hi + 7, :]
                both = low + high
                upd[hi : hi + 7, :] = jnp.where(row7_az < 3, both, high)
                upd[lo + 1 : lo + 8, :] = jnp.where(row7_az < 3, both, low)
        for n in range(36):
            lo, hi = n * 8 + 4, 5 * PLANE + n * 8
            both = upd[lo : lo + 4, :] + upd[hi : hi + 4, :]
            upd[lo : lo + 4, :] = both
            upd[hi : hi + 4, :] = both

    def assemble_meridian(planes, packed):
        for a in planes:
            for b in range(0, 6, 2):
                ends = []
                for n in (a * 6 + b, a * 6 + b + 1):
                    lo, hi = slice(n * 48, n * 48 + 8), slice(n * 48 + 40, n * 48 + 48)
                    low, high = upd[lo, :], upd[hi, :]
                    low_moved, high_moved = pltpu.roll(low, 127, 1), pltpu.roll(high, 1, 1)
                    upd[hi, :] = high + jnp.where(lane < 127, low_moved, zero)
                    upd[lo, :] = low + jnp.where(lane > 0, high_moved, zero)
                    ends.append((low, low_moved, high, high_moved))
                n = a * 6 + b
                pairs = (
                    jnp.where(lane == 127, ends[0][1], ends[1][0]),
                    jnp.where(lane == 127, ends[0][2], ends[1][3]),
                )
                for s in (0, 1):
                    moved = pltpu.roll(pairs[s], n + 1, 1)
                    packed[s] = jnp.where(jnp.logical_or(lane == n, lane == n + 1), moved, packed[s])
        return packed

    def remote(src, dst, k, n, peer):
        return pltpu.make_async_remote_copy(
            src_ref=src,
            dst_ref=dst,
            send_sem=face_send.at[k, n],
            recv_sem=face_recv.at[k, n],
            device_id=peer,
            device_id_type=MESH,
        )

    def face_copies(k):
        copies = [remote(dep_out.at[k], dep_in.at[k], k, 0, at(0, 0, 1))]
        for s, da in enumerate((-1, 1)):
            copies.append(remote(az_out.at[k, s], az_in.at[k, s], k, 1 + s, at(da, 0, 0)))
        for s, dm in enumerate((-1, 1)):
            for i, da in enumerate((-1, 0, 1)):
                n = 3 + s * 3 + i
                copies.append(remote(mer_out.at[k, s], mer_in.at[k, s * 3 + i], k, n, at(da, dm, 0)))
        return copies

    def exchange(k, copies):
        copies[0].wait_recv()
        for d in (0, 1):
            first = (5 * PLANE + 4, 0)[d]

            @pl.when(dep == d)
            def _():
                for n in range(36):
                    r = first + n * 8
                    upd[r : r + 4, :] = upd[r : r + 4, :] + dep_in[k, n * 4 : n * 4 + 4, :]

        assemble_azimuth_depth()
        packed = assemble_meridian(range(6), [zero, zero])
        for s, there in enumerate((has_low, has_high)):
            mer_out[k, s] = packed[s]

            @pl.when(there)
            def _():
                for copy in copies[3 + 3 * s : 6 + 3 * s]:
                    copy.start()

        for s, (b, e) in enumerate(((0, 0), (5, 3))):
            for a in range(6):
                first = a * PLANE + b * 48 + e
                az_out[k, s, a * 12 : a * 12 + 8, :] = upd[pl.ds(first, 8, stride=4), :]
                az_out[k, s, a * 12 + 8 : a * 12 + 12, :] = upd[pl.ds(first + 32, 4, stride=4), :]
            copies[1 + s].start()

    def finish(copies):
        for copy in copies[1:3]:
            copy.wait_recv()
        for s, came in enumerate((has_high, has_low)):

            @pl.when(came)
            def _():
                for copy in copies[3 + 3 * s : 6 + 3 * s]:
                    copy.wait_recv()

    def finish_sends(copies):
        for copy in copies[:3]:
            copy.wait_send()
        for s, to in enumerate((has_low, has_high)):

            @pl.when(to)
            def _():
                for copy in copies[3 + 3 * s : 6 + 3 * s]:
                    copy.wait_send()

    def add_halo(k, field, planes):
        for s, (b, e) in enumerate(((5, 3), (0, 0))):
            for a in planes:
                first = a * PLANE + b * 48 + e
                for skip, count in ((0, 8), (8, 4)):
                    r = pl.ds(first + 4 * skip, count, stride=4)
                    field[r, :] = field[r, :] + az_in[k, s, a * 12 + skip : a * 12 + skip + count, :]

        for s, (c, to_lane, there) in enumerate(((5, 127, has_high), (0, 0, has_low))):

            @pl.when(there)
            def _():
                from_high, direct, from_low = (mer_in[k, s * 3 + i] for i in range(3))
                for n in [a * 6 + b for a in planes for b in range(6)]:
                    moved = pltpu.roll(direct, (to_lane - n) % 128, 1)
                    r = slice(n * 48 + c * 8, n * 48 + c * 8 + 8)
                    field[r, :] = field[r, :] + jnp.where(lane == to_lane, moved, zero)
                for a in planes:
                    moved = pltpu.roll(from_high, (to_lane - a * 6) % 128, 1)
                    moved = jnp.where(jnp.logical_and(lane == to_lane, row_az == 0), moved, zero)
                    r = a * PLANE + 5 * 48 + c * 8 + 3
                    field[r : r + 5, :] = field[r : r + 5, :] + moved[0:5]
                    moved = pltpu.roll(from_low, (to_lane - a * 6 - 5) % 128, 1)
                    moved = jnp.where(jnp.logical_and(lane == to_lane, row_az == 3), moved, zero)
                    r = a * PLANE + c * 8
                    field[r : r + 5, :] = field[r : r + 5, :] + moved[3:8]

    def strip(field):
        sums = []
        for first in (0, 5 * PLANE + 4):
            total = jnp.zeros((4, 128), F32)
            for n in range(36):
                r = slice(first + n * 8, first + n * 8 + 4)
                total = total + face_weight[n * 4 : n * 4 + 4, :] * (mass[r, :] * field[r, :])
            sums.append(total)
        return jnp.where(dep == 0, sums[0], sums[1])

    loads[0].wait()
    heat_gradients(1)
    loads[8].wait()
    late_table = felt_table(1)
    loads[1].wait()
    loads[2].wait()
    coefficients(late_table)
    loads[3].wait()
    loads[4].wait()

    loads[9].wait()
    first_copies = face_copies(0)
    update(adj, 0, first_copies[0])
    exchange(0, first_copies)

    strip_late = strip(adj)

    def add_mid(a, _):
        here = rows(a * PLANE, PLANE)
        mid[here, :] = adj[here, :] + upd[here, :]
        return 0

    lax.fori_loop(0, 6, add_mid, 0)
    loads[5].wait()
    heat_gradients(0)
    coefficients(felt_table(0))
    finish(first_copies)
    add_halo(0, mid, (0, 5))

    strip_grad = STEP * (strip_late + strip(mid))
    total = jnp.broadcast_to(jnp.sum(strip_grad, axis=1, keepdims=True), (4, 128))
    group_of = lax.div(lane1, 2 * PAN_DEV)
    mine = jnp.zeros((1, 128), F32)
    for e in range(4):
        mine = jnp.where(group_of == e, total[e : e + 1, :], mine)
    tot_out[...] = mine

    def tot_copies(to, slot):
        return [
            pltpu.make_async_remote_copy(
                src_ref=tot_out,
                dst_ref=tot_in.at[s, slot],
                send_sem=tot_send.at[s, to],
                recv_sem=tot_recv.at[s, slot],
                device_id=column(-s, to),
                device_id_type=MESH,
            )
            for s in (0, 1)
        ]

    def send_totals(position, _):
        for copy in tot_copies(position, mer):
            copy.start()
        return 0

    lax.fori_loop(0, mer, send_totals, 0)
    add_halo(0, mid, (1, 2, 3, 4))
    second_copies = face_copies(1)
    update(mid, 1, second_copies[0])
    exchange(1, second_copies)

    lane4 = lax.broadcasted_iota(jnp.int32, (4, 128), 1)
    suffix = strip_grad
    for shift in (1, 2, 4, 8, 16, 32, 64):
        suffix = suffix + jnp.where(lane4 < 128 - shift, pltpu.roll(suffix, 128 - shift, 1), 0.0)

    flat = (az * N_MER + mer) * N_DEP + dep
    before = (lax.rem(az + N_AZ - 1, N_AZ) * N_MER + mer) * N_DEP + dep
    loads[10].wait()
    owners = owner[...]
    own = owners - flat * PAN_DEV
    prev = owners - before * PAN_DEV
    slot = jnp.where(
        jnp.logical_and(own >= 0, own < PAN_DEV),
        own,
        jnp.where(jnp.logical_and(prev >= 0, prev < PAN_DEV), prev + PAN_DEV, -1),
    )
    panel = lax.broadcasted_iota(jnp.int32, (2 * PAN_DEV, 128), 0)
    hits = [jnp.broadcast_to(slot[e : e + 1, :], (2 * PAN_DEV, 128)) == panel for e in range(4)]
    counts = jnp.concatenate([jnp.where(hit, 1.0, 0.0) for hit in hits], axis=0)
    parts = jnp.concatenate(
        [jnp.where(hits[e], jnp.broadcast_to(suffix[e : e + 1, :], (2 * PAN_DEV, 128)), 0.0) for e in range(4)], axis=0
    )

    def lane_sums(values, precision):
        return lax.dot_general(
            jnp.ones((8, 128), values.dtype),
            values,
            (((1,), (1,)), ((), ())),
            precision=precision,
            preferred_element_type=F32,
        )

    counts = lane_sums(counts.astype(jnp.bfloat16), None)
    parts = lane_sums(parts, lax.Precision.HIGHEST)
    pan_out[0] = parts
    pan_out[1] = counts
    pan_copy = pltpu.make_async_remote_copy(
        src_ref=pan_out,
        dst_ref=pan_in,
        send_sem=pan_send,
        recv_sem=pan_recv,
        device_id=at(-1, 0, 0),
        device_id_type=MESH,
    )
    pan_copy.start()

    def add_out(a, _):
        here = rows(a * PLANE, PLANE)
        out[here, :] = mid[here, :] + upd[here, :]
        return 0

    finish(second_copies)
    add_halo(1, upd, range(6))
    lax.fori_loop(0, 6, add_out, 0)

    pan_copy.wait_recv()
    def finish_totals(position, _):
        for copy in tot_copies(position, mer):
            copy.wait_send()
        return 0

    lax.fori_loop(0, mer, finish_totals, 0)
    finish_sends(first_copies)
    finish_sends(second_copies)
    pan_copy.wait_send()
    pan_other = pan_in[...]

    def receive_totals(position, sums):
        for copy in tot_copies(0, position):
            copy.wait_recv()
        return tuple(total + tot_in[s, position] for s, total in enumerate(sums))

    none = jnp.zeros((1, 128), F32)
    carried = lax.fori_loop(mer + 1, N_MER, receive_totals, (none, none))

    whole = parts + counts * carried[0]
    other = pan_other[0] + pan_other[1] * carried[1]
    pieces = [whole] + [pltpu.roll(whole, 128 - 32 * e, 1) for e in (1, 2, 3)]
    pieces += [pltpu.roll(other, 128 - 32 * e - PAN_DEV, 1) for e in (0, 1, 2, 3)]
    while len(pieces) > 1:
        pieces = [pieces[i] + pieces[i + 1] for i in range(0, len(pieces), 2)]
    whole = pieces[0]
    panels[...] = whole[0:1, 0:PAN_DEV]


def shards(
    adjoint_end,
    temp_early,
    temp_late,
    mass_inverse,
    thermal_transport_coefficient,
    jacobian_quadrature_scales,
    measured,
    sensor_cell_slot,
    sensor_gridsite_slot,
    face_weight,
    panel_owner,
):
    shape = adjoint_end.shape

    def flat(array):
        return array.reshape(-1, 128)

    hbm = pl.BlockSpec(memory_space=pltpu.HBM)
    vmem = pl.BlockSpec(memory_space=pltpu.VMEM)
    field = pltpu.VMEM((ROWS, 128), F32)
    padded = pltpu.VMEM((ROWS + 32, 128), F32)
    small = pltpu.VMEM((8, 128), F32)
    start, panel_grad = pl.pallas_call(
        kernel,
        out_shape=(
            pltpu.VMEM((ROWS, 128), F32),
            pltpu.VMEM((1, PAN_DEV), F32),
        ),
        in_specs=[hbm] * 11,
        out_specs=(vmem, vmem),
        scratch_shapes=[
            pltpu.SMEM((2, SENSORS), F32),
            pltpu.SMEM((SENSORS,), jnp.int32),
            pltpu.SMEM((SENSORS,), jnp.int32),
            pltpu.VMEM((144, 128), F32),
            pltpu.VMEM((4, 128), jnp.int32),
            field,
            pltpu.VMEM((108, 16, 128), jnp.bfloat16),
            pltpu.VMEM((108, 16, 128), jnp.bfloat16),
            field,
            field,
            pltpu.VMEM((3 * ROWS, 128), jnp.bfloat16),
            field,
            pltpu.VMEM((3, ROWS, 128), F32),
            pltpu.VMEM((3, ROWS, 128), F32),
            field,
            pltpu.VMEM((ROWS, 128), jnp.bfloat16),
            field,
            padded,
            padded,
            pltpu.VMEM((2, SENSORS, 128), F32),
            pltpu.VMEM((2, 2, 72, 128), F32),
            pltpu.VMEM((2, 2, 72, 128), F32),
            pltpu.VMEM((2, 144, 128), F32),
            pltpu.VMEM((2, 144, 128), F32),
            pltpu.VMEM((2, 2, 8, 128), F32),
            pltpu.VMEM((2, 6, 8, 128), F32),
            pltpu.VMEM((1, 128), F32),
            pltpu.VMEM((2, N_MER, 1, 128), F32),
            pltpu.VMEM((2, 8, 128), F32),
            pltpu.VMEM((2, 8, 128), F32),
            pltpu.SemaphoreType.DMA((11,)),
            pltpu.SemaphoreType.DMA((2, 9)),
            pltpu.SemaphoreType.DMA((2, 9)),
            pltpu.SemaphoreType.DMA((2, N_MER)),
            pltpu.SemaphoreType.DMA((2, N_MER)),
            pltpu.SemaphoreType.DMA,
            pltpu.SemaphoreType.DMA,
        ],
        compiler_params=pltpu.CompilerParams(
            collective_id=0, has_side_effects=True, vmem_limit_bytes=60 * 1024 * 1024
        ),
        name="adjoint_steps",
    )(
        flat(adjoint_end),
        temp_early.reshape(108, 16, 128),
        temp_late.reshape(108, 16, 128),
        flat(mass_inverse),
        flat(thermal_transport_coefficient),
        flat(jacobian_quadrature_scales),
        measured,
        sensor_cell_slot,
        sensor_gridsite_slot,
        flat(face_weight),
        flat(panel_owner),
    )
    return start.reshape(shape), panel_grad.reshape(PAN_DEV)


def solution(mesh):
    field = P(None, None, None, "depth", "azimuth", "meridian")
    line = P(("azimuth", "meridian", "depth"))
    placed = (
        field,
        field,
        field,
        field,
        field,
        P(None, None, None, None, "depth", "azimuth", "meridian"),
        P(None, ("azimuth", "meridian", "depth")),
        line,
        line,
        P("depth", None, None, "azimuth", "meridian"),
        P("depth", "azimuth", "meridian"),
    )
    return jax.shard_map(shards, mesh=mesh, in_specs=placed, out_specs=(field, line), check_vma=False)
```
